128 devices in a mesh: cplx: 2 (over core), samp: 32 (over z, y_lo, x), head: 2 (over y_hi).
Axes of the slice: x: 4, y: 4 (y_hi: 2, y_lo: 2; y = y_hi * 2 + y_lo), z: 4, core: 2. Of those that a mesh axis runs over, the one named last changes fastest.
Arguments:
- activations: bfloat16 [2, 32, 256, 768], P('cplx', 'samp'), may hold values from -6 to 6
- conditioning: bfloat16 [2, 256, 384], P('cplx'), may hold values from -6 to 6
- pair: bfloat16 [2, 256, 256, 128], P('cplx', 'samp'), may hold values from -6 to 6
- counts: int32 [2], P('cplx'), may hold values from 128 to 256, as said below
- ada_weight: bfloat16 [2, 384, 1536], replicated, may hold values from -0.3125 to 0.3125
- ada_bias: bfloat16 [2, 768], replicated, may hold values from -4 to 4
- cond_gain: bfloat16 [2, 384], replicated, may hold values from 0.099609375 to 1.8984375
- zero_weight: bfloat16 [2, 384, 768], replicated, may hold values from -0.3125 to 0.3125
- zero_bias: bfloat16 [2, 768], replicated, may hold values from -4 to 4
- qkvg_weight: bfloat16 [768, 4, 768], P(None, None, 'head'), may hold values from -0.21875 to 0.21875
- q_bias: bfloat16 [768], P('head'), may hold values from -3 to 3
- out_weight: bfloat16 [768, 768], P('head'), may hold values from -2.5 to 2.5
- in_weight: bfloat16 [768, 2, 1536], P(None, None, 'head'), may hold values from -0.21875 to 0.21875
- hid_weight: bfloat16 [1536, 768], P('head'), may hold values from -0.15625 to 0.15625
- pair_gain: bfloat16 [128], replicated, may hold values from 0.099609375 to 1.8984375
- bias_weight: bfloat16 [128, 16], P(None, 'head'), may hold values from -0.5 to 0.5
- cotangent: bfloat16 [2, 32, 256, 768], P('cplx', 'samp'), may hold values from -6 to 6
Outputs:
- mixed: bfloat16 [2, 32, 256, 768], P('cplx', 'samp')
- grad_activations: float32 [2, 32, 256, 768], P('cplx', 'samp')
- grad_conditioning: float32 [2, 256, 384], P('cplx')
- grad_pair: float32 [2, 256, 256, 128], P('cplx', 'samp')
- grad_ada_weight: float32 [2, 384, 1536], replicated
- grad_ada_bias: float32 [2, 768], replicated
- grad_cond_gain: float32 [2, 384], replicated
- grad_zero_weight: float32 [2, 384, 768], replicated
- grad_zero_bias: float32 [2, 768], replicated
- grad_qkvg_weight: float32 [768, 4, 768], P(None, None, 'head')
- grad_q_bias: float32 [768], P('head')
- grad_out_weight: float32 [768, 768], P('head')
- grad_in_weight: float32 [768, 2, 1536], P(None, None, 'head')
- grad_hid_weight: float32 [1536, 768], P('head')
- grad_pair_gain: float32 [128], replicated
- grad_bias_weight: float32 [128, 16], P(None, 'head')
The draws below stay inside these ranges and needn't reach their ends.
Inputs may be any that keep to these rules, and one draw needn't show every extreme that they name: `counts`: one complex uses all 256 positions, the other at least half of them.
All inputs are finite; a program needn't handle non-finite values.
Results may differ from the reference program's by a relative error of at most 0.028.
Values may be sent and summed in bfloat16 or wider, within the bound.
A program may use at most 128 MiB of HBM per device.

```python
import math
import jax
import jax.numpy as jnp
from jax import lax

D = 768
H = 16
HD = 48
P_SIZE = 128
C = 384
F = 1536
N = 256
SAMPLES = 32


def draw_counts(key, part):
    key = jax.random.fold_in(key, 11)
    length_key = jax.random.fold_in(key, 5)
    order_key = jax.random.fold_in(key, 9)
    short_lens = jax.random.randint(length_key, (2,), N // 2, N, dtype=jnp.int32)
    full_slot = jax.random.randint(order_key, (), 0, 2, dtype=jnp.int32)
    slots = jnp.arange(2, dtype=jnp.int32)
    return jnp.where(slots == full_slot, jnp.int32(N), short_lens).astype(jnp.int32)


def block_levels(rng, extent, split, smallest, high):
    loudness, own = 1.0, jax.random.fold_in(rng, 6)
    for position, parts in split:
        heights = jnp.exp(jax.random.uniform(jax.random.fold_in(own, position), (parts,), jnp.float32, smallest / len(split), high / len(split)))
        loudness = loudness * jnp.repeat(heights, extent[position] // parts).reshape([-1 if axis == position else 1 for axis in range(len(extent))])
    return loudness


def scatter_about(stream_key, extent, scale, bound, split=(), kind=jnp.bfloat16):
    gain = block_levels(stream_key, extent, split, -0.22, 0.18) if split else 1.0
    entries = jax.random.normal(stream_key, extent, jnp.float32) * scale * gain
    return jnp.minimum(jnp.maximum(entries, -bound), bound).astype(kind)


def setup_inputs(seed: int = 0) -> dict:
    key_of = jax.random.split(jax.random.key(seed), 18)
    return {
        "activations": scatter_about(key_of[0], (2, SAMPLES, N, D), 1.0, 6.0, ((0, 2), (1, 32))),
        "conditioning": scatter_about(key_of[1], (2, N, C), 1.0, 6.0, ((0, 2),)),
        "pair": scatter_about(key_of[2], (2, N, N, P_SIZE), 1.0, 6.0, ((0, 2), (1, 32))),
        "counts": draw_counts(jax.random.fold_in(key_of[17], 71), 0),
        "ada_weight": scatter_about(key_of[4], (2, C, 2 * D), C ** -0.5, 0.3125),
        "ada_bias": scatter_about(key_of[5], (2, D), 1.0, 4.0),
        "cond_gain": jnp.clip(1.0 + 0.18 * jax.random.normal(key_of[6], (2, C), jnp.float32), 0.099609375, 1.8984375).astype(jnp.bfloat16),
        "zero_weight": scatter_about(key_of[7], (2, C, D), C ** -0.5, 0.3125),
        "zero_bias": scatter_about(key_of[8], (2, D), 1.0, 4.0),
        "qkvg_weight": scatter_about(key_of[9], (D, 4, D), D ** -0.5, 0.21875, ((2, 2),)),
        "q_bias": scatter_about(key_of[10], (D,), 0.5, 3.0, ((0, 2),)),
        "out_weight": scatter_about(key_of[11], (D, D), (max(D // 128, 1)) ** -0.5, 2.5, ((0, 2),)),
        "in_weight": scatter_about(key_of[12], (D, 2, F), D ** -0.5, 0.21875, ((2, 2),)),
        "hid_weight": scatter_about(key_of[13], (F, D), F ** -0.5, 0.15625, ((0, 2),)),
        "pair_gain": jnp.clip(1.0 + 0.18 * jax.random.normal(key_of[14], (P_SIZE,), jnp.float32), 0.099609375, 1.8984375).astype(jnp.bfloat16),
        "bias_weight": scatter_about(key_of[15], (P_SIZE, H), P_SIZE ** -0.5, 0.5, ((1, 2),)),
        "cotangent": scatter_about(key_of[16], (2, SAMPLES, N, D), 1.0, 6.0, ((0, 2), (1, 32))),
    }


@jax.custom_vjp
def low(v):
    return lax.optimization_barrier(v.astype(jnp.bfloat16)).astype(jnp.float32)

@jax.custom_vjp
def low_back(v):
    return v

def low_keep(v):
    return (low(v), None)

def low_pass(kept, grad):
    return (grad,)

def back_keep(v):
    return (v, None)

def back_low(kept, grad):
    return (low(grad),)
low.defvjp(low_keep, low_pass)
low_back.defvjp(back_keep, back_low)
EPS = 1e-05
HIGH = lax.Precision.HIGHEST

def rounded(tensor):
    return low(low_back(tensor))

def normalize(tensor):
    row_mean = lax.optimization_barrier(jnp.mean(tensor, -1, keepdims=True))
    centered = tensor - row_mean
    return centered * lax.rsqrt(lax.optimization_barrier(jnp.mean(centered * centered, -1, keepdims=True)) + EPS)

def complex_forward(act_one, single, pair_one, count_one, ada_weight, ada_bias, cond_gain, zero_weight, zero_bias, qkvg_weight, q_bias, out_weight, in_weight, hid_weight, pair_gain, bias_weight):
    single_hat = normalize(single)
    scaled = single_hat[None] * cond_gain[:, None, :]
    projected = jnp.einsum('wnc,wcd->wnd', scaled, ada_weight, precision=HIGH)
    mod_gate = jax.nn.sigmoid(projected[:, :, :D] + ada_bias[:, None, :])
    mod_shift = projected[:, :, D:]
    zero_gate = jax.nn.sigmoid(jnp.einsum('nc,wcd->wnd', single, zero_weight, precision=HIGH) + zero_bias[:, None, :])
    pair_low = low(normalize(pair_one) * pair_gain)
    pair_bias = rounded(jnp.einsum('ijp,ph->hij', pair_low, bias_weight, precision=HIGH))
    act_hat = normalize(act_one)
    attn_in = low(mod_gate[0] * act_hat + mod_shift[0])
    trans_in = low(mod_gate[1] * act_hat + mod_shift[1])
    heads_in = jnp.einsum('snd,dke->ksne', attn_in, qkvg_weight, precision=HIGH)
    queries = rounded(heads_in[0] + q_bias).reshape(SAMPLES, N, H, HD)
    key_heads = rounded(heads_in[1]).reshape(SAMPLES, N, H, HD)
    values = rounded(heads_in[2]).reshape(SAMPLES, N, H, HD)
    gate_pre = low_back(heads_in[3])
    key_valid = jnp.arange(N) < count_one
    score_scale = 1.0 / math.sqrt(HD)

    def attend(per_sample):
        q_one, k_one, v_one = per_sample
        raw_scores = low_back(jnp.einsum('ihe,jhe->hij', q_one, k_one, precision=HIGH) * score_scale + pair_bias)
        masked = jnp.where(key_valid[None, None, :], raw_scores, -1000000000.0)
        attn_probs = low(jax.nn.softmax(masked, axis=-1))
        return jnp.einsum('hij,jhe->ihe', attn_probs, v_one, precision=HIGH)
    attended = low_back(lax.map(jax.checkpoint(attend), (queries, key_heads, values)).reshape(SAMPLES, N, D))
    gated_out = low(jax.nn.sigmoid(gate_pre) * attended)
    attn_out = low_back(jnp.dot(gated_out, out_weight, precision=HIGH))
    hidden_in = jnp.einsum('snd,dkf->ksnf', trans_in, in_weight, precision=HIGH)
    gate_in = low_back(hidden_in[0])
    up_in = low_back(hidden_in[1])
    hidden = low(jax.nn.silu(gate_in) * up_in)
    trans_out = low_back(jnp.dot(hidden, hid_weight, precision=HIGH))
    return act_one + zero_gate[0] * attn_out + zero_gate[1] * trans_out

def reference(activations, conditioning, pair, counts, ada_weight, ada_bias, cond_gain, zero_weight, zero_bias, qkvg_weight, q_bias, out_weight, in_weight, hid_weight, pair_gain, bias_weight, cotangent):
    weight_f = tuple((tensor.astype(jnp.float32) for tensor in (ada_weight, ada_bias, cond_gain, zero_weight, zero_bias, qkvg_weight, q_bias, out_weight, in_weight, hid_weight, pair_gain, bias_weight)))

    def forward(act_all, single_all, pair_all, *weight_list):
        results = [complex_forward(act_all[cplx_index], single_all[cplx_index], pair_all[cplx_index], counts[cplx_index], *weight_list) for cplx_index in range(2)]
        return jnp.stack(results)
    result, pullback = jax.vjp(forward, activations.astype(jnp.float32), conditioning.astype(jnp.float32), pair.astype(jnp.float32), *weight_f)
    grad_all = pullback(cotangent.astype(jnp.float32))
    return (result.astype(jnp.bfloat16), grad_all[0], grad_all[1], grad_all[2], grad_all[3], grad_all[4], grad_all[5], grad_all[6], grad_all[7], grad_all[8], grad_all[9], grad_all[10], grad_all[11], grad_all[12], grad_all[13], grad_all[14])
```

```python
import functools
import math

import jax
import jax.numpy as jnp
from jax import lax
from jax.experimental import pallas as pl
from jax.experimental.pallas import tpu as pltpu
from jax.sharding import PartitionSpec as P

D = 768
HD = 48
EPS = 1e-05
HIGH = lax.Precision.HIGHEST
MESH = pl.DeviceIdType.MESH
BF = jnp.bfloat16
F32 = jnp.float32
NS = 32
VMEM = pltpu.VMEM


def place():
    samp = lax.axis_index("samp")
    return {
        "c": lax.axis_index("cplx"),
        "h": lax.axis_index("head"),
        "s": samp,
        "z": samp // 8,
        "l": (samp // 4) % 2,
        "x": samp % 4,
        "y": lax.axis_index("head") * 2 + (samp // 4) % 2,
    }


SIZE = {"z": 4, "x": 4, "y": 4, "l": 2}


def peer_on(at, axis, step):
    z, x, lo, hd = at["z"], at["x"], at["l"], at["h"]
    q = (at[axis] + step) % SIZE[axis]
    if axis == "z":
        z = q
    elif axis == "x":
        x = q
    elif axis == "l":
        lo = q
    else:
        hd, lo = q // 2, q % 2
    return {"cplx": at["c"], "samp": z * 8 + lo * 4 + x, "head": hd}, q


def signal(bar, dev):
    pl.semaphore_signal(bar, inc=1, device_id=dev, device_id_type=MESH)


def samp_dev(at, other):
    return {"cplx": at["c"], "samp": other, "head": at["h"]}


def head_dev(at):
    return {"cplx": at["c"], "samp": at["s"], "head": 1 - at["h"]}


def core_dev(at):
    return {"cplx": 1 - at["c"], "samp": at["s"], "head": at["h"]}


def rcopy(src, dst, send, recv, dev):
    return pltpu.make_async_remote_copy(
        src_ref=src, dst_ref=dst, send_sem=send, recv_sem=recv, device_id=dev, device_id_type=MESH
    )


def greet_samp(at, bar):
    def one(i, _):
        signal(bar, samp_dev(at, (at["s"] + i) % NS))
        return 0

    lax.fori_loop(1, NS, one, 0)


def gather_kernel(part_ref, wt_ref, full_ref, wo_ref, send, recv, hsend, hrecv):
    at = place()
    me = at["s"]
    bar = pltpu.get_barrier_semaphore()
    greet_samp(at, bar)
    signal(bar, head_dev(at))
    pl.semaphore_wait(bar, NS)

    def copy(i):
        return rcopy(
            part_ref, full_ref.at[me], send.at[i], recv.at[i], samp_dev(at, (me + i) % NS)
        )

    def begin(i, _):
        copy(i).start()
        return 0

    def end(i, _):
        copy(i).wait()
        return 0

    lax.fori_loop(1, NS, begin, 0)
    other = rcopy(wt_ref, wo_ref, hsend, hrecv, head_dev(at))
    other.start()
    full_ref[me] = part_ref[...]
    lax.fori_loop(1, NS, end, 0)
    other.wait()


def gather_bias(part, weight_t):
    return pl.pallas_call(
        gather_kernel,
        out_shape=(
            jax.ShapeDtypeStruct((NS,) + part.shape, BF),
            jax.ShapeDtypeStruct(weight_t.shape, BF),
        ),
        in_specs=[pl.BlockSpec(memory_space=VMEM)] * 2,
        out_specs=[pl.BlockSpec(memory_space=VMEM)] * 2,
        scratch_shapes=[
            pltpu.SemaphoreType.DMA((NS,)),
            pltpu.SemaphoreType.DMA((NS,)),
            pltpu.SemaphoreType.DMA,
            pltpu.SemaphoreType.DMA,
        ],
        compiler_params=pltpu.CompilerParams(
            collective_id=0, has_side_effects=True, vmem_limit_bytes=16 * 2**20
        ),
        name="gather_bias",
    )(part, weight_t)


def scatter_kernel(
    gb_ref, mix_ref, act_ref, own_ref, oth_ref, mixo_ref, acto_ref, slots, send, recv, hsend, hrecv
):
    at = place()
    me = at["s"]
    bar = pltpu.get_barrier_semaphore()
    greet_samp(at, bar)
    signal(bar, head_dev(at))
    pl.semaphore_wait(bar, NS)

    def copy(i):
        to = (me + i) % NS
        return rcopy(gb_ref.at[to], slots.at[me], send.at[i], recv.at[i], samp_dev(at, to))

    def begin(i, _):
        copy(i).start()
        return 0

    def end(i, _):
        copy(i).wait()
        return 0

    lax.fori_loop(1, NS, begin, 0)
    hd = head_dev(at)
    mix = rcopy(mix_ref, mixo_ref, hsend.at[0], hrecv.at[0], hd)
    mix.start()
    act = rcopy(act_ref, acto_ref, hsend.at[1], hrecv.at[1], hd)
    act.start()
    slots[me] = gb_ref[me]
    lax.fori_loop(1, NS, end, 0)

    def add(i, total):
        return total + slots[i].astype(F32)

    own_ref[...] = lax.fori_loop(0, NS, add, jnp.zeros(own_ref.shape, F32)).astype(BF)
    rows = rcopy(own_ref, oth_ref, hsend.at[2], hrecv.at[2], hd)
    rows.start()
    mix.wait()
    act.wait()
    rows.wait()


def scatter_bias(gb, mix, act):
    return pl.pallas_call(
        scatter_kernel,
        out_shape=(
            jax.ShapeDtypeStruct(gb.shape[1:], BF),
            jax.ShapeDtypeStruct(gb.shape[1:], BF),
            jax.ShapeDtypeStruct(mix.shape, BF),
            jax.ShapeDtypeStruct(act.shape, BF),
        ),
        in_specs=[pl.BlockSpec(memory_space=VMEM)] * 3,
        out_specs=[pl.BlockSpec(memory_space=VMEM)] * 4,
        scratch_shapes=[
            pltpu.VMEM(gb.shape, BF),
            pltpu.SemaphoreType.DMA((NS,)),
            pltpu.SemaphoreType.DMA((NS,)),
            pltpu.SemaphoreType.DMA((3,)),
            pltpu.SemaphoreType.DMA((3,)),
        ],
        compiler_params=pltpu.CompilerParams(
            collective_id=1, has_side_effects=True, vmem_limit_bytes=16 * 2**20
        ),
        name="scatter_bias",
    )(gb, mix, act)


W_TILES, A_TILES, C_TILES = 1664, 1024, 64
W_HALF, A_HALF = W_TILES // 2, A_TILES // 2
GROUPS = (
    (0, 0, W_HALF // 2, "zxl"),
    (0, W_HALF // 2, W_HALF // 2, "xzl"),
    (1, 0, A_HALF // 2, "yzx"),
    (1, A_HALF // 2, A_HALF // 2, "yxz"),
    (2, 0, C_TILES, "yzx"),
)


def sum_kernel(w_ref, a_ref, c_ref, wo_ref, ao_ref, co_ref, *rest):
    rest = list(rest)
    wr, ar = rest[:2]
    work = rest[2:5]
    recvs = [rest[5 + 3 * g : 8 + 3 * g] for g in range(len(GROUPS))]
    csend, crecv, rsend, rrecv, gsend, grecv, fsend, frecv = rest[5 + 3 * len(GROUPS) :]
    outs = (wo_ref, ao_ref, co_ref)
    at = place()
    core = at["c"]
    bar = pltpu.get_barrier_semaphore()
    friends = [core_dev(at)]
    for axis, steps in (("z", 3), ("x", 3), ("y", 3)):
        friends += [peer_on(at, axis, i)[0] for i in range(1, steps + 1)]
    for dev in friends:
        signal(bar, dev)
    pl.semaphore_wait(bar, len(friends))

    first = []
    for i, (src, got, half) in enumerate(((w_ref, wr, W_HALF), (a_ref, ar, A_HALF))):
        cp = rcopy(
            src.at[pl.ds((1 - core) * half, half)], got, csend.at[i], crecv.at[i], core_dev(at)
        )
        cp.start()
        first.append(cp)
    work[2][...] = c_ref[...]

    base = [None] * len(GROUPS)
    pending = [None] * len(GROUPS)

    def rs_start(g, stage):
        buf, _, tiles, axes = GROUPS[g]
        axis = axes[stage]
        count = SIZE[axis]
        for a in axes[:stage]:
            tiles //= SIZE[a]
        part = tiles // count
        cps = []
        for i in range(1, count):
            dev, q = peer_on(at, axis, i)
            cp = rcopy(
                work[buf].at[pl.ds(base[g] + q * part, part)],
                recvs[g][stage].at[i - 1],
                rsend.at[g, stage, i - 1],
                rrecv.at[g, stage, i - 1],
                dev,
            )
            cp.start()
            cps.append(cp)
        pending[g] = cps
        return part

    def rs_end(g, stage, part):
        buf, _, _, axes = GROUPS[g]
        for cp in pending[g]:
            cp.wait()
        here = base[g] + at[axes[stage]] * part
        block = part
        while block > 16 and block % 2 == 0:
            block //= 2

        def add(i, _):
            rows = pl.ds(i * block, block)
            mine = pl.ds(here + i * block, block)
            total = work[buf][mine].astype(F32)
            for j in range(SIZE[axes[stage]] - 1):
                total = total + recvs[g][stage][j, rows].astype(F32)
            work[buf][mine] = total.astype(BF)
            return 0

        lax.fori_loop(0, part // block, add, 0)
        base[g] = here

    for i, (src, got, half) in enumerate(((w_ref, wr, W_HALF), (a_ref, ar, A_HALF))):
        first[i].wait()

        def add(j, _):
            rows = pl.ds(j * 16, 16)
            work[i][rows] = (
                src[pl.ds(core * half + j * 16, 16)].astype(F32) + got[rows].astype(F32)
            ).astype(BF)
            return 0

        lax.fori_loop(0, half // 16, add, 0)

    parts = [None] * len(GROUPS)
    for g in range(len(GROUPS)):
        base[g] = GROUPS[g][1]
        parts[g] = rs_start(g, 0)
    for stage in range(3):
        for g in range(len(GROUPS)):
            rs_end(g, stage, parts[g])
            if stage < 2:
                parts[g] = rs_start(g, stage + 1)

    shift = [core * W_HALF, core * A_HALF, 0]
    for g in range(len(GROUPS)):
        buf = GROUPS[g][0]
        outs[buf][pl.ds(shift[buf] + base[g], parts[g])] = work[buf][pl.ds(base[g], parts[g])]

    def ag_start(g, stage):
        buf, _, _, axes = GROUPS[g]
        axis = axes[stage]
        rows = pl.ds(shift[buf] + base[g], parts[g])
        cps = []
        for i in range(1, SIZE[axis]):
            dev, _ = peer_on(at, axis, i)
            cp = rcopy(
                outs[buf].at[rows],
                outs[buf].at[rows],
                gsend.at[g, stage, i - 1],
                grecv.at[g, stage, i - 1],
                dev,
            )
            cp.start()
            cps.append(cp)
        pending[g] = cps

    def ag_end(g, stage):
        axis = GROUPS[g][3][stage]
        for cp in pending[g]:
            cp.wait()
        base[g] = base[g] - at[axis] * parts[g]
        parts[g] = parts[g] * SIZE[axis]

    last = []
    for stage in (2, 1, 0):
        for g in range(len(GROUPS)):
            if stage < 2:
                ag_end(g, stage + 1)
            ag_start(g, stage)
    for g in range(len(GROUPS)):
        ag_end(g, 0)
        buf = GROUPS[g][0]
        if buf < 2:
            rows = pl.ds(shift[buf] + GROUPS[g][1], GROUPS[g][2])
            cp = rcopy(outs[buf].at[rows], outs[buf].at[rows], fsend.at[g], frecv.at[g], core_dev(at))
            cp.start()
            last.append(cp)
    for cp in last:
        cp.wait()


def sum_tiles(w, a, c):
    recvs = []
    for _, _, tiles, axes in GROUPS:
        for axis in axes:
            tiles //= SIZE[axis]
            recvs.append(pltpu.VMEM((SIZE[axis] - 1, tiles, 16, 128), BF))
    n = len(GROUPS)
    return pl.pallas_call(
        sum_kernel,
        out_shape=tuple(jax.ShapeDtypeStruct(t.shape, BF) for t in (w, a, c)),
        in_specs=[pl.BlockSpec(memory_space=VMEM)] * 3,
        out_specs=[pl.BlockSpec(memory_space=VMEM)] * 3,
        scratch_shapes=[
            pltpu.VMEM((W_HALF, 16, 128), BF),
            pltpu.VMEM((A_HALF, 16, 128), BF),
            pltpu.VMEM((W_HALF, 16, 128), BF),
            pltpu.VMEM((A_HALF, 16, 128), BF),
            pltpu.VMEM((C_TILES, 16, 128), BF),
            *recvs,
            pltpu.SemaphoreType.DMA((2,)),
            pltpu.SemaphoreType.DMA((2,)),
            pltpu.SemaphoreType.DMA((n, 3, 3)),
            pltpu.SemaphoreType.DMA((n, 3, 3)),
            pltpu.SemaphoreType.DMA((n, 3, 3)),
            pltpu.SemaphoreType.DMA((n, 3, 3)),
            pltpu.SemaphoreType.DMA((n,)),
            pltpu.SemaphoreType.DMA((n,)),
        ],
        compiler_params=pltpu.CompilerParams(
            collective_id=2, has_side_effects=True, vmem_limit_bytes=56 * 2**20
        ),
        name="sum_tiles",
    )(w, a, c)


def to_tiles(m):
    rows, cols = m.shape
    m = m.astype(BF).reshape(rows // 16, 16, cols // 128, 128)
    return m.transpose(2, 0, 1, 3).reshape(-1, 16, 128)


def from_tiles(t, rows, cols):
    t = t.reshape(cols // 128, rows // 16, 16, 128).transpose(1, 2, 0, 3)
    return t.reshape(rows, cols).astype(F32)


def fill(parts, count):
    have = sum(p.shape[0] for p in parts)
    return jnp.concatenate(list(parts) + [jnp.zeros((count - have, 16, 128), BF)], 0)


def small_tile(vectors):
    flat = jnp.concatenate([v.reshape(-1, 128) for v in vectors], 0).astype(BF)
    return jnp.pad(flat, ((0, -flat.shape[0] % 16), (0, 0))).reshape(-1, 16, 128)


def normalize(tensor):
    row_mean = jnp.mean(tensor, -1, keepdims=True)
    centered = tensor - row_mean
    inv_std = lax.rsqrt(jnp.mean(centered * centered, -1, keepdims=True) + EPS)
    return (centered * inv_std, inv_std)


def norm_back(grad_hat, normed, inv_std):
    return inv_std * (
        grad_hat
        - jnp.mean(grad_hat, -1, keepdims=True)
        - normed * jnp.mean(grad_hat * normed, -1, keepdims=True)
    )


def mm(spec, a, b):
    return jnp.einsum(spec, a, b, preferred_element_type=F32)


def local(
    activations,
    conditioning,
    pair,
    counts,
    ada_weight,
    ada_bias,
    cond_gain,
    zero_weight,
    zero_bias,
    qkvg_weight,
    q_bias,
    out_weight,
    in_weight,
    hid_weight,
    pair_gain,
    bias_weight,
    cotangent,
):
    act_f = activations[0, 0].astype(F32)
    length = act_f.shape[0]
    heads = bias_weight.shape[1]
    width = q_bias.shape[0]
    scale = 1.0 / math.sqrt(HD)
    pair_gain_f = pair_gain.astype(F32)
    pair_hat, pair_inv = normalize(pair[0].astype(F32))
    pair_low = (pair_hat * pair_gain_f).astype(BF)
    bias_part = mm("rjp,ph->hrj", pair_low, bias_weight).astype(BF)
    rows = bias_part.shape[1]
    weight_t = jnp.pad(bias_weight.T, ((0, 16 - heads), (0, 0)))
    bias_all, weight_o = gather_bias(bias_part.reshape(heads * rows, length), weight_t)
    pair_bias = (
        bias_all.reshape(NS, heads, rows, length).transpose(1, 0, 2, 3).reshape(heads, length, length)
    )
    single_low = conditioning[0]
    single = single_low.astype(F32)
    ada_float = ada_weight.astype(F32)
    gain_float = cond_gain.astype(F32)
    single_hat, single_inv = normalize(single)
    scaled = single_hat[None] * gain_float[:, None, :]
    scaled_hi = scaled.astype(BF)
    scaled_lo = (scaled - scaled_hi.astype(F32)).astype(BF)
    projected = mm("wnc,wcd->wnd", scaled_hi, ada_weight) + mm("wnc,wcd->wnd", scaled_lo, ada_weight)
    mod_gate = jax.nn.sigmoid(projected[:, :, :D] + ada_bias.astype(F32)[:, None, :])
    mod_shift = projected[:, :, D:]
    zero_gate = jax.nn.sigmoid(
        mm("nc,wcd->wnd", single_low, zero_weight) + zero_bias.astype(F32)[:, None, :]
    )
    act_hat, act_inv = normalize(act_f)
    attn_in = (mod_gate[0] * act_hat + mod_shift[0]).astype(BF)
    trans_in = (mod_gate[1] * act_hat + mod_shift[1]).astype(BF)
    heads_in = mm("nd,dke->kne", attn_in, qkvg_weight)
    queries = (heads_in[0] + q_bias.astype(F32)).astype(BF).reshape(length, heads, HD)
    key_heads = heads_in[1].astype(BF).reshape(length, heads, HD)
    values = heads_in[2].astype(BF).reshape(length, heads, HD)
    gate_pre = heads_in[3]
    key_valid = lax.broadcasted_iota(jnp.int32, (length,), 0) < counts[0]
    scores = mm("ihe,jhe->hij", queries, key_heads) * scale + pair_bias.astype(F32)
    scores = jnp.where(key_valid[None, None, :], scores, -1000000000.0)
    row_max = jnp.max(scores, -1, keepdims=True)
    exp_scores = jnp.exp(scores - row_max)
    attn_probs = exp_scores / jnp.sum(exp_scores, -1, keepdims=True)
    probs_low = attn_probs.astype(BF)
    attended = mm("hij,jhe->ihe", probs_low, values).reshape(length, width)
    gate_sig = jax.nn.sigmoid(gate_pre)
    gated_out = (gate_sig * attended).astype(BF)
    attn_part = mm("nf,fd->nd", gated_out, out_weight)
    hidden_in = mm("nd,dkf->knf", trans_in, in_weight)
    gate_in = hidden_in[0]
    up_in = hidden_in[1]
    gate_in_sig = jax.nn.sigmoid(gate_in)
    silu_val = gate_in * gate_in_sig
    hidden = (silu_val * up_in).astype(BF)
    trans_part = mm("nf,fd->nd", hidden, hid_weight)
    mix_part = (zero_gate[0] * attn_part + zero_gate[1] * trans_part).astype(BF)
    grad_out = cotangent[0, 0].astype(F32)
    grad_attn_out = (zero_gate[0] * grad_out).astype(BF)
    grad_trans_out = (zero_gate[1] * grad_out).astype(BF)
    zero_pre = (
        jnp.stack([grad_out * attn_part, grad_out * trans_part]) * zero_gate * (1.0 - zero_gate)
    )
    zero_pre_low = zero_pre.astype(BF)
    grad_zero_weight = mm("nc,wnd->wcd", single_low, zero_pre_low)
    grad_zero_bias = jnp.sum(zero_pre, 1)
    grad_out_weight = mm("nf,nd->fd", gated_out, grad_attn_out)
    grad_gated = mm("nd,fd->nf", grad_attn_out, out_weight)
    grad_gate_pre = (grad_gated * attended * gate_sig * (1.0 - gate_sig)).astype(BF)
    grad_attended = (grad_gated * gate_sig).astype(BF).reshape(length, heads, HD)
    grad_probs = mm("ihe,jhe->hij", grad_attended, values)
    delta = jnp.sum(attn_probs * grad_probs, -1, keepdims=True)
    grad_scores = (attn_probs * (grad_probs - delta)).astype(BF)
    grad_queries = (
        (mm("hij,jhe->ihe", grad_scores, key_heads) * scale).astype(BF).reshape(length, width)
    )
    grad_keys = (
        (mm("hij,ihe->jhe", grad_scores, queries) * scale).astype(BF).reshape(length, width)
    )
    grad_values = mm("hij,ihe->jhe", probs_low, grad_attended).astype(BF).reshape(length, width)
    grad_heads = jnp.stack([grad_queries, grad_keys, grad_values, grad_gate_pre])
    grad_qkvg_weight = mm("nd,kne->kde", attn_in, grad_heads)
    grad_q_bias = jnp.sum(grad_queries, 0, dtype=F32)
    grad_attn_in = mm("kne,dke->nd", grad_heads, qkvg_weight)
    grad_hidden = mm("nd,fd->nf", grad_trans_out, hid_weight)
    grad_hid_weight = mm("nf,nd->fd", hidden, grad_trans_out)
    grad_gate_in = grad_hidden * up_in * gate_in_sig * (1.0 + gate_in * (1.0 - gate_in_sig))
    grad_up_in = grad_hidden * silu_val
    grad_ffn = jnp.stack([grad_gate_in, grad_up_in]).astype(BF)
    grad_in_weight = mm("nd,knf->kdf", trans_in, grad_ffn)
    grad_trans_in = mm("knf,dkf->nd", grad_ffn, in_weight)
    act_part = (mod_gate[0] * grad_attn_in + mod_gate[1] * grad_trans_in).astype(BF)
    gb_rows = (
        grad_scores.reshape(heads, NS, rows, length)
        .transpose(1, 0, 2, 3)
        .reshape(NS, heads * rows, length)
    )
    gb_own, gb_other, mix_other, act_other = scatter_bias(gb_rows, mix_part, act_part)

    mixed = (act_f + (mix_part.astype(F32) + mix_other.astype(F32))).astype(BF)
    grad_act_hat = act_part.astype(F32) + act_other.astype(F32)
    grad_act = grad_out + norm_back(grad_act_hat, act_hat, act_inv)

    first = lax.axis_index("head") == 0
    gb_own = gb_own.reshape(heads, rows, length)
    gb_other = gb_other.reshape(heads, rows, length)
    gb_all = jnp.concatenate(
        [jnp.where(first, gb_own, gb_other), jnp.where(first, gb_other, gb_own)], 0
    )
    wt_own, wt_other = weight_t[:heads], weight_o[:heads]
    wt_all = jnp.concatenate(
        [jnp.where(first, wt_own, wt_other), jnp.where(first, wt_other, wt_own)], 0
    )
    grad_bias_weight = mm("rjp,hrj->hp", pair_low, gb_own)
    grad_pair_low = mm("hrj,hp->rjp", gb_all, wt_all)
    grad_pair_gain = jnp.sum(grad_pair_low * pair_hat, (0, 1))
    grad_pair = norm_back(grad_pair_low * pair_gain_f, pair_hat, pair_inv)

    grad_norm_out = jnp.stack([grad_attn_in, grad_trans_in])
    gate_grad = grad_norm_out * act_hat[None] * mod_gate * (1.0 - mod_gate)
    grad_ada_pre = jnp.concatenate([gate_grad, grad_norm_out], -1).astype(BF)
    grad_ada_weight = mm("wnc,wnd->wcd", scaled_hi, grad_ada_pre)
    grad_ada_bias = jnp.sum(gate_grad, 1)
    grad_scaled = mm("wnd,wcd->wnc", grad_ada_pre, ada_weight)
    grad_cond_gain = jnp.sum(grad_scaled * single_hat[None], 1)
    grad_single_hat = jnp.sum(grad_scaled * gain_float[:, None, :], 0)
    grad_single = norm_back(grad_single_hat, single_hat, single_inv) + mm(
        "wnd,wcd->nc", zero_pre_low, zero_weight
    )

    w_small = small_tile([grad_q_bias, grad_bias_weight])
    a_small = small_tile([grad_ada_bias, grad_zero_bias, grad_cond_gain, grad_pair_gain * 0.5])
    w_parts = [to_tiles(grad_qkvg_weight[k]) for k in range(4)]
    w_parts += [to_tiles(grad_out_weight)]
    w_parts += [to_tiles(grad_in_weight[k]) for k in range(2)]
    w_parts += [to_tiles(grad_hid_weight), w_small]
    a_parts = [to_tiles(grad_ada_weight[k]) for k in range(2)]
    a_parts += [to_tiles(grad_zero_weight[k]) for k in range(2)] + [a_small]
    w_sum, a_sum, c_sum = sum_tiles(
        fill(w_parts, W_TILES), fill(a_parts, A_TILES), fill([to_tiles(grad_single)], C_TILES)
    )

    def split(tiles, parts):
        out, start = [], 0
        for p in parts:
            out.append(tiles[start : start + p.shape[0]])
            start += p.shape[0]
        return out

    ws = split(w_sum, w_parts)
    asum = split(a_sum, a_parts)
    g_qkvg = jnp.stack([from_tiles(ws[k], D, width) for k in range(4)], 1)
    g_out = from_tiles(ws[4], width, D)
    hidden_units = hid_weight.shape[0]
    g_in = jnp.stack([from_tiles(ws[5 + k], D, hidden_units) for k in range(2)], 1)
    g_hid = from_tiles(ws[7], hidden_units, D)
    wsm = ws[8].reshape(-1, 128).astype(F32)
    cond = single.shape[1]
    g_ada = jnp.stack([from_tiles(asum[k], cond, 2 * D) for k in range(2)])
    g_zero = jnp.stack([from_tiles(asum[2 + k], cond, D) for k in range(2)])
    asm = asum[4].reshape(-1, 128).astype(F32)
    g_single = from_tiles(c_sum[: length * cond // 2048], length, cond)
    return (
        mixed[None, None],
        grad_act[None, None],
        g_single[None],
        grad_pair[None],
        g_ada,
        asm[0:12].reshape(2, D),
        asm[24:30].reshape(2, cond),
        g_zero,
        asm[12:24].reshape(2, D),
        g_qkvg,
        wsm[0:3].reshape(width),
        g_out,
        g_in,
        g_hid,
        asm[30],
        wsm[3:11].T,
    )


def solution(mesh):
    placed = (
        P("cplx", "samp", None, None),
        P("cplx", None, None),
        P("cplx", "samp", None, None),
        P("cplx"),
        P(),
        P(),
        P(),
        P(),
        P(),
        P(None, None, "head"),
        P("head"),
        P("head", None),
        P(None, None, "head"),
        P("head", None),
        P(),
        P(None, "head"),
        P("cplx", "samp", None, None),
    )
    return jax.shard_map(
        local,
        mesh=mesh,
        in_specs=placed,
        out_specs=(
            P("cplx", "samp", None, None),
            P("cplx", "samp", None, None),
            P("cplx", None, None),
            P("cplx", "samp", None, None),
            P(),
            P(),
            P(),
            P(),
            P(),
            P(None, None, "head"),
            P("head"),
            P("head", None),
            P(None, None, "head"),
            P("head", None),
            P(),
            P(None, "head"),
        ),
        check_vma=False,
    )
```

```python
import functools
import math

import jax
import jax.numpy as jnp
from jax import lax
from jax.experimental import pallas as pl
from jax.experimental.pallas import tpu as pltpu
from jax.sharding import PartitionSpec as P

D = 768
HD = 48
EPS = 1e-05
HIGH = lax.Precision.HIGHEST
MESH = pl.DeviceIdType.MESH
BF = jnp.bfloat16
F32 = jnp.float32
NS = 32
VMEM = pltpu.VMEM


def place():
    samp = lax.axis_index("samp")
    return {
        "c": lax.axis_index("cplx"),
        "h": lax.axis_index("head"),
        "s": samp,
        "z": samp // 8,
        "l": (samp // 4) % 2,
        "x": samp % 4,
        "y": lax.axis_index("head") * 2 + (samp // 4) % 2,
    }


SIZE = {"z": 4, "x": 4, "y": 4, "l": 2}


def peer_on(at, axis, step):
    z, x, lo, hd = at["z"], at["x"], at["l"], at["h"]
    q = (at[axis] + step) % SIZE[axis]
    if axis == "z":
        z = q
    elif axis == "x":
        x = q
    elif axis == "l":
        lo = q
    else:
        hd, lo = q // 2, q % 2
    return {"cplx": at["c"], "samp": z * 8 + lo * 4 + x, "head": hd}, q


def signal(bar, dev):
    pl.semaphore_signal(bar, inc=1, device_id=dev, device_id_type=MESH)


def samp_dev(at, other):
    return {"cplx": at["c"], "samp": other, "head": at["h"]}


def head_dev(at):
    return {"cplx": at["c"], "samp": at["s"], "head": 1 - at["h"]}


def core_dev(at):
    return {"cplx": 1 - at["c"], "samp": at["s"], "head": at["h"]}


def rcopy(src, dst, send, recv, dev):
    return pltpu.make_async_remote_copy(
        src_ref=src, dst_ref=dst, send_sem=send, recv_sem=recv, device_id=dev, device_id_type=MESH
    )


def greet_samp(at, bar):
    def one(i, _):
        signal(bar, samp_dev(at, (at["s"] + i) % NS))
        return 0

    lax.fori_loop(1, NS, one, 0)


def gather_kernel(part_ref, wt_ref, full_ref, wo_ref, send, recv, hsend, hrecv):
    at = place()
    me = at["s"]
    bar = pltpu.get_barrier_semaphore()
    greet_samp(at, bar)
    signal(bar, head_dev(at))
    pl.semaphore_wait(bar, NS)

    def copy(i):
        return rcopy(
            part_ref, full_ref.at[me], send.at[i], recv.at[i], samp_dev(at, (me + i) % NS)
        )

    def begin(i, _):
        copy(i).start()
        return 0

    def end(i, _):
        copy(i).wait()
        return 0

    lax.fori_loop(1, NS, begin, 0)
    other = rcopy(wt_ref, wo_ref, hsend, hrecv, head_dev(at))
    other.start()
    full_ref[me] = part_ref[...]
    lax.fori_loop(1, NS, end, 0)
    other.wait()


def gather_bias(part, weight_t):
    return pl.pallas_call(
        gather_kernel,
        out_shape=(
            jax.ShapeDtypeStruct((NS,) + part.shape, BF),
            jax.ShapeDtypeStruct(weight_t.shape, BF),
        ),
        in_specs=[pl.BlockSpec(memory_space=VMEM)] * 2,
        out_specs=[pl.BlockSpec(memory_space=VMEM)] * 2,
        scratch_shapes=[
            pltpu.SemaphoreType.DMA((NS,)),
            pltpu.SemaphoreType.DMA((NS,)),
            pltpu.SemaphoreType.DMA,
            pltpu.SemaphoreType.DMA,
        ],
        compiler_params=pltpu.CompilerParams(
            collective_id=0, has_side_effects=True, vmem_limit_bytes=16 * 2**20
        ),
        name="gather_bias",
    )(part, weight_t)


def scatter_kernel(
    gb_ref, mix_ref, act_ref, own_ref, oth_ref, mixo_ref, acto_ref, slots, send, recv, hsend, hrecv
):
    at = place()
    me = at["s"]
    bar = pltpu.get_barrier_semaphore()
    greet_samp(at, bar)
    signal(bar, head_dev(at))
    pl.semaphore_wait(bar, NS)

    def copy(i):
        to = (me + i) % NS
        return rcopy(gb_ref.at[to], slots.at[me], send.at[i], recv.at[i], samp_dev(at, to))

    def begin(i, _):
        copy(i).start()
        return 0

    def end(i, _):
        copy(i).wait()
        return 0

    lax.fori_loop(1, NS, begin, 0)
    hd = head_dev(at)
    mix = rcopy(mix_ref, mixo_ref, hsend.at[0], hrecv.at[0], hd)
    mix.start()
    act = rcopy(act_ref, acto_ref, hsend.at[1], hrecv.at[1], hd)
    act.start()
    slots[me] = gb_ref[me]
    lax.fori_loop(1, NS, end, 0)

    def add(i, total):
        return total + slots[i].astype(F32)

    own_ref[...] = lax.fori_loop(0, NS, add, jnp.zeros(own_ref.shape, F32)).astype(BF)
    rows = rcopy(own_ref, oth_ref, hsend.at[2], hrecv.at[2], hd)
    rows.start()
    mix.wait()
    act.wait()
    rows.wait()


def scatter_bias(gb, mix, act):
    return pl.pallas_call(
        scatter_kernel,
        out_shape=(
            jax.ShapeDtypeStruct(gb.shape[1:], BF),
            jax.ShapeDtypeStruct(gb.shape[1:], BF),
            jax.ShapeDtypeStruct(mix.shape, BF),
            jax.ShapeDtypeStruct(act.shape, BF),
        ),
        in_specs=[pl.BlockSpec(memory_space=VMEM)] * 3,
        out_specs=[pl.BlockSpec(memory_space=VMEM)] * 4,
        scratch_shapes=[
            pltpu.VMEM(gb.shape, BF),
            pltpu.SemaphoreType.DMA((NS,)),
            pltpu.SemaphoreType.DMA((NS,)),
            pltpu.SemaphoreType.DMA((3,)),
            pltpu.SemaphoreType.DMA((3,)),
        ],
        compiler_params=pltpu.CompilerParams(
            collective_id=1, has_side_effects=True, vmem_limit_bytes=16 * 2**20
        ),
        name="scatter_bias",
    )(gb, mix, act)


W_TILES, A_TILES, C_TILES = 1664, 1024, 64
W_HALF, A_HALF = W_TILES // 2, A_TILES // 2
GROUPS = (
    (0, 0, W_HALF // 2, "zxl"),
    (0, W_HALF // 2, W_HALF // 2, "xzl"),
    (1, 0, A_HALF // 2, "yzx"),
    (1, A_HALF // 2, A_HALF // 2, "yxz"),
    (2, 0, C_TILES, "yzx"),
)


def sum_kernel(w_ref, a_ref, c_ref, wo_ref, ao_ref, co_ref, *rest):
    rest = list(rest)
    wr, ar = rest[:2]
    work = rest[2:5]
    recvs = [rest[5 + 3 * g : 8 + 3 * g] for g in range(len(GROUPS))]
    csend, crecv, rsend, rrecv, gsend, grecv, fsend, frecv = rest[5 + 3 * len(GROUPS) :]
    outs = (wo_ref, ao_ref, co_ref)
    at = place()
    core = at["c"]
    bar = pltpu.get_barrier_semaphore()
    friends = [core_dev(at)]
    for axis, steps in (("z", 3), ("x", 3), ("y", 3)):
        friends += [peer_on(at, axis, i)[0] for i in range(1, steps + 1)]
    for dev in friends:
        signal(bar, dev)
    pl.semaphore_wait(bar, len(friends))

    first = []
    for i, (src, got, half) in enumerate(((w_ref, wr, W_HALF), (a_ref, ar, A_HALF))):
        cp = rcopy(
            src.at[pl.ds((1 - core) * half, half)], got, csend.at[i], crecv.at[i], core_dev(at)
        )
        cp.start()
        first.append(cp)
    work[2][...] = c_ref[...]

    base = [None] * len(GROUPS)
    pending = [None] * len(GROUPS)

    def rs_start(g, stage):
        buf, _, tiles, axes = GROUPS[g]
        axis = axes[stage]
        count = SIZE[axis]
        for a in axes[:stage]:
            tiles //= SIZE[a]
        part = tiles // count
        cps = []
        for i in range(1, count):
            dev, q = peer_on(at, axis, i)
            cp = rcopy(
                work[buf].at[pl.ds(base[g] + q * part, part)],
                recvs[g][stage].at[i - 1],
                rsend.at[g, stage, i - 1],
                rrecv.at[g, stage, i - 1],
                dev,
            )
            cp.start()
            cps.append(cp)
        pending[g] = cps
        return part

    def rs_end(g, stage, part):
        buf, _, _, axes = GROUPS[g]
        for cp in pending[g]:
            cp.wait()
        here = base[g] + at[axes[stage]] * part
        block = part
        while block > 16 and block % 2 == 0:
            block //= 2

        def add(i, _):
            rows = pl.ds(i * block, block)
            mine = pl.ds(here + i * block, block)
            total = work[buf][mine].astype(F32)
            for j in range(SIZE[axes[stage]] - 1):
                total = total + recvs[g][stage][j, rows].astype(F32)
            work[buf][mine] = total.astype(BF)
            return 0

        lax.fori_loop(0, part // block, add, 0)
        base[g] = here

    for i, (src, got, half) in enumerate(((w_ref, wr, W_HALF), (a_ref, ar, A_HALF))):
        first[i].wait()

        def add(j, _):
            rows = pl.ds(j * 16, 16)
            work[i][rows] = (
                src[pl.ds(core * half + j * 16, 16)].astype(F32) + got[rows].astype(F32)
            ).astype(BF)
            return 0

        lax.fori_loop(0, half // 16, add, 0)

    parts = [None] * len(GROUPS)
    for g in range(len(GROUPS)):
        base[g] = GROUPS[g][1]
        parts[g] = rs_start(g, 0)
    for stage in range(3):
        for g in range(len(GROUPS)):
            rs_end(g, stage, parts[g])
            if stage < 2:
                parts[g] = rs_start(g, stage + 1)

    shift = [core * W_HALF, core * A_HALF, 0]
    for g in range(len(GROUPS)):
        buf = GROUPS[g][0]
        outs[buf][pl.ds(shift[buf] + base[g], parts[g])] = work[buf][pl.ds(base[g], parts[g])]

    def ag_start(g, stage):
        buf, _, _, axes = GROUPS[g]
        axis = axes[stage]
        rows = pl.ds(shift[buf] + base[g], parts[g])
        cps = []
        for i in range(1, SIZE[axis]):
            dev, _ = peer_on(at, axis, i)
            cp = rcopy(
                outs[buf].at[rows],
                outs[buf].at[rows],
                gsend.at[g, stage, i - 1],
                grecv.at[g, stage, i - 1],
                dev,
            )
            cp.start()
            cps.append(cp)
        pending[g] = cps

    def ag_end(g, stage):
        axis = GROUPS[g][3][stage]
        for cp in pending[g]:
            cp.wait()
        base[g] = base[g] - at[axis] * parts[g]
        parts[g] = parts[g] * SIZE[axis]

    last = []
    for stage in (2, 1, 0):
        for g in range(len(GROUPS)):
            if stage < 2:
                ag_end(g, stage + 1)
            ag_start(g, stage)
    for g in range(len(GROUPS)):
        ag_end(g, 0)
        buf = GROUPS[g][0]
        if buf < 2:
            rows = pl.ds(shift[buf] + GROUPS[g][1], GROUPS[g][2])
            cp = rcopy(outs[buf].at[rows], outs[buf].at[rows], fsend.at[g], frecv.at[g], core_dev(at))
            cp.start()
            last.append(cp)
    for cp in last:
        cp.wait()


def sum_tiles(w, a, c):
    recvs = []
    for _, _, tiles, axes in GROUPS:
        for axis in axes:
            tiles //= SIZE[axis]
            recvs.append(pltpu.VMEM((SIZE[axis] - 1, tiles, 16, 128), BF))
    n = len(GROUPS)
    return pl.pallas_call(
        sum_kernel,
        out_shape=tuple(jax.ShapeDtypeStruct(t.shape, BF) for t in (w, a, c)),
        in_specs=[pl.BlockSpec(memory_space=VMEM)] * 3,
        out_specs=[pl.BlockSpec(memory_space=VMEM)] * 3,
        scratch_shapes=[
            pltpu.VMEM((W_HALF, 16, 128), BF),
            pltpu.VMEM((A_HALF, 16, 128), BF),
            pltpu.VMEM((W_HALF, 16, 128), BF),
            pltpu.VMEM((A_HALF, 16, 128), BF),
            pltpu.VMEM((C_TILES, 16, 128), BF),
            *recvs,
            pltpu.SemaphoreType.DMA((2,)),
            pltpu.SemaphoreType.DMA((2,)),
            pltpu.SemaphoreType.DMA((n, 3, 3)),
            pltpu.SemaphoreType.DMA((n, 3, 3)),
            pltpu.SemaphoreType.DMA((n, 3, 3)),
            pltpu.SemaphoreType.DMA((n, 3, 3)),
            pltpu.SemaphoreType.DMA((n,)),
            pltpu.SemaphoreType.DMA((n,)),
        ],
        compiler_params=pltpu.CompilerParams(
            collective_id=2, has_side_effects=True, vmem_limit_bytes=56 * 2**20
        ),
        name="sum_tiles",
    )(w, a, c)


SCALE = 1.0 / math.sqrt(HD)


def dot(a, b):
    return lax.dot_general(a, b, (((1,), (0,)), ((), ())), preferred_element_type=F32)


def dot_t(a, b):
    return lax.dot_general(a, b, (((1,), (1,)), ((), ())), preferred_element_type=F32)


def dot_l(a, b):
    return lax.dot_general(a, b, (((0,), (0,)), ((), ())), preferred_element_type=F32)


def mean(v):
    return jnp.mean(v, -1, keepdims=True)


def normalize(tensor):
    centered = tensor - mean(tensor)
    inv_std = lax.rsqrt(mean(centered * centered) + EPS)
    return (centered * inv_std, inv_std)


def norm_back(grad_hat, normed, inv_std):
    return inv_std * (grad_hat - mean(grad_hat) - normed * mean(grad_hat * normed))


def sigmoid(v):
    return 1.0 / (1.0 + jnp.exp(-v))


def flip(v):
    return v.astype(F32).T.astype(BF)


def loop(count, body):
    def step(i, _):
        body(i)
        return 0

    lax.fori_loop(0, count, step, 0)


def put(ref, start, value):
    rows, cols = value.shape
    n = rows // 16
    for j in range(cols // 128):
        ref[pl.ds(start + j * n, n)] = (
            value[:, j * 128 : (j + 1) * 128].astype(BF).reshape(n, 16, 128)
        )


T_QKVG, T_OUT, T_IN, T_HID, T_WSMALL = 0, 576, 720, 1296, 1584
T_ADA, T_ZERO, T_ASMALL = (0, 288), (576, 720), 864


def pair_kernel(pair_ref, gain_ref, wt_ref, part_ref, rows_ref):
    wt = wt_ref[...]
    gain = gain_ref[...]
    for r in range(pair_ref.shape[0]):
        hat, _ = normalize(pair_ref[r].astype(F32))
        low = (hat * gain).astype(BF)
        rows_ref[:, r, :] = dot_t(wt, low)[:8]
    part_ref[...] = rows_ref[...].reshape(part_ref.shape).astype(BF)


def block_kernel(
    act_ref,
    cot_ref,
    single_ref,
    mask_ref,
    ada_ref,
    zero_ref,
    wq_ref,
    out_ref,
    in_ref,
    hid_ref,
    adab_ref,
    zerob_ref,
    gain_ref,
    qb_ref,
    bias_ref,
    w_ref,
    a_ref,
    c_ref,
    mix_ref,
    actp_ref,
    gb_ref,
    shat,
    sinv,
    s_hi,
    s_lo,
    s_t,
    one_t,
    mg,
    ms,
    zg,
    hat,
    ain,
    tin,
    gao,
    gto,
    hidden,
    ffn,
    pre,
    zp,
    mixf,
    actf,
    gsh,
    zterm,
    qkv,
    gsig,
    ggat,
    gatt,
    acc,
    gheads,
    flipped,
    held,
    small_a,
    small_w,
):
    n = act_ref.shape[0]
    blocks = [slice(i * 256, (i + 1) * 256) for i in range(3)]
    small_a[...] = jnp.zeros(small_a.shape, F32)
    small_w[...] = jnp.zeros(small_w.shape, F32)

    def cond(i):
        rows = pl.ds(i * 32, 32)
        normed, inv = normalize(single_ref[rows].astype(F32))
        shat[rows] = normed
        sinv[rows] = jnp.broadcast_to(inv, (32, 128))
        for w in range(2):
            scaled = normed * gain_ref[w : w + 1]
            high = scaled.astype(BF)
            s_hi[w, rows] = high
            s_lo[w, rows] = (scaled - high.astype(F32)).astype(BF)

    loop(n // 32, cond)
    for w in range(2):
        s_t[w] = flip(s_hi[w])
    one_t[...] = flip(single_ref[...])
    for w in range(2):
        for b in blocks:
            later = slice(D + b.start, D + b.stop)
            pre_gate = dot(s_hi[w], ada_ref[w, :, b]) + dot(s_lo[w], ada_ref[w, :, b])
            mg[w, :, b] = sigmoid(pre_gate + adab_ref[w : w + 1, b])
            ms[w, :, b] = dot(s_hi[w], ada_ref[w, :, later]) + dot(s_lo[w], ada_ref[w, :, later])
            zg[w, :, b] = sigmoid(dot(single_ref[...], zero_ref[w, :, b]) + zerob_ref[w : w + 1, b])

    def norm_in(i):
        rows = pl.ds(i * 16, 16)
        normed, _ = normalize(act_ref[rows].astype(F32))
        hat[rows] = normed
        ain[rows] = (mg[0, rows] * normed + ms[0, rows]).astype(BF)
        tin[rows] = (mg[1, rows] * normed + ms[1, rows]).astype(BF)
        g = cot_ref[rows].astype(F32)
        gao[rows] = (zg[0, rows] * g).astype(BF)
        gto[rows] = (zg[1, rows] * g).astype(BF)

    loop(n // 16, norm_in)

    def branch_out(w, b, part):
        gate = zg[w, :, b]
        share = gate * part
        mixf[:, b] = share if w == 1 else mixf[:, b] + share
        grad = cot_ref[:, b].astype(F32) * share * (1.0 - gate)
        zp[:, b] = grad.astype(BF)
        for j in range(2):
            small_a[6 * w + b.start // 128 + j + 12 : 6 * w + b.start // 128 + j + 13] = jnp.sum(
                grad[:, j * 128 : (j + 1) * 128], 0, keepdims=True
            )

    def branch_in(w, b, grad_in):
        gate = mg[w, :, b]
        share = gate * grad_in
        actf[:, b] = share if w == 1 else actf[:, b] + share
        grad = share * hat[:, b] * (1.0 - gate)
        pre[:, b] = grad.astype(BF)
        pre[:, D + b.start : D + b.stop] = grad_in.astype(BF)
        for j in range(2):
            small_a[6 * w + b.start // 128 + j : 6 * w + b.start // 128 + j + 1] = jnp.sum(
                grad[:, j * 128 : (j + 1) * 128], 0, keepdims=True
            )

    def conditioned(w):
        for i in range(6):
            b = slice(i * 256, (i + 1) * 256)
            put(a_ref, T_ADA[w] + i * 48, dot(s_t[w], pre[:, b]))
        for i, b in enumerate(blocks):
            put(a_ref, T_ZERO[w] + i * 48, dot(one_t[...], zp[:, b]))
        for j in range(3):
            b = slice(j * 128, (j + 1) * 128)
            scaled = dot_t(pre[...], ada_ref[w, b, :])
            small_a[24 + 3 * w + j : 25 + 3 * w + j] = jnp.sum(scaled * shat[:, b], 0, keepdims=True)
            share = scaled * gain_ref[w : w + 1, b]
            through = dot_t(zp[...], zero_ref[w, b, :])
            gsh[:, b] = share if w == 1 else gsh[:, b] + share
            zterm[:, b] = through if w == 1 else zterm[:, b] + through

    for b in blocks:
        gate_in = dot(tin[...], in_ref[0, :, b])
        up_in = dot(tin[...], in_ref[1, :, b])
        grad_hidden = dot_t(gto[...], hid_ref[b, :])
        sig = sigmoid(gate_in)
        silu = gate_in * sig
        hidden[:, b] = (silu * up_in).astype(BF)
        ffn[:, b] = (grad_hidden * up_in * sig * (1.0 + gate_in * (1.0 - sig))).astype(BF)
        ffn[:, D + b.start : D + b.stop] = (grad_hidden * silu).astype(BF)
    for b in blocks:
        branch_out(1, b, dot(hidden[...], hid_ref[:, b]))
    flipped[...] = flip(hidden[...])
    for i, b in enumerate(blocks):
        put(w_ref, T_HID + i * 96, dot(flipped[...], gto[:, b]))
    flipped[...] = flip(tin[...])
    for i in range(6):
        put(w_ref, T_IN + i * 96, dot(flipped[...], ffn[:, i * 256 : (i + 1) * 256]))
    for b in blocks:
        branch_in(1, b, dot_t(ffn[:, :D], in_ref[0, b, :]) + dot_t(ffn[:, D:], in_ref[1, b, :]))
    conditioned(1)

    qkv[0] = (dot(ain[...], wq_ref[0]) + qb_ref[...]).astype(BF)
    qkv[1] = dot(ain[...], wq_ref[1]).astype(BF)
    qkv[2] = dot(ain[...], wq_ref[2]).astype(BF)
    gsig[...] = sigmoid(dot(ain[...], wq_ref[3]))
    ggat[...] = dot_t(gao[...], out_ref[...])
    gatt[...] = (ggat[...] * gsig[...]).astype(BF)
    acc[...] = jnp.zeros(acc.shape, F32)
    lane = lax.broadcasted_iota(jnp.int32, (1, 256), 1)
    for h in range(8):
        lo = 0 if h < 5 else 128
        win = slice(lo, lo + 256)
        first = h * HD - lo
        mine = (lane >= first) & (lane < first + HD)
        pick = jnp.where(mine, 1.0, 0.0).astype(BF)
        q_m = qkv[0, :, win] * pick
        k_m = qkv[1, :, win] * pick
        v_m = qkv[2, :, win] * pick
        g_m = gatt[:, win] * pick
        pair_rows = bias_ref[:, (h // 2) * 16 : (h // 2) * 16 + 16, :].astype(F32)
        bias = pair_rows[:, (h % 2) * 8 : (h % 2) * 8 + 8, :].reshape(n, n)
        scores = dot_t(q_m, qkv[1, :, win]) * SCALE + bias + mask_ref[...]
        top = jnp.max(scores, -1, keepdims=True)
        weights = jnp.exp(scores - top)
        probs = weights * (1.0 / jnp.sum(weights, -1, keepdims=True))
        low = probs.astype(BF)
        acc[0, :, win] += dot(low, v_m)
        grad_probs = dot_t(g_m, qkv[2, :, win])
        delta = jnp.sum(probs * grad_probs, -1, keepdims=True)
        grad_s = probs * (grad_probs - delta)
        grad_low = grad_s.astype(BF)
        acc[1, :, win] += dot(grad_low, k_m)
        acc[2, :, win] += dot_l(grad_low, q_m)
        acc[3, :, win] += dot_l(low, g_m)
        split = grad_s.reshape(NS, 8, n)
        if h % 2 == 0:
            held[...] = split
        else:
            gb_ref[:, (h // 2) * 16 : (h // 2) * 16 + 16, :] = jnp.concatenate(
                [held[...], split], 1
            ).astype(BF)
    attended = acc[0]
    gated = (gsig[...] * attended).astype(BF)
    gheads[:, 1152:] = (ggat[...] * attended * gsig[...] * (1.0 - gsig[...])).astype(BF)
    grad_q = (acc[1] * SCALE).astype(BF)
    gheads[:, :384] = grad_q
    gheads[:, 384:768] = (acc[2] * SCALE).astype(BF)
    gheads[:, 768:1152] = acc[3].astype(BF)
    for j in range(3):
        small_w[j : j + 1] = jnp.sum(
            grad_q[:, j * 128 : (j + 1) * 128].astype(F32), 0, keepdims=True
        )
    for b in blocks:
        branch_out(0, b, dot(gated, out_ref[:, b]))
    mix_ref[...] = mixf[...].astype(BF)
    flipped[:384] = flip(gated)
    for i, b in enumerate(blocks):
        put(w_ref, T_OUT + i * 48, dot(flipped[:384], gao[:, b]))
    flipped[...] = flip(ain[...])
    for i in range(6):
        put(w_ref, T_QKVG + i * 96, dot(flipped[...], gheads[:, i * 256 : (i + 1) * 256]))
    for b in blocks:
        total = dot_t(gheads[:, :384], wq_ref[0, b, :])
        for k in range(1, 4):
            total = total + dot_t(gheads[:, k * 384 : (k + 1) * 384], wq_ref[k, b, :])
        branch_in(0, b, total)
    actp_ref[...] = actf[...].astype(BF)
    conditioned(0)

    grad_single = norm_back(gsh[...], shat[...], sinv[:, :1]) + zterm[...]
    put(c_ref, 0, grad_single)
    c_ref[48:] = jnp.zeros((C_TILES - 48, 16, 128), BF)
    w_ref[T_WSMALL:] = jnp.zeros((W_TILES - T_WSMALL, 16, 128), BF)
    a_ref[T_ASMALL:] = jnp.zeros((A_TILES - T_ASMALL, 16, 128), BF)
    w_ref[T_WSMALL] = small_w[...].astype(BF)
    a_ref[T_ASMALL : T_ASMALL + 2] = small_a[...].astype(BF).reshape(2, 16, 128)


def whole(shape, dtype):
    return jax.ShapeDtypeStruct(shape, dtype)


def pair_bias_rows(pair, gain, weight_t):
    return pl.pallas_call(
        pair_kernel,
        out_shape=whole((64, 256), BF),
        in_specs=[pl.BlockSpec(memory_space=VMEM)] * 3,
        out_specs=pl.BlockSpec(memory_space=VMEM),
        scratch_shapes=[pltpu.VMEM((8, 8, 256), F32)],
        compiler_params=pltpu.CompilerParams(vmem_limit_bytes=16 * 2**20),
        name="pair_bias_rows",
    )(pair, gain, weight_t)


def run_block(*args):
    n = 256
    return pl.pallas_call(
        block_kernel,
        out_shape=(
            whole((W_TILES, 16, 128), BF),
            whole((A_TILES, 16, 128), BF),
            whole((C_TILES, 16, 128), BF),
            whole((n, D), BF),
            whole((n, D), BF),
            whole((NS, 64, n), BF),
        ),
        in_specs=[pl.BlockSpec(memory_space=VMEM)] * len(args),
        out_specs=[pl.BlockSpec(memory_space=VMEM)] * 6,
        scratch_shapes=[
            pltpu.VMEM((n, 384), F32),
            pltpu.VMEM((n, 128), F32),
            pltpu.VMEM((2, n, 384), BF),
            pltpu.VMEM((2, n, 384), BF),
            pltpu.VMEM((2, 384, n), BF),
            pltpu.VMEM((384, n), BF),
            pltpu.VMEM((2, n, D), F32),
            pltpu.VMEM((2, n, D), F32),
            pltpu.VMEM((2, n, D), F32),
            pltpu.VMEM((n, D), F32),
            pltpu.VMEM((n, D), BF),
            pltpu.VMEM((n, D), BF),
            pltpu.VMEM((n, D), BF),
            pltpu.VMEM((n, D), BF),
            pltpu.VMEM((n, D), BF),
            pltpu.VMEM((n, 2 * D), BF),
            pltpu.VMEM((n, 2 * D), BF),
            pltpu.VMEM((n, D), BF),
            pltpu.VMEM((n, D), F32),
            pltpu.VMEM((n, D), F32),
            pltpu.VMEM((n, 384), F32),
            pltpu.VMEM((n, 384), F32),
            pltpu.VMEM((3, n, 384), BF),
            pltpu.VMEM((n, 384), F32),
            pltpu.VMEM((n, 384), F32),
            pltpu.VMEM((n, 384), BF),
            pltpu.VMEM((4, n, 384), F32),
            pltpu.VMEM((n, 1536), BF),
            pltpu.VMEM((D, n), BF),
            pltpu.VMEM((NS, 8, n), F32),
            pltpu.VMEM((32, 128), F32),
            pltpu.VMEM((16, 128), F32),
        ],
        compiler_params=pltpu.CompilerParams(vmem_limit_bytes=60 * 2**20),
        name="block",
    )(*args)


def pair_back_kernel(
    pair_ref, gain_ref, wt_ref, own_ref, all_ref, grad_ref, small_ref, rows_own, rows_all
):
    gain = gain_ref[...]
    wt = wt_ref[...]
    rows_own[...] = own_ref[...].astype(F32).reshape(8, 8, 256)
    rows_all[...] = all_ref[...].astype(F32).reshape(16, 8, 256)
    weight = jnp.zeros((8, 128), F32)
    total = jnp.zeros((1, 128), F32)
    for r in range(8):
        hat, inv = normalize(pair_ref[r].astype(F32))
        low = (hat * gain).astype(BF)
        weight = weight + dot(rows_own[:, r, :].astype(BF), low)
        grad_low = dot_l(rows_all[:, r, :].astype(BF), wt)
        total = total + jnp.sum(grad_low * hat, 0, keepdims=True)
        grad_ref[r] = norm_back(grad_low * gain, hat, inv)
    small_ref[:8] = weight
    small_ref[8:] = jnp.broadcast_to(total, (8, 128))


def pair_back(pair, gain, wt, own, every):
    return pl.pallas_call(
        pair_back_kernel,
        out_shape=(whole((8, 256, 128), F32), whole((16, 128), F32)),
        in_specs=[pl.BlockSpec(memory_space=VMEM)] * 5,
        out_specs=[pl.BlockSpec(memory_space=VMEM)] * 2,
        scratch_shapes=[pltpu.VMEM((8, 8, 256), F32), pltpu.VMEM((16, 8, 256), F32)],
        compiler_params=pltpu.CompilerParams(vmem_limit_bytes=16 * 2**20),
        name="pair_back",
    )(pair, gain, wt, own, every)


def finish_kernel(
    w_ref,
    a_ref,
    c_ref,
    act_ref,
    cot_ref,
    mix_ref,
    mixo_ref,
    actp_ref,
    acto_ref,
    mixed_out,
    act_out,
    single_out,
    ada_out,
    zero_out,
    qkvg_out,
    wout_out,
    in_out,
    hid_out,
    small_out,
    mixed,
    act,
    single,
    ada,
    zero,
    qkvg,
    wout,
    win,
    hid,
    small,
    sems,
):
    copies = []

    def leave(src, dst):
        cp = pltpu.make_async_copy(src, dst, sems.at[len(copies)])
        cp.start()
        copies.append(cp)

    def get(ref, start, rows, cols=128):
        count = rows // 16
        return ref[pl.ds(start, count)].astype(F32).reshape(rows, 128)

    for k in range(4):
        for j in range(3):
            qkvg[:, k, j * 128 : (j + 1) * 128] = get(w_ref, T_QKVG + (k * 3 + j) * 48, 768)
    leave(qkvg, qkvg_out)
    for k in range(2):
        for j in range(6):
            win[:, k, j * 128 : (j + 1) * 128] = get(w_ref, T_IN + (k * 6 + j) * 48, 768)
    leave(win, in_out)
    for j in range(6):
        hid[:, j * 128 : (j + 1) * 128] = get(w_ref, T_HID + j * 48, 768)
    leave(hid, hid_out)
    for w in range(2):
        for j in range(12):
            ada[w, :, j * 128 : (j + 1) * 128] = get(a_ref, T_ADA[w] + j * 24, 384)
        leave(ada.at[w], ada_out.at[w])
    for w in range(2):
        for j in range(6):
            zero[w, :, j * 128 : (j + 1) * 128] = get(a_ref, T_ZERO[w] + j * 24, 384)
        leave(zero.at[w], zero_out.at[w])
    for j in range(6):
        wout[:, j * 128 : (j + 1) * 128] = get(w_ref, T_OUT + j * 24, 384)
    leave(wout, wout_out)
    for j in range(3):
        single[:, j * 128 : (j + 1) * 128] = get(c_ref, j * 16, 256)
    leave(single, single_out)
    small[:16] = w_ref[T_WSMALL].astype(F32)
    small[16:] = a_ref[T_ASMALL : T_ASMALL + 2].astype(F32).reshape(32, 128)
    leave(small, small_out)

    def last(i):
        rows = pl.ds(i * 16, 16)
        value = act_ref[rows].astype(F32)
        mixed[rows] = (value + (mix_ref[rows].astype(F32) + mixo_ref[rows].astype(F32))).astype(BF)
        normed, inv = normalize(value)
        grad = actp_ref[rows].astype(F32) + acto_ref[rows].astype(F32)
        act[rows] = cot_ref[rows].astype(F32) + norm_back(grad, normed, inv)

    loop(16, last)
    leave(mixed, mixed_out)
    leave(act, act_out)
    for cp in copies:
        cp.wait()


def finish(*args):
    shapes = [
        whole((256, D), BF),
        whole((256, D), F32),
        whole((256, 384), F32),
        whole((2, 384, 2 * D), F32),
        whole((2, 384, D), F32),
        whole((D, 4, 384), F32),
        whole((384, D), F32),
        whole((D, 2, D), F32),
        whole((D, D), F32),
        whole((48, 128), F32),
    ]
    return pl.pallas_call(
        finish_kernel,
        out_shape=tuple(shapes),
        in_specs=[pl.BlockSpec(memory_space=VMEM)] * len(args),
        out_specs=[pl.BlockSpec(memory_space=pl.ANY)] * len(shapes),
        scratch_shapes=[pltpu.VMEM(s.shape, s.dtype) for s in shapes]
        + [pltpu.SemaphoreType.DMA((16,))],
        compiler_params=pltpu.CompilerParams(vmem_limit_bytes=60 * 2**20),
        name="finish",
    )(*args)


def local(
    activations,
    conditioning,
    pair,
    counts,
    ada_weight,
    ada_bias,
    cond_gain,
    zero_weight,
    zero_bias,
    qkvg_weight,
    q_bias,
    out_weight,
    in_weight,
    hid_weight,
    pair_gain,
    bias_weight,
    cotangent,
):
    act = activations[0, 0]
    cot = cotangent[0, 0]
    gain = pair_gain.astype(F32)[None]
    weight_t = jnp.pad(bias_weight.T, ((0, 8), (0, 0)))
    part = pair_bias_rows(pair[0], gain, weight_t)
    bias_all, weight_o = gather_bias(part, weight_t)
    mask = jnp.where(lax.broadcasted_iota(jnp.int32, (1, 256), 1) < counts[0], 0.0, -1e9)
    w, a, c, mix, actp, gb = run_block(
        act,
        cot,
        conditioning[0],
        mask.astype(F32),
        ada_weight,
        zero_weight,
        qkvg_weight.transpose(1, 0, 2),
        out_weight,
        in_weight.transpose(1, 0, 2),
        hid_weight,
        ada_bias.astype(F32),
        zero_bias.astype(F32),
        cond_gain.astype(F32),
        q_bias.astype(F32)[None],
        bias_all,
    )
    own, other, mixo, acto = scatter_bias(gb, mix, actp)
    first = lax.axis_index("head") == 0
    every = jnp.concatenate([jnp.where(first, own, other), jnp.where(first, other, own)], 0)
    wt_all = jnp.concatenate(
        [
            jnp.where(first, weight_t[:8], weight_o[:8]),
            jnp.where(first, weight_o[:8], weight_t[:8]),
        ],
        0,
    )
    grad_pair, small = pair_back(pair[0], gain, wt_all, own, every)
    w = w.at[T_WSMALL, 3:11].set(small[:8].astype(BF))
    a = a.at[T_ASMALL + 1, 14].set((small[8] * 0.5).astype(BF))
    w, a, c = sum_tiles(w, a, c)
    mixed, act_g, single, ada, zero, qkvg, wout, win, hid, sm = finish(
        w, a, c, act, cot, mix, mixo, actp, acto
    )
    return (
        mixed[None, None],
        act_g[None, None],
        single[None],
        grad_pair[None],
        ada,
        sm[16:28].reshape(2, D),
        sm[40:46].reshape(2, 384),
        zero,
        sm[28:40].reshape(2, D),
        qkvg,
        sm[0:3].reshape(384),
        wout,
        win,
        hid,
        sm[46],
        sm[3:11].T,
    )


def solution(mesh):
    placed = (
        P("cplx", "samp", None, None),
        P("cplx", None, None),
        P("cplx", "samp", None, None),
        P("cplx"),
        P(),
        P(),
        P(),
        P(),
        P(),
        P(None, None, "head"),
        P("head"),
        P("head", None),
        P(None, None, "head"),
        P("head", None),
        P(),
        P(None, "head"),
        P("cplx", "samp", None, None),
    )
    return jax.shard_map(
        local,
        mesh=mesh,
        in_specs=placed,
        out_specs=(
            P("cplx", "samp", None, None),
            P("cplx", "samp", None, None),
            P("cplx", None, None),
            P("cplx", "samp", None, None),
            P(),
            P(),
            P(),
            P(),
            P(),
            P(None, None, "head"),
            P("head"),
            P("head", None),
            P(None, None, "head"),
            P("head", None),
            P(),
            P(None, "head"),
        ),
        check_vma=False,
    )
```

```python
import functools
import math

import jax
import jax.numpy as jnp
from jax import lax
from jax.experimental import pallas as pl
from jax.experimental.pallas import tpu as pltpu
from jax.sharding import PartitionSpec as P

D = 768
HD = 48
EPS = 1e-05
HIGH = lax.Precision.HIGHEST
MESH = pl.DeviceIdType.MESH
BF = jnp.bfloat16
F32 = jnp.float32
NS = 32
VMEM = pltpu.VMEM


def place():
    samp = lax.axis_index("samp")
    return {
        "c": lax.axis_index("cplx"),
        "h": lax.axis_index("head"),
        "s": samp,
        "z": samp // 8,
        "l": (samp // 4) % 2,
        "x": samp % 4,
        "y": lax.axis_index("head") * 2 + (samp // 4) % 2,
    }


SIZE = {"z": 4, "x": 4, "y": 4, "l": 2}


def peer_on(at, axis, step):
    z, x, lo, hd = at["z"], at["x"], at["l"], at["h"]
    q = (at[axis] + step) % SIZE[axis]
    if axis == "z":
        z = q
    elif axis == "x":
        x = q
    elif axis == "l":
        lo = q
    else:
        hd, lo = q // 2, q % 2
    return {"cplx": at["c"], "samp": z * 8 + lo * 4 + x, "head": hd}, q


def signal(bar, dev):
    pl.semaphore_signal(bar, inc=1, device_id=dev, device_id_type=MESH)


def samp_dev(at, other):
    return {"cplx": at["c"], "samp": other, "head": at["h"]}


def head_dev(at):
    return {"cplx": at["c"], "samp": at["s"], "head": 1 - at["h"]}


def core_dev(at):
    return {"cplx": 1 - at["c"], "samp": at["s"], "head": at["h"]}


def rcopy(src, dst, send, recv, dev):
    return pltpu.make_async_remote_copy(
        src_ref=src, dst_ref=dst, send_sem=send, recv_sem=recv, device_id=dev, device_id_type=MESH
    )


def greet_samp(at, bar):
    def one(i, _):
        signal(bar, samp_dev(at, (at["s"] + i) % NS))
        return 0

    lax.fori_loop(1, NS, one, 0)


SCALE = 1.0 / math.sqrt(HD)


def dot(a, b):
    return lax.dot_general(a, b, (((1,), (0,)), ((), ())), preferred_element_type=F32)


def dot_t(a, b):
    return lax.dot_general(a, b, (((1,), (1,)), ((), ())), preferred_element_type=F32)


def dot_l(a, b):
    return lax.dot_general(a, b, (((0,), (0,)), ((), ())), preferred_element_type=F32)


def mean(v):
    return jnp.mean(v, -1, keepdims=True)


def normalize(tensor):
    centered = tensor - mean(tensor)
    inv_std = lax.rsqrt(mean(centered * centered) + EPS)
    return (centered * inv_std, inv_std)


def norm_back(grad_hat, normed, inv_std):
    return inv_std * (grad_hat - mean(grad_hat) - normed * mean(grad_hat * normed))


def sigmoid(v):
    return 1.0 / (1.0 + jnp.exp(-v))


def flip(v):
    return v.astype(F32).T.astype(BF)


def loop(count, body):
    def step(i, _):
        body(i)
        return 0

    lax.fori_loop(0, count, step, 0)


def put(ref, start, value):
    rows, cols = value.shape
    n = rows // 16
    for j in range(cols // 128):
        ref[pl.ds(start + j * n, n)] = (
            value[:, j * 128 : (j + 1) * 128].astype(BF).reshape(n, 16, 128)
        )


TILES = (832, 384, 768, 512, 64)
HALF = (416, 192, 384, 256, 64)
GROUPS = (
    (0, 0, 192, "zxl"),
    (0, 192, 224, "xzl"),
    (1, 0, 128, "yzx"),
    (1, 128, 64, "zyx"),
    (2, 0, 192, "zxl"),
    (2, 192, 192, "xzl"),
    (3, 0, 192, "yxz"),
    (3, 192, 64, "xyz"),
    (4, 0, 64, "yzx"),
)
FIRST = (0, 1, 2, 3)
SECOND = (4, 5, 6, 7, 8)
T_IN, T_HID = 0, 576
T_ADA, T_ZERO = (0, 0), (288, 288)
T_QKVG, T_OUT, T_HID2, T_WPAD = 0, 576, 720, 752
T_ZERO2, T_SMALL, T_APAD = 432, 480, 482

INPUTS = (
    ("pair", (8, 256, 128)),
    ("pgain", (128,)),
    ("wt", (8, 128)),
    ("single", (256, 384)),
    ("gain", (2, 384)),
    ("ada", (2, 384, 1536)),
    ("adab", (2, 768)),
    ("zero", (2, 384, 768)),
    ("zerob", (2, 768)),
    ("act", (256, 768)),
    ("cot", (256, 768)),
    ("win", (2, 768, 768)),
    ("hid", (768, 768)),
    ("wq", (4, 768, 384)),
    ("qb", (384,)),
    ("wout", (384, 768)),
)
N = 256
SCRATCH = (
    ("rows", (8, 8, N), F32),
    ("part", (64, N), BF),
    ("bias", (NS, 64, N), BF),
    ("wall", (2, 16, 128), BF),
    ("shat", (N, 384), F32),
    ("sinv", (N, 128), F32),
    ("s_hi", (2, N, 384), BF),
    ("s_lo", (2, N, 384), BF),
    ("s_t", (2, 384, N), BF),
    ("one_t", (384, N), BF),
    ("mg", (2, N, D), F32),
    ("ms", (2, N, D), F32),
    ("zg", (2, N, D), F32),
    ("hat", (N, D), F32),
    ("ain", (N, D), BF),
    ("tin", (N, D), BF),
    ("gao", (N, D), BF),
    ("gto", (N, D), BF),
    ("hidden", (N, D), BF),
    ("ffn", (N, 2 * D), BF),
    ("pre", (N, 2 * D), BF),
    ("zp", (N, D), BF),
    ("mixf", (N, D), F32),
    ("actf", (N, D), F32),
    ("mixs", (N, D), BF),
    ("mixr", (N, D), BF),
    ("acts", (N, D), BF),
    ("actr", (N, D), BF),
    ("gsh", (N, 384), F32),
    ("zterm", (N, 384), F32),
    ("qkv", (3, N, 384), BF),
    ("gsig", (N, 384), F32),
    ("ggat", (N, 384), F32),
    ("gatt", (N, 384), BF),
    ("acc", (4, N, 384), F32),
    ("gheads", (N, 1536), BF),
    ("flipped", (D, N), BF),
    ("held", (NS, 8, N), F32),
    ("small_a", (32, 128), F32),
    ("small_w", (16, 128), F32),
    ("gb", (2, NS, 32, N), BF),
    ("gb1", (2, 3, 8, 32, N), BF),
    ("gb2", (2, 7, 32, N), BF),
    ("gball", (2, 64, N), BF),
    ("gpair", (8, N, 128), F32),
    ("slot", (4, 4, 16, 128), F32),
)
SEMS = (
    ("ld", (len(INPUTS),)),
    ("bs", (NS,)),
    ("br", (NS,)),
    ("hs", (4,)),
    ("hr", (4,)),
    ("cs", (5,)),
    ("cr", (5,)),
    ("rs", (len(GROUPS), 3, 3)),
    ("rr", (len(GROUPS), 3, 3)),
    ("gs", (len(GROUPS), 3, 3)),
    ("gr", (len(GROUPS), 3, 3)),
    ("fs", (len(GROUPS),)),
    ("fr", (len(GROUPS),)),
    ("b1s", (2, 3)),
    ("b1r", (2, 3)),
    ("b2s", (2, 7)),
    ("b2r", (2, 7)),
    ("ss", (4, 3)),
    ("sr", (4, 3)),
    ("out", (12,)),
)
OUTPUTS = tuple(("sum%d" % i, (t, 16, 128), BF) for i, t in enumerate(TILES)) + (
    ("small_o", (16, 128), F32),
    ("mixed_o", (N, D), BF),
    ("act_o", (N, D), F32),
    ("pair_o", (8, N, 128), F32),
)


class Refs:
    pass


def recv_shapes():
    shapes = []
    for g, (_, _, tiles, axes) in enumerate(GROUPS):
        for s, axis in enumerate(axes):
            tiles //= SIZE[axis]
            shapes.append(((g, s), (SIZE[axis] - 1, tiles, 16, 128)))
    return shapes


class Sums:
    def __init__(self, r, at):
        self.r, self.at = r, at
        core = at["c"]
        self.shift = [core * HALF[b] if b < 4 else 0 for b in range(5)]
        self.base = [None] * len(GROUPS)
        self.part = [None] * len(GROUPS)
        self.pending = [None] * len(GROUPS)
        self.pairs = {}
        self.last = {}

    def core_start(self, buf):
        r, at, half = self.r, self.at, HALF[buf]
        cp = rcopy(
            r.tiles[buf].at[pl.ds((1 - at["c"]) * half, half)],
            r.sums[buf].at[pl.ds((1 - at["c"]) * half, half)],
            r.cs.at[buf],
            r.cr.at[buf],
            core_dev(at),
        )
        cp.start()
        self.pairs[buf] = cp

    def core_end(self, buf):
        r, half, start = self.r, HALF[buf], self.shift[buf]
        self.pairs[buf].wait()

        def add(j):
            rows = pl.ds(start + j * 16, 16)
            r.tiles[buf][rows] = (
                r.tiles[buf][rows].astype(F32) + r.sums[buf][rows].astype(F32)
            ).astype(BF)

        loop(half // 16, add)

    def rs_start(self, g, stage):
        r, at = self.r, self.at
        buf, start, tiles, axes = GROUPS[g]
        axis = axes[stage]
        count = SIZE[axis]
        for a in axes[:stage]:
            tiles //= SIZE[a]
        if stage == 0:
            self.base[g] = self.shift[buf] + start
        part = tiles // count
        cps = []
        for i in range(1, count):
            dev, q = peer_on(at, axis, i)
            cp = rcopy(
                r.tiles[buf].at[pl.ds(self.base[g] + q * part, part)],
                r.recv[g, stage].at[i - 1],
                r.rs.at[g, stage, i - 1],
                r.rr.at[g, stage, i - 1],
                dev,
            )
            cp.start()
            cps.append(cp)
        self.pending[g] = cps
        self.part[g] = part

    def rs_end(self, g, stage):
        r = self.r
        buf, _, _, axes = GROUPS[g]
        part = self.part[g]
        for cp in self.pending[g]:
            cp.wait()
        here = self.base[g] + self.at[axes[stage]] * part
        block = max(b for b in range(1, 17) if part % b == 0)

        def add(i):
            rows = pl.ds(i * block, block)
            mine = pl.ds(here + i * block, block)
            total = r.tiles[buf][mine].astype(F32)
            for j in range(SIZE[axes[stage]] - 1):
                total = total + r.recv[g, stage][j, rows].astype(F32)
            to = r.sums if stage == 2 else r.tiles
            to[buf][mine] = total.astype(BF)

        loop(part // block, add)
        self.base[g] = here

    def ag_start(self, g, stage):
        r = self.r
        buf, _, _, axes = GROUPS[g]
        rows = pl.ds(self.base[g], self.part[g])
        cps = []
        for i in range(1, SIZE[axes[stage]]):
            dev, _ = peer_on(self.at, axes[stage], i)
            cp = rcopy(
                r.sums[buf].at[rows],
                r.sums[buf].at[rows],
                r.gs.at[g, stage, i - 1],
                r.gr.at[g, stage, i - 1],
                dev,
            )
            cp.start()
            cps.append(cp)
        self.pending[g] = cps

    def ag_end(self, g, stage):
        axis = GROUPS[g][3][stage]
        for cp in self.pending[g]:
            cp.wait()
        self.base[g] = self.base[g] - self.at[axis] * self.part[g]
        self.part[g] = self.part[g] * SIZE[axis]

    def share_start(self, g):
        r = self.r
        buf, start, tiles, _ = GROUPS[g]
        if buf < 4:
            rows = pl.ds(self.shift[buf] + start, tiles)
            cp = rcopy(
                r.sums[buf].at[rows], r.sums[buf].at[rows], r.fs.at[g], r.fr.at[g], core_dev(self.at)
            )
            cp.start()
            self.last[g] = cp

    def share_end(self, g):
        if g in self.last:
            self.last[g].wait()


def mega_kernel(*refs):
    r = Refs()
    refs = list(refs)

    def take(count):
        got = refs[:count]
        del refs[:count]
        return got

    counts_ref = take(1)[0]
    hbm = take(len(INPUTS))
    outs = dict(zip([o[0] for o in OUTPUTS], take(len(OUTPUTS))))
    for (name, _), ref in zip(INPUTS, take(len(INPUTS))):
        setattr(r, name, ref)
    for (name, _, _), ref in zip(SCRATCH, take(len(SCRATCH))):
        setattr(r, name, ref)
    r.tiles = take(5)
    r.sums = take(5)
    r.recv = {}
    for (key, _), ref in zip(recv_shapes(), take(len(recv_shapes()))):
        r.recv[key] = ref
    for (name, _), ref in zip(SEMS, take(len(SEMS))):
        setattr(r, name, ref)

    at = place()
    me, hd = at["s"], at["h"]
    blocks = [slice(i * 256, (i + 1) * 256) for i in range(3)]
    loads = {}
    for i, (name, _) in enumerate(INPUTS):
        cp = pltpu.make_async_copy(hbm[i], getattr(r, name), r.ld.at[i])
        cp.start()
        loads[name] = cp

    def need(*names):
        for name in names:
            loads[name].wait()

    copies = []

    def leave(src, name):
        cp = pltpu.make_async_copy(src, outs[name], r.out.at[len(copies)])
        cp.start()
        copies.append(cp)

    need("pair", "pgain", "wt")
    pgain = r.pgain[...].astype(F32).reshape(1, 128)
    wt = r.wt[...]
    r.wall[hd] = jnp.concatenate([wt.astype(F32), jnp.zeros((8, 128), F32)], 0).astype(BF)
    for i in range(8):
        normed, _ = normalize(r.pair[i].astype(F32))
        r.rows[:, i, :] = dot_t(wt, (normed * pgain).astype(BF))
    r.part[...] = r.rows[...].reshape(64, N).astype(BF)
    r.bias[me] = r.part[...]
    bar = pltpu.get_barrier_semaphore()
    greet_samp(at, bar)
    cross = {"cplx": at["c"], "samp": at["z"] * 8 + (1 - at["l"]) * 4 + at["x"], "head": 1 - hd}
    for dev in (head_dev(at), core_dev(at), cross):
        signal(bar, dev)
    pl.semaphore_wait(bar, NS + 2)

    def bias_copy(i):
        return rcopy(
            r.part, r.bias.at[me], r.bs.at[i], r.br.at[i], samp_dev(at, (me + i) % NS)
        )

    loop(NS - 1, lambda i: bias_copy(i + 1).start())
    wt_copy = rcopy(r.wall.at[hd], r.wall.at[hd], r.hs.at[0], r.hr.at[0], head_dev(at))
    wt_copy.start()

    r.small_a[...] = jnp.zeros(r.small_a.shape, F32)
    r.small_w[...] = jnp.zeros(r.small_w.shape, F32)
    need("single", "gain")
    gains = r.gain[...].astype(F32)

    def cond(i):
        rows = pl.ds(i * 32, 32)
        normed, inv = normalize(r.single[rows].astype(F32))
        r.shat[rows] = normed
        r.sinv[rows] = jnp.broadcast_to(inv, (32, 128))
        for w in range(2):
            scaled = normed * gains[w : w + 1]
            high = scaled.astype(BF)
            r.s_hi[w, rows] = high
            r.s_lo[w, rows] = (scaled - high.astype(F32)).astype(BF)

    loop(N // 32, cond)
    for w in range(2):
        r.s_t[w] = flip(r.s_hi[w])
    r.one_t[...] = flip(r.single[...])
    need("ada", "adab", "zero", "zerob")
    adab = r.adab[...].astype(F32)
    zerob = r.zerob[...].astype(F32)
    for w in range(2):
        for b in blocks:
            later = slice(D + b.start, D + b.stop)
            pre_gate = dot(r.s_hi[w], r.ada[w, :, b]) + dot(r.s_lo[w], r.ada[w, :, b])
            r.mg[w, :, b] = sigmoid(pre_gate + adab[w : w + 1, b])
            r.ms[w, :, b] = dot(r.s_hi[w], r.ada[w, :, later]) + dot(r.s_lo[w], r.ada[w, :, later])
            r.zg[w, :, b] = sigmoid(dot(r.single[...], r.zero[w, :, b]) + zerob[w : w + 1, b])
    need("act", "cot")

    def norm_in(i):
        rows = pl.ds(i * 16, 16)
        normed, _ = normalize(r.act[rows].astype(F32))
        r.hat[rows] = normed
        r.ain[rows] = (r.mg[0, rows] * normed + r.ms[0, rows]).astype(BF)
        r.tin[rows] = (r.mg[1, rows] * normed + r.ms[1, rows]).astype(BF)
        g = r.cot[rows].astype(F32)
        r.gao[rows] = (r.zg[0, rows] * g).astype(BF)
        r.gto[rows] = (r.zg[1, rows] * g).astype(BF)

    loop(N // 16, norm_in)

    def branch_out(w, b, part):
        gate = r.zg[w, :, b]
        share = gate * part
        r.mixf[:, b] = share if w == 1 else r.mixf[:, b] + share
        grad = r.cot[:, b].astype(F32) * share * (1.0 - gate)
        r.zp[:, b] = grad.astype(BF)
        for j in range(2):
            row = 12 + 6 * w + b.start // 128 + j
            r.small_a[row : row + 1] = jnp.sum(grad[:, j * 128 : (j + 1) * 128], 0, keepdims=True)

    def branch_in(w, b, grad_in):
        gate = r.mg[w, :, b]
        share = gate * grad_in
        r.actf[:, b] = share if w == 1 else r.actf[:, b] + share
        grad = share * r.hat[:, b] * (1.0 - gate)
        r.pre[:, b] = grad.astype(BF)
        r.pre[:, D + b.start : D + b.stop] = grad_in.astype(BF)
        for j in range(2):
            row = 6 * w + b.start // 128 + j
            r.small_a[row : row + 1] = jnp.sum(grad[:, j * 128 : (j + 1) * 128], 0, keepdims=True)

    def conditioned(w, to):
        for i in range(6):
            put(to, T_ADA[w] + i * 48, dot(r.s_t[w], r.pre[:, i * 256 : (i + 1) * 256]))
        for i, b in enumerate(blocks):
            value = dot(r.one_t[...], r.zp[:, b])
            if w == 1 and i == 2:
                put(r.tiles[3], T_ZERO2, value)
            else:
                put(to, T_ZERO[w] + i * 48, value)

    def conditioning_back(w):
        for j in range(3):
            b = slice(j * 128, (j + 1) * 128)
            scaled = dot_t(r.pre[...], r.ada[w, b, :])
            row = 24 + 3 * w + j
            r.small_a[row : row + 1] = jnp.sum(scaled * r.shat[:, b], 0, keepdims=True)
            share = scaled * gains[w : w + 1, b]
            through = dot_t(r.zp[...], r.zero[w, b, :])
            r.gsh[:, b] = share if w == 1 else r.gsh[:, b] + share
            r.zterm[:, b] = through if w == 1 else r.zterm[:, b] + through

    need("win", "hid")
    for b in blocks:
        gate_in = dot(r.tin[...], r.win[0, :, b])
        up_in = dot(r.tin[...], r.win[1, :, b])
        grad_hidden = dot_t(r.gto[...], r.hid[b, :])
        sig = sigmoid(gate_in)
        silu = gate_in * sig
        r.hidden[:, b] = (silu * up_in).astype(BF)
        r.ffn[:, b] = (grad_hidden * up_in * sig * (1.0 + gate_in * (1.0 - sig))).astype(BF)
        r.ffn[:, D + b.start : D + b.stop] = (grad_hidden * silu).astype(BF)
    sums = Sums(r, at)
    r.flipped[...] = flip(r.hidden[...])
    for i, b in enumerate(blocks):
        value = dot(r.flipped[...], r.gto[:, b])
        if i < 2:
            put(r.tiles[0], T_HID + i * 96, value)
        else:
            put(r.tiles[0], T_HID + 192, value[:, :128])
            put(r.tiles[0], T_HID + 240, value[:256, 128:])
            put(r.tiles[2], T_HID2, value[256:, 128:])
    r.flipped[...] = flip(r.tin[...])
    for i in range(6):
        put(r.tiles[0], T_IN + i * 96, dot(r.flipped[...], r.ffn[:, i * 256 : (i + 1) * 256]))
    sums.core_start(0)
    for b in blocks:
        branch_out(1, b, dot(r.hidden[...], r.hid[:, b]))
    for b in blocks:
        branch_in(
            1, b, dot_t(r.ffn[:, :D], r.win[0, b, :]) + dot_t(r.ffn[:, D:], r.win[1, b, :])
        )
    conditioned(1, r.tiles[1])
    sums.core_start(1)
    sums.core_end(0)
    sums.rs_start(0, 0)
    sums.rs_start(1, 0)
    conditioning_back(1)

    need("wq", "qb", "wout")
    r.qkv[0] = (dot(r.ain[...], r.wq[0]) + r.qb[...].astype(F32).reshape(1, 384)).astype(BF)
    r.qkv[1] = dot(r.ain[...], r.wq[1]).astype(BF)
    r.qkv[2] = dot(r.ain[...], r.wq[2]).astype(BF)
    r.gsig[...] = sigmoid(dot(r.ain[...], r.wq[3]))
    r.ggat[...] = dot_t(r.gao[...], r.wout[...])
    r.gatt[...] = (r.ggat[...] * r.gsig[...]).astype(BF)
    sums.core_end(1)
    sums.rs_start(2, 0)
    sums.rs_start(3, 0)
    loop(NS - 1, lambda i: bias_copy(i + 1).wait())
    wt_copy.wait()
    r.acc[...] = jnp.zeros(r.acc.shape, F32)
    lane = lax.broadcasted_iota(jnp.int32, (1, 256), 1)
    mask = jnp.where(lane < counts_ref[0], 0.0, -1e9)
    for h in range(8):
        lo = 0 if h < 5 else 128
        win = slice(lo, lo + 256)
        first = h * HD - lo
        mine = (lane >= first) & (lane < first + HD)
        pick = jnp.where(mine, 1.0, 0.0).astype(BF)
        q_m = r.qkv[0, :, win] * pick
        k_m = r.qkv[1, :, win] * pick
        v_m = r.qkv[2, :, win] * pick
        g_m = r.gatt[:, win] * pick
        pair_rows = r.bias[:, (h // 2) * 16 : (h // 2) * 16 + 16, :].astype(F32)
        bias = pair_rows[:, (h % 2) * 8 : (h % 2) * 8 + 8, :].reshape(N, N)
        scores = dot_t(q_m, r.qkv[1, :, win]) * SCALE + bias + mask
        top = jnp.max(scores, -1, keepdims=True)
        weights = jnp.exp(scores - top)
        probs = weights * (1.0 / jnp.sum(weights, -1, keepdims=True))
        low = probs.astype(BF)
        r.acc[0, :, win] += dot(low, v_m)
        grad_probs = dot_t(g_m, r.qkv[2, :, win])
        delta = jnp.sum(probs * grad_probs, -1, keepdims=True)
        grad_s = probs * (grad_probs - delta)
        grad_low = grad_s.astype(BF)
        r.acc[1, :, win] += dot(grad_low, k_m)
        r.acc[2, :, win] += dot_l(grad_low, q_m)
        r.acc[3, :, win] += dot_l(low, g_m)
        split = grad_s.reshape(NS, 8, N)
        if h % 2 == 0:
            r.held[...] = split
        else:
            two = jnp.concatenate([r.held[...], split], 1).astype(BF)
            rows = slice((h // 2 % 2) * 16, (h // 2 % 2) * 16 + 16)
            if h < 4:
                r.gb[0, :, rows, :] = two
            else:
                for s in range(NS):
                    r.gb[1, s % 4 * 8 + s // 8 * 2 + s // 4 % 2, rows, :] = two[s]
    first_hop = []
    for half, axis in enumerate("zx"):
        for i in range(1, 4):
            dev, q = peer_on(at, axis, i)
            cp = rcopy(
                r.gb.at[half, pl.ds(q * 8, 8)],
                r.gb1.at[half, i - 1],
                r.b1s.at[half, i - 1],
                r.b1r.at[half, i - 1],
                dev,
            )
            cp.start()
            first_hop.append(cp)
    for g in FIRST:
        sums.rs_end(g, 0)
        sums.rs_start(g, 1)
    attended = r.acc[0]
    gated = (r.gsig[...] * attended).astype(BF)
    r.gheads[:, 1152:] = (r.ggat[...] * attended * r.gsig[...] * (1.0 - r.gsig[...])).astype(BF)
    grad_q = (r.acc[1] * SCALE).astype(BF)
    r.gheads[:, :384] = grad_q
    r.gheads[:, 384:768] = (r.acc[2] * SCALE).astype(BF)
    r.gheads[:, 768:1152] = r.acc[3].astype(BF)
    for j in range(3):
        r.small_w[9 + j : 10 + j] = jnp.sum(
            grad_q[:, j * 128 : (j + 1) * 128].astype(F32), 0, keepdims=True
        )
    for b in blocks:
        branch_out(0, b, dot(gated, r.wout[:, b]))
    r.mixs[...] = r.mixf[...].astype(BF)
    mix_copy = rcopy(r.mixs, r.mixr, r.hs.at[1], r.hr.at[1], head_dev(at))
    mix_copy.start()
    r.flipped[:384] = flip(gated)
    for i, b in enumerate(blocks):
        put(r.tiles[2], T_OUT + i * 48, dot(r.flipped[:384], r.gao[:, b]))
    r.flipped[...] = flip(r.ain[...])
    for i in range(6):
        put(r.tiles[2], T_QKVG + i * 96, dot(r.flipped[...], r.gheads[:, i * 256 : (i + 1) * 256]))
    r.tiles[2][T_WPAD:] = jnp.zeros((TILES[2] - T_WPAD, 16, 128), BF)
    sums.core_start(2)
    for g in FIRST:
        sums.rs_end(g, 1)
        sums.rs_start(g, 2)
    for b in blocks:
        total = dot_t(r.gheads[:, :384], r.wq[0, b, :])
        for k in range(1, 4):
            total = total + dot_t(r.gheads[:, k * 384 : (k + 1) * 384], r.wq[k, b, :])
        branch_in(0, b, total)
    r.acts[...] = r.actf[...].astype(BF)
    act_copy = rcopy(r.acts, r.actr, r.hs.at[2], r.hr.at[2], head_dev(at))
    act_copy.start()
    sums.core_end(2)
    sums.rs_start(4, 0)
    sums.rs_start(5, 0)
    for cp in first_hop:
        cp.wait()
    second_hop = []
    for half in range(2):
        own = pl.ds(at["zx"[half]] * 8, 8)
        total = r.gb[half, own].astype(F32)
        for i in range(3):
            total = total + r.gb1[half, i].astype(F32)
        r.gb[half, own] = total.astype(BF)
        for i in range(1, 8):
            if half == 0:
                lo, x = (at["l"] + i // 4) % 2, (at["x"] + i % 4) % 4
                dev, q = samp_dev(at, at["z"] * 8 + lo * 4 + x), lo * 4 + x
            else:
                z, lo = (at["z"] + i // 2) % 4, (at["l"] + i % 2) % 2
                dev, q = samp_dev(at, z * 8 + lo * 4 + at["x"]), z * 2 + lo
            cp = rcopy(
                r.gb.at[half, at["zx"[half]] * 8 + q],
                r.gb2.at[half, i - 1],
                r.b2s.at[half, i - 1],
                r.b2r.at[half, i - 1],
                dev,
            )
            cp.start()
            second_hop.append(cp)
    conditioned(0, r.tiles[3])
    conditioning_back(0)
    grad_single = norm_back(r.gsh[...], r.shat[...], r.sinv[:, :1]) + r.zterm[...]
    put(r.tiles[4], 0, grad_single)
    r.tiles[4][48:] = jnp.zeros((TILES[4] - 48, 16, 128), BF)
    r.tiles[3][T_SMALL:T_APAD] = r.small_a[...].astype(BF).reshape(2, 16, 128)
    r.tiles[3][T_APAD:] = jnp.zeros((TILES[3] - T_APAD, 16, 128), BF)
    sums.core_start(3)
    sums.rs_start(8, 0)
    for g in FIRST:
        sums.rs_end(g, 2)
        sums.ag_start(g, 2)
    sums.core_end(3)
    sums.rs_start(6, 0)
    sums.rs_start(7, 0)
    for cp in second_hop:
        cp.wait()
    places = (at["z"] * 8 + at["l"] * 4 + at["x"], at["x"] * 8 + at["z"] * 2 + at["l"])
    for half in range(2):
        total = r.gb[half, places[half]].astype(F32)
        for i in range(7):
            total = total + r.gb2[half, i].astype(F32)
        r.gball[hd, half * 32 : half * 32 + 32] = total.astype(BF)
    rows_copy = rcopy(r.gball.at[hd], r.gball.at[hd], r.hs.at[3], r.hr.at[3], head_dev(at))
    rows_copy.start()
    for g in FIRST:
        sums.ag_end(g, 2)
        sums.ag_start(g, 1)
    mix_copy.wait()

    def last_mix(i):
        rows = pl.ds(i * 16, 16)
        value = r.mixs[rows].astype(F32) + r.mixr[rows].astype(F32)
        r.hidden[rows] = (r.act[rows].astype(F32) + value).astype(BF)

    loop(16, last_mix)
    leave(r.hidden, "mixed_o")

    rows_copy.wait()
    r.rows[...] = r.gball[hd].astype(F32).reshape(8, 8, N)
    r.held[:16] = r.gball[...].astype(F32).reshape(16, 8, N)
    wt_all = (
        jnp.concatenate([r.wall[0].astype(F32)[:8], r.wall[1].astype(F32)[:8]], 0).astype(BF)
    )
    weight = jnp.zeros((8, 128), F32)
    total = jnp.zeros((1, 128), F32)
    for i in range(8):
        normed, inv = normalize(r.pair[i].astype(F32))
        weight = weight + dot(r.rows[:, i, :].astype(BF), (normed * pgain).astype(BF))
        grad_low = dot_l(r.held[:16, i, :].astype(BF), wt_all)
        total = total + jnp.sum(grad_low * normed, 0, keepdims=True)
        r.gpair[i] = norm_back(grad_low * pgain, normed, inv)
    leave(r.gpair, "pair_o")
    r.small_w[:8] = weight
    r.small_w[8:9] = total

    def small_start(k):
        axis = "czxl"[k]
        mine = at[axis]
        r.slot[k, mine] = r.small_w[...]
        cps = []
        for i in range(1, SIZE.get(axis, 2)):
            dev = core_dev(at) if axis == "c" else peer_on(at, axis, i)[0]
            cp = rcopy(
                r.slot.at[k, mine], r.slot.at[k, mine], r.ss.at[k, i - 1], r.sr.at[k, i - 1], dev
            )
            cp.start()
            cps.append(cp)
        return cps

    def small_end(k, cps):
        for cp in cps:
            cp.wait()
        total = r.slot[k, 0]
        for i in range(1, SIZE.get("czxl"[k], 2)):
            total = total + r.slot[k, i]
        r.small_w[...] = total

    tiny = small_start(0)
    for g in SECOND:
        sums.rs_end(g, 0)
        sums.rs_start(g, 1)
    small_end(0, tiny)
    tiny = small_start(1)
    for g in FIRST:
        sums.ag_end(g, 1)
        sums.ag_start(g, 0)
    act_copy.wait()

    def last_act(i):
        rows = pl.ds(i * 16, 16)
        grad = r.acts[rows].astype(F32) + r.actr[rows].astype(F32)
        normed, inv = normalize(r.act[rows].astype(F32))
        r.mixf[rows] = r.cot[rows].astype(F32) + norm_back(grad, normed, inv)

    loop(16, last_act)
    leave(r.mixf, "act_o")
    for g in SECOND:
        sums.rs_end(g, 1)
        sums.rs_start(g, 2)
    small_end(1, tiny)
    tiny = small_start(2)
    for g in FIRST:
        sums.ag_end(g, 0)
        sums.share_start(g)
    for g in SECOND:
        sums.rs_end(g, 2)
        sums.ag_start(g, 2)
    small_end(2, tiny)
    tiny = small_start(3)
    for g in SECOND:
        sums.ag_end(g, 2)
        sums.ag_start(g, 1)
    for g in FIRST:
        sums.share_end(g)
    for b in (0, 1):
        leave(r.sums[b], "sum%d" % b)
    small_end(3, tiny)
    leave(r.small_w, "small_o")
    for g in SECOND:
        sums.ag_end(g, 1)
        sums.ag_start(g, 0)
    for g in SECOND:
        sums.ag_end(g, 0)
        sums.share_start(g)
    leave(r.sums[4], "sum4")
    for g in SECOND:
        sums.share_end(g)
    for b in (2, 3):
        leave(r.sums[b], "sum%d" % b)
    for cp in copies:
        cp.wait()


def whole(shape, dtype):
    return jax.ShapeDtypeStruct(shape, dtype)


def mega(counts, *args):
    return pl.pallas_call(
        mega_kernel,
        out_shape=tuple(whole(shape, dtype) for _, shape, dtype in OUTPUTS),
        in_specs=[pl.BlockSpec(memory_space=pltpu.SMEM)]
        + [pl.BlockSpec(memory_space=pl.ANY)] * len(INPUTS),
        out_specs=[pl.BlockSpec(memory_space=pl.ANY)] * len(OUTPUTS),
        scratch_shapes=[pltpu.VMEM(shape, BF) for _, shape in INPUTS]
        + [pltpu.VMEM(shape, dtype) for _, shape, dtype in SCRATCH]
        + [pltpu.VMEM((t, 16, 128), BF) for t in TILES]
        + [pltpu.VMEM((t, 16, 128), BF) for t in TILES]
        + [pltpu.VMEM(shape, BF) for _, shape in recv_shapes()]
        + [pltpu.SemaphoreType.DMA(shape) for _, shape in SEMS],
        compiler_params=pltpu.CompilerParams(
            collective_id=0, has_side_effects=True, vmem_limit_bytes=63 * 2**20
        ),
        name="block",
    )(counts, *args)


FINAL = (
    ("qkvg", (D, 4, 384)),
    ("win", (D, 2, D)),
    ("hid", (D, D)),
    ("ada", (2, 384, 2 * D)),
    ("zero", (2, 384, D)),
    ("wout", (384, D)),
    ("single", (N, 384)),
    ("adab", (2, D)),
    ("zerob", (2, D)),
    ("gain", (2, 384)),
    ("wt", (8, 128)),
    ("qb", (384,)),
    ("pgain", (128,)),
)


def finish_kernel(*refs):
    refs = list(refs)

    def take(count):
        got = refs[:count]
        del refs[:count]
        return got

    ins = take(9)
    outs = take(3 + len(FINAL))
    held = take(9)
    f = Refs()
    for (name, _), ref in zip(FINAL, take(len(FINAL))):
        setattr(f, name, ref)
    in_sem, out_sem = take(2)
    loads = []
    for i in range(9):
        cp = pltpu.make_async_copy(ins[i], held[i], in_sem.at[i])
        cp.start()
        loads.append(cp)
    copies = []

    def leave(name):
        i = [k for k, _ in FINAL].index(name)
        cp = pltpu.make_async_copy(getattr(f, name), outs[3 + i], out_sem.at[3 + i])
        cp.start()
        copies.append(cp)

    def get(b, start, rows):
        return held[b][pl.ds(start, rows // 16)].astype(F32).reshape(rows, 128)

    cols = [slice(j * 128, (j + 1) * 128) for j in range(12)]
    loads[0].wait()
    for k in range(2):
        for j in range(6):
            f.win[:, k, cols[j]] = get(0, T_IN + (k * 6 + j) * 48, 768)
    leave("win")
    for i in range(3):
        loads[6 + i].wait()
        cp = pltpu.make_async_copy(held[6 + i], outs[i], out_sem.at[i])
        cp.start()
        copies.append(cp)
    loads[2].wait()
    for j in range(5):
        f.hid[:, cols[j]] = get(0, T_HID + j * 48, 768)
    f.hid[:256, cols[5]] = get(0, T_HID + 240, 256)
    f.hid[256:, cols[5]] = get(2, T_HID2, 512)
    leave("hid")
    for k in range(4):
        for j in range(3):
            f.qkvg[:, k, cols[j]] = get(2, T_QKVG + (k * 3 + j) * 48, 768)
    leave("qkvg")
    for j in range(6):
        f.wout[:, cols[j]] = get(2, T_OUT + j * 24, 384)
    leave("wout")
    loads[1].wait()
    loads[3].wait()
    for w in range(2):
        for j in range(12):
            f.ada[w, :, cols[j]] = get(3 - 2 * w, T_ADA[w] + j * 24, 384)
    leave("ada")
    for w in range(2):
        for j in range(6):
            if w == 1 and j >= 4:
                f.zero[w, :, cols[j]] = get(3, T_ZERO2 + (j - 4) * 24, 384)
            else:
                f.zero[w, :, cols[j]] = get(3 - 2 * w, T_ZERO[w] + j * 24, 384)
    leave("zero")
    loads[4].wait()
    for j in range(3):
        f.single[:, cols[j]] = get(4, j * 16, 256)
    leave("single")
    small = held[3][T_SMALL:T_APAD].astype(F32).reshape(32, 128)
    for w in range(2):
        for j in range(6):
            f.adab[w : w + 1, cols[j]] = small[6 * w + j : 6 * w + j + 1]
            f.zerob[w : w + 1, cols[j]] = small[12 + 6 * w + j : 13 + 6 * w + j]
        for j in range(3):
            f.gain[w : w + 1, cols[j]] = small[24 + 3 * w + j : 25 + 3 * w + j]
    loads[5].wait()
    f.wt[...] = held[5][:8]
    f.pgain[...] = held[5][8]
    for j in range(3):
        f.qb[cols[j]] = held[5][9 + j]
    for name in ("adab", "zerob", "gain", "wt", "pgain", "qb"):
        leave(name)
    for cp in copies:
        cp.wait()


def finish(*args):
    shapes = [whole((N, D), BF), whole((N, D), F32), whole((8, N, 128), F32)]
    shapes += [whole(shape, F32) for _, shape in FINAL]
    return pl.pallas_call(
        finish_kernel,
        out_shape=tuple(shapes),
        in_specs=[pl.BlockSpec(memory_space=pl.ANY)] * len(args),
        out_specs=[pl.BlockSpec(memory_space=pl.ANY)] * len(shapes),
        scratch_shapes=[pltpu.VMEM(a.shape, a.dtype) for a in args]
        + [pltpu.VMEM(shape, F32) for _, shape in FINAL]
        + [pltpu.SemaphoreType.DMA((9,)), pltpu.SemaphoreType.DMA((len(shapes),))],
        compiler_params=pltpu.CompilerParams(vmem_limit_bytes=60 * 2**20),
        name="finish",
    )(*args)


def local(
    activations,
    conditioning,
    pair,
    counts,
    ada_weight,
    ada_bias,
    cond_gain,
    zero_weight,
    zero_bias,
    qkvg_weight,
    q_bias,
    out_weight,
    in_weight,
    hid_weight,
    pair_gain,
    bias_weight,
    cotangent,
):
    results = mega(
        counts,
        pair[0],
        pair_gain,
        bias_weight.T,
        conditioning[0],
        cond_gain,
        ada_weight,
        ada_bias,
        zero_weight,
        zero_bias,
        activations[0, 0],
        cotangent[0, 0],
        in_weight.transpose(1, 0, 2),
        hid_weight,
        qkvg_weight.transpose(1, 0, 2),
        q_bias,
        out_weight,
    )
    outs = finish(*results)
    mixed, act, grad_pair = outs[:3]
    o = dict(zip([name for name, _ in FINAL], outs[3:]))
    return (
        mixed[None, None],
        act[None, None],
        o["single"][None],
        grad_pair[None],
        o["ada"],
        o["adab"],
        o["gain"],
        o["zero"],
        o["zerob"],
        o["qkvg"],
        o["qb"],
        o["wout"],
        o["win"],
        o["hid"],
        o["pgain"],
        o["wt"].T,
    )


def solution(mesh):
    placed = (
        P("cplx", "samp", None, None),
        P("cplx", None, None),
        P("cplx", "samp", None, None),
        P("cplx"),
        P(),
        P(),
        P(),
        P(),
        P(),
        P(None, None, "head"),
        P("head"),
        P("head", None),
        P(None, None, "head"),
        P("head", None),
        P(),
        P(None, "head"),
        P("cplx", "samp", None, None),
    )
    return jax.shard_map(
        local,
        mesh=mesh,
        in_specs=placed,
        out_specs=(
            P("cplx", "samp", None, None),
            P("cplx", "samp", None, None),
            P("cplx", None, None),
            P("cplx", "samp", None, None),
            P(),
            P(),
            P(),
            P(),
            P(),
            P(None, None, "head"),
            P("head"),
            P("head", None),
            P(None, None, "head"),
            P("head", None),
            P(),
            P(None, "head"),
        ),
        check_vma=False,
    )
```

```python
import functools
import math

import jax
import jax.numpy as jnp
from jax import lax
from jax.experimental import pallas as pl
from jax.experimental.pallas import tpu as pltpu
from jax.sharding import PartitionSpec as P

D = 768
HD = 48
EPS = 1e-05
HIGH = lax.Precision.HIGHEST
MESH = pl.DeviceIdType.MESH
BF = jnp.bfloat16
F32 = jnp.float32
NS = 32
VMEM = pltpu.VMEM


def place():
    samp = lax.axis_index("samp")
    return {
        "c": lax.axis_index("cplx"),
        "h": lax.axis_index("head"),
        "s": samp,
        "z": samp // 8,
        "l": (samp // 4) % 2,
        "x": samp % 4,
        "y": lax.axis_index("head") * 2 + (samp // 4) % 2,
    }


SIZE = {"z": 4, "x": 4, "y": 4, "l": 2}


def extent(axes):
    size = 1
    for a in axes:
        size *= SIZE[a]
    return size


def index_on(at, axes):
    index = 0
    for a in axes:
        index = index * SIZE[a] + at[a]
    return index


def peer_on(at, axes, step):
    now = dict(at)
    for a in reversed(axes):
        now[a] = (at[a] + step % SIZE[a]) % SIZE[a]
        step //= SIZE[a]
    if "y" in axes:
        now["h"], now["l"] = now["y"] // 2, now["y"] % 2
    dev = {"cplx": at["c"], "samp": now["z"] * 8 + now["l"] * 4 + now["x"], "head": now["h"]}
    return dev, index_on(now, axes)


def signal(bar, dev):
    pl.semaphore_signal(bar, inc=1, device_id=dev, device_id_type=MESH)


def samp_dev(at, other):
    return {"cplx": at["c"], "samp": other, "head": at["h"]}


def head_dev(at):
    return {"cplx": at["c"], "samp": at["s"], "head": 1 - at["h"]}


def core_dev(at):
    return {"cplx": 1 - at["c"], "samp": at["s"], "head": at["h"]}


def rcopy(src, dst, send, recv, dev):
    return pltpu.make_async_remote_copy(
        src_ref=src, dst_ref=dst, send_sem=send, recv_sem=recv, device_id=dev, device_id_type=MESH
    )


def greet_samp(at, bar):
    def one(i, _):
        signal(bar, samp_dev(at, (at["s"] + i) % NS))
        return 0

    lax.fori_loop(1, NS, one, 0)


SCALE = 1.0 / math.sqrt(HD)


def dot(a, b):
    return lax.dot_general(a, b, (((1,), (0,)), ((), ())), preferred_element_type=F32)


def dot_t(a, b):
    return lax.dot_general(a, b, (((1,), (1,)), ((), ())), preferred_element_type=F32)


def dot_l(a, b):
    return lax.dot_general(a, b, (((0,), (0,)), ((), ())), preferred_element_type=F32)


def mean(v):
    return jnp.mean(v, -1, keepdims=True)


def normalize(tensor):
    centered = tensor - mean(tensor)
    inv_std = lax.rsqrt(mean(centered * centered) + EPS)
    return (centered * inv_std, inv_std)


def norm_back(grad_hat, normed, inv_std):
    return inv_std * (grad_hat - mean(grad_hat) - normed * mean(grad_hat * normed))


def sigmoid(v):
    return 1.0 / (1.0 + jnp.exp(-v))


def flip(v):
    return v.astype(F32).T.astype(BF)


def loop(count, body):
    def step(i, _):
        body(i)
        return 0

    lax.fori_loop(0, count, step, 0)


def put(ref, start, value):
    rows, cols = value.shape
    n = rows // 16
    for j in range(cols // 128):
        ref[pl.ds(start + j * n, n)] = (
            value[:, j * 128 : (j + 1) * 128].astype(BF).reshape(n, 16, 128)
        )


TILES = (832, 384, 768, 512, 64)
HALF = (416, 192, 384, 256, 64)
GROUPS = (
    (0, 0, 192, ("z", "xl")),
    (0, 192, 224, ("x", "zl")),
    (1, 0, 128, ("y", "zx")),
    (1, 128, 64, ("z", "yx")),
    (2, 0, 192, ("z", "xl")),
    (2, 192, 192, ("x", "zl")),
    (3, 0, 128, ("y", "xz")),
    (3, 128, 64, ("z", "yx")),
    (3, 192, 64, ("x", "yz")),
    (4, 0, 64, ("y", "zx")),
)
FIRST = (0, 1, 2, 3)
SECOND = (4, 5, 6, 7, 8, 9)
T_IN, T_HID = 0, 576
T_ADA, T_ZERO = (0, 0), (288, 288)
T_QKVG, T_OUT, T_HID2, T_WPAD = 0, 576, 720, 752
T_ZERO2, T_SMALL, T_APAD = 432, 480, 482

INPUTS = (
    ("pair", (8, 256, 128)),
    ("pgain", (128,)),
    ("wt", (8, 128)),
    ("single", (256, 384)),
    ("gain", (2, 384)),
    ("ada", (2, 384, 1536)),
    ("adab", (2, 768)),
    ("zero", (2, 384, 768)),
    ("zerob", (2, 768)),
    ("act", (256, 768)),
    ("cot", (256, 768)),
    ("win", (2, 768, 768)),
    ("hid", (768, 768)),
    ("wq", (4, 768, 384)),
    ("qb", (384,)),
    ("wout", (384, 768)),
)
LOADS = (
    ("pair", "pgain", "wt", "single", "gain", "adab", "zerob", "ada1", "zero1", "act", "cot")
    + ("win", "hid", "ada0", "zero0", "wq", "qb", "wout")
)
N = 256
SCRATCH = (
    ("rows", (8, 8, N), F32),
    ("part", (64, N), BF),
    ("bias", (NS, 64, N), BF),
    ("wall", (2, 16, 128), BF),
    ("shat", (N, 384), F32),
    ("sinv", (N, 128), F32),
    ("s_hi", (2, N, 384), BF),
    ("s_lo", (2, N, 384), BF),
    ("s_t", (2, 384, N), BF),
    ("one_t", (384, N), BF),
    ("mg", (2, N, D), F32),
    ("ms", (N, D), F32),
    ("zg", (2, N, D), F32),
    ("hat", (N, D), F32),
    ("ain", (N, D), BF),
    ("tin", (N, D), BF),
    ("gao", (N, D), BF),
    ("gto", (N, D), BF),
    ("hidden", (N, D), BF),
    ("ffn", (N, 2 * D), BF),
    ("pre", (N, 2 * D), BF),
    ("zp", (N, D), BF),
    ("mixf", (N, D), F32),
    ("actf", (N, D), F32),
    ("mixs", (N, D), BF),
    ("mixr", (N, D), BF),
    ("acts", (N, D), BF),
    ("actr", (N, D), BF),
    ("gsh", (N, 384), F32),
    ("zterm", (N, 384), F32),
    ("qkv", (3, N, 384), BF),
    ("gsig", (N, 384), F32),
    ("ggat", (N, 384), F32),
    ("gatt", (N, 384), BF),
    ("acc", (4, N, 384), F32),
    ("gheads", (N, 1536), BF),
    ("flipped", (D, N), BF),
    ("held", (NS, 8, N), F32),
    ("small_a", (32, 128), F32),
    ("small_w", (16, 128), F32),
    ("gb", (2, NS, 32, N), BF),
    ("gb1", (2, 3, 8, 32, N), BF),
    ("gb2", (2, 7, 32, N), BF),
    ("gball", (2, 64, N), BF),
    ("gpair", (8, N, 128), F32),
    ("slot", (4, 4, 16, 128), F32),
)
SEMS = (
    ("ld", (len(LOADS),)),
    ("bs", (1,)),
    ("br", (1,)),
    ("hs", (4,)),
    ("hr", (4,)),
    ("cs", (4,)),
    ("cr", (4,)),
    ("rs", (len(GROUPS), 2)),
    ("rr", (len(GROUPS), 2)),
    ("gs", (len(GROUPS), 2)),
    ("gr", (len(GROUPS), 2)),
    ("fs", (4,)),
    ("fr", (4,)),
    ("b1s", (2,)),
    ("b1r", (2,)),
    ("b2s", (2,)),
    ("b2r", (2,)),
    ("out", (9,)),
    ("ss", (4,)),
    ("sr", (4,)),
)
OUTPUTS = tuple(("sum%d" % i, (t, 16, 128), BF) for i, t in enumerate(TILES)) + (
    ("small_o", (16, 128), F32),
    ("mixed_o", (N, D), BF),
    ("act_o", (N, D), F32),
    ("pair_o", (8, N, 128), F32),
)


class Refs:
    pass


def recv_shapes():
    shapes = []
    for g, (_, _, tiles, axes) in enumerate(GROUPS):
        for s, axis in enumerate(axes):
            tiles //= extent(axis)
            shapes.append(((g, s), (extent(axis) - 1, tiles, 16, 128)))
    return shapes


def arrived(like, send, recv, at):
    cp = rcopy(like, like, send, recv, core_dev(at))
    cp.wait_send()
    cp.wait_recv()


class Sums:
    def __init__(self, r, at):
        self.r, self.at = r, at
        core = at["c"]
        self.shift = [core * HALF[b] if b < 4 else 0 for b in range(5)]
        self.base = [None] * len(GROUPS)
        self.part = [None] * len(GROUPS)
        self.pairs = {}

    def core_start(self, buf):
        r, at, half = self.r, self.at, HALF[buf]
        cp = rcopy(
            r.tiles[buf].at[pl.ds((1 - at["c"]) * half, half)],
            r.sums[buf].at[pl.ds((1 - at["c"]) * half, half)],
            r.cs.at[buf],
            r.cr.at[buf],
            core_dev(at),
        )
        cp.start()
        self.pairs[buf] = cp

    def core_end(self, buf):
        r, half, start = self.r, HALF[buf], self.shift[buf]
        self.pairs[buf].wait()

        def add(j):
            rows = pl.ds(start + j * 16, 16)
            r.tiles[buf][rows] = (
                r.tiles[buf][rows].astype(F32) + r.sums[buf][rows].astype(F32)
            ).astype(BF)

        loop(half // 16, add)

    def rs_start(self, g, stage):
        r, at = self.r, self.at
        buf, start, tiles, axes = GROUPS[g]
        axis = axes[stage]
        count = extent(axis)
        for a in axes[:stage]:
            tiles //= extent(a)
        if stage == 0:
            self.base[g] = self.shift[buf] + start
        part = tiles // count
        for i in range(1, count):
            dev, q = peer_on(at, axis, i)
            rcopy(
                r.tiles[buf].at[pl.ds(self.base[g] + q * part, part)],
                r.recv[g, stage].at[i - 1],
                r.rs.at[g, stage],
                r.rr.at[g, stage],
                dev,
            ).start()
        self.part[g] = part

    def rs_end(self, g, stage):
        r = self.r
        buf, _, _, axes = GROUPS[g]
        part = self.part[g]
        got = r.recv[g, stage]
        arrived(got, r.rs.at[g, stage], r.rr.at[g, stage], self.at)
        here = self.base[g] + index_on(self.at, axes[stage]) * part
        block = max(b for b in range(1, 17) if part % b == 0)

        def add(i):
            rows = pl.ds(i * block, block)
            mine = pl.ds(here + i * block, block)
            total = r.tiles[buf][mine].astype(F32)
            for j in range(extent(axes[stage]) - 1):
                total = total + r.recv[g, stage][j, rows].astype(F32)
            to = r.sums if stage == 1 else r.tiles
            to[buf][mine] = total.astype(BF)

        loop(part // block, add)
        self.base[g] = here

    def ag_start(self, g, stage):
        r = self.r
        buf, _, _, axes = GROUPS[g]
        rows = pl.ds(self.base[g], self.part[g])
        for i in range(1, extent(axes[stage])):
            dev, _ = peer_on(self.at, axes[stage], i)
            rcopy(
                r.sums[buf].at[rows],
                r.sums[buf].at[rows],
                r.gs.at[g, stage],
                r.gr.at[g, stage],
                dev,
            ).start()

    def ag_end(self, g, stage):
        r = self.r
        buf, _, _, axes = GROUPS[g]
        axis = axes[stage]
        count = (extent(axis) - 1) * self.part[g]
        arrived(r.sums[buf].at[pl.ds(0, count)], r.gs.at[g, stage], r.gr.at[g, stage], self.at)
        self.base[g] = self.base[g] - index_on(self.at, axis) * self.part[g]
        self.part[g] = self.part[g] * extent(axis)

    def share_start(self, g):
        r = self.r
        buf, start, tiles, _ = GROUPS[g]
        if buf < 4:
            rows = pl.ds(self.shift[buf] + start, tiles)
            rcopy(
                r.sums[buf].at[rows],
                r.sums[buf].at[rows],
                r.fs.at[buf],
                r.fr.at[buf],
                core_dev(self.at),
            ).start()

    def share_end(self, buf):
        r = self.r
        arrived(r.sums[buf].at[pl.ds(0, HALF[buf])], r.fs.at[buf], r.fr.at[buf], self.at)


def mega_kernel(*refs):
    r = Refs()
    refs = list(refs)

    def take(count):
        got = refs[:count]
        del refs[:count]
        return got

    counts_ref = take(1)[0]
    hbm = take(len(INPUTS))
    outs = dict(zip([o[0] for o in OUTPUTS], take(len(OUTPUTS))))
    for (name, _), ref in zip(INPUTS, take(len(INPUTS))):
        setattr(r, name, ref)
    for (name, _, _), ref in zip(SCRATCH, take(len(SCRATCH))):
        setattr(r, name, ref)
    r.tiles = take(5)
    r.sums = take(5)
    r.recv = {}
    for (key, _), ref in zip(recv_shapes(), take(len(recv_shapes()))):
        r.recv[key] = ref
    for (name, _), ref in zip(SEMS, take(len(SEMS))):
        setattr(r, name, ref)

    at = place()
    me, hd = at["s"], at["h"]
    blocks = [slice(i * 256, (i + 1) * 256) for i in range(3)]
    loads = {}
    places = {name: i for i, (name, _) in enumerate(INPUTS)}
    for k, name in enumerate(LOADS):
        src, dst = hbm[places[name.rstrip("01")]], getattr(r, name.rstrip("01"))
        if name[-1] in "01":
            src, dst = src.at[int(name[-1])], dst.at[int(name[-1])]
        cp = pltpu.make_async_copy(src, dst, r.ld.at[k])
        cp.start()
        loads[name] = cp

    def need(*names):
        for name in names:
            loads[name].wait()

    copies = []

    def leave(src, name):
        cp = pltpu.make_async_copy(src, outs[name], r.out.at[len(copies)])
        cp.start()
        copies.append(cp)

    need("pair", "pgain", "wt")
    pgain = r.pgain[...].astype(F32).reshape(1, 128)
    wt = r.wt[...]
    r.wall[hd] = jnp.concatenate([wt.astype(F32), jnp.zeros((8, 128), F32)], 0).astype(BF)
    for i in range(8):
        normed, _ = normalize(r.pair[i].astype(F32))
        r.rows[:, i, :] = dot_t(wt, (normed * pgain).astype(BF))
    r.part[...] = r.rows[...].reshape(64, N).astype(BF)
    r.bias[me] = r.part[...]
    bar = pltpu.get_barrier_semaphore()
    greet_samp(at, bar)
    cross = {"cplx": at["c"], "samp": at["z"] * 8 + (1 - at["l"]) * 4 + at["x"], "head": 1 - hd}
    for dev in (head_dev(at), core_dev(at), cross):
        signal(bar, dev)
    pl.semaphore_wait(bar, NS + 2)

    def bias_copy(i):
        return rcopy(
            r.part, r.bias.at[me], r.bs.at[0], r.br.at[0], samp_dev(at, (me + i) % NS)
        )

    loop(NS - 1, lambda i: bias_copy(i + 1).start())
    wt_copy = rcopy(r.wall.at[hd], r.wall.at[hd], r.hs.at[0], r.hr.at[0], head_dev(at))
    wt_copy.start()

    r.small_a[...] = jnp.zeros(r.small_a.shape, F32)
    r.small_w[...] = jnp.zeros(r.small_w.shape, F32)
    need("single", "gain")
    gains = r.gain[...].astype(F32)

    def cond(i):
        rows = pl.ds(i * 32, 32)
        normed, inv = normalize(r.single[rows].astype(F32))
        r.shat[rows] = normed
        r.sinv[rows] = jnp.broadcast_to(inv, (32, 128))
        for w in range(2):
            scaled = normed * gains[w : w + 1]
            high = scaled.astype(BF)
            r.s_hi[w, rows] = high
            r.s_lo[w, rows] = (scaled - high.astype(F32)).astype(BF)

    loop(N // 32, cond)

    def modulation(w):
        adab = r.adab[...].astype(F32)
        zerob = r.zerob[...].astype(F32)
        for b in blocks:
            later = slice(D + b.start, D + b.stop)
            pre_gate = dot(r.s_hi[w], r.ada[w, :, b]) + dot(r.s_lo[w], r.ada[w, :, b])
            r.mg[w, :, b] = sigmoid(pre_gate + adab[w : w + 1, b])
            r.ms[:, b] = dot(r.s_hi[w], r.ada[w, :, later]) + dot(r.s_lo[w], r.ada[w, :, later])
            r.zg[w, :, b] = sigmoid(dot(r.single[...], r.zero[w, :, b]) + zerob[w : w + 1, b])

    def branch_start(w, x_ref, g_ref):
        def some(i):
            rows = pl.ds(i * 16, 16)
            if w == 1:
                normed, _ = normalize(r.act[rows].astype(F32))
                r.hat[rows] = normed
            else:
                normed = r.hat[rows]
            x_ref[rows] = (r.mg[w, rows] * normed + r.ms[rows]).astype(BF)
            g_ref[rows] = (r.zg[w, rows] * r.cot[rows].astype(F32)).astype(BF)

        loop(N // 16, some)

    need("adab", "zerob", "ada1", "zero1")
    modulation(1)
    need("act", "cot")
    branch_start(1, r.tin, r.gto)

    def branch_out(w, b, part):
        gate = r.zg[w, :, b]
        share = gate * part
        r.mixf[:, b] = share if w == 1 else r.mixf[:, b] + share
        grad = r.cot[:, b].astype(F32) * share * (1.0 - gate)
        r.zp[:, b] = grad.astype(BF)
        for j in range(2):
            row = 12 + 6 * w + b.start // 128 + j
            r.small_a[row : row + 1] = jnp.sum(grad[:, j * 128 : (j + 1) * 128], 0, keepdims=True)

    def branch_in(w, b, grad_in):
        gate = r.mg[w, :, b]
        share = gate * grad_in
        r.actf[:, b] = share if w == 1 else r.actf[:, b] + share
        grad = share * r.hat[:, b] * (1.0 - gate)
        r.pre[:, b] = grad.astype(BF)
        r.pre[:, D + b.start : D + b.stop] = grad_in.astype(BF)
        for j in range(2):
            row = 6 * w + b.start // 128 + j
            r.small_a[row : row + 1] = jnp.sum(grad[:, j * 128 : (j + 1) * 128], 0, keepdims=True)

    def conditioned(w, to):
        for i in range(6):
            put(to, T_ADA[w] + i * 48, dot(r.s_t[w], r.pre[:, i * 256 : (i + 1) * 256]))
        for i, b in enumerate(blocks):
            value = dot(r.one_t[...], r.zp[:, b])
            if w == 1 and i == 2:
                put(r.tiles[3], T_ZERO2, value)
            else:
                put(to, T_ZERO[w] + i * 48, value)

    def conditioning_back(w):
        for j in range(3):
            b = slice(j * 128, (j + 1) * 128)
            scaled = dot_t(r.pre[...], r.ada[w, b, :])
            row = 24 + 3 * w + j
            r.small_a[row : row + 1] = jnp.sum(scaled * r.shat[:, b], 0, keepdims=True)
            share = scaled * gains[w : w + 1, b]
            through = dot_t(r.zp[...], r.zero[w, b, :])
            r.gsh[:, b] = share if w == 1 else r.gsh[:, b] + share
            r.zterm[:, b] = through if w == 1 else r.zterm[:, b] + through

    for w in range(2):
        r.s_t[w] = flip(r.s_hi[w])
    r.one_t[...] = flip(r.single[...])
    need("win", "hid")
    for b in blocks:
        gate_in = dot(r.tin[...], r.win[0, :, b])
        up_in = dot(r.tin[...], r.win[1, :, b])
        grad_hidden = dot_t(r.gto[...], r.hid[b, :])
        sig = sigmoid(gate_in)
        silu = gate_in * sig
        r.hidden[:, b] = (silu * up_in).astype(BF)
        r.ffn[:, b] = (grad_hidden * up_in * sig * (1.0 + gate_in * (1.0 - sig))).astype(BF)
        r.ffn[:, D + b.start : D + b.stop] = (grad_hidden * silu).astype(BF)
    sums = Sums(r, at)
    r.flipped[...] = flip(r.hidden[...])
    for i, b in enumerate(blocks):
        value = dot(r.flipped[...], r.gto[:, b])
        if i < 2:
            put(r.tiles[0], T_HID + i * 96, value)
        else:
            put(r.tiles[0], T_HID + 192, value[:, :128])
            put(r.tiles[0], T_HID + 240, value[:256, 128:])
            put(r.tiles[2], T_HID2, value[256:, 128:])
    r.flipped[...] = flip(r.tin[...])
    for i in range(6):
        put(r.tiles[0], T_IN + i * 96, dot(r.flipped[...], r.ffn[:, i * 256 : (i + 1) * 256]))
    sums.core_start(0)
    for b in blocks:
        branch_out(1, b, dot(r.hidden[...], r.hid[:, b]))
    for b in blocks:
        branch_in(
            1, b, dot_t(r.ffn[:, :D], r.win[0, b, :]) + dot_t(r.ffn[:, D:], r.win[1, b, :])
        )
    conditioned(1, r.tiles[1])
    sums.core_start(1)
    sums.core_end(0)
    sums.rs_start(0, 0)
    sums.rs_start(1, 0)
    need("ada0", "zero0")
    modulation(0)
    branch_start(0, r.ain, r.gao)
    sums.core_end(1)
    sums.rs_start(2, 0)
    sums.rs_start(3, 0)

    need("wq", "qb", "wout")
    r.qkv[0] = (dot(r.ain[...], r.wq[0]) + r.qb[...].astype(F32).reshape(1, 384)).astype(BF)
    r.qkv[1] = dot(r.ain[...], r.wq[1]).astype(BF)
    r.qkv[2] = dot(r.ain[...], r.wq[2]).astype(BF)
    r.gsig[...] = sigmoid(dot(r.ain[...], r.wq[3]))
    r.ggat[...] = dot_t(r.gao[...], r.wout[...])
    r.gatt[...] = (r.ggat[...] * r.gsig[...]).astype(BF)
    conditioning_back(1)
    arrived(r.bias.at[pl.ds(0, NS - 1)], r.bs.at[0], r.br.at[0], at)
    wt_copy.wait()
    r.acc[...] = jnp.zeros(r.acc.shape, F32)
    lane = lax.broadcasted_iota(jnp.int32, (1, 256), 1)
    mask = jnp.where(lane < counts_ref[0], 0.0, -1e9)
    for h in range(8):
        lo = 0 if h < 5 else 128
        win = slice(lo, lo + 256)
        first = h * HD - lo
        mine = (lane >= first) & (lane < first + HD)
        pick = jnp.where(mine, 1.0, 0.0).astype(BF)
        q_m = r.qkv[0, :, win] * pick
        k_m = r.qkv[1, :, win] * pick
        v_m = r.qkv[2, :, win] * pick
        g_m = r.gatt[:, win] * pick
        pair_rows = r.bias[:, (h // 2) * 16 : (h // 2) * 16 + 16, :].astype(F32)
        bias = pair_rows[:, (h % 2) * 8 : (h % 2) * 8 + 8, :].reshape(N, N)
        scores = dot_t(q_m, r.qkv[1, :, win]) * SCALE + bias + mask
        top = jnp.max(scores, -1, keepdims=True)
        weights = jnp.exp(scores - top)
        probs = weights * (1.0 / jnp.sum(weights, -1, keepdims=True))
        low = probs.astype(BF)
        r.acc[0, :, win] += dot(low, v_m)
        grad_probs = dot_t(g_m, r.qkv[2, :, win])
        delta = jnp.sum(probs * grad_probs, -1, keepdims=True)
        grad_s = probs * (grad_probs - delta)
        grad_low = grad_s.astype(BF)
        r.acc[1, :, win] += dot(grad_low, k_m)
        r.acc[2, :, win] += dot_l(grad_low, q_m)
        r.acc[3, :, win] += dot_l(low, g_m)
        split = grad_s.reshape(NS, 8, N)
        if h % 2 == 0:
            r.held[...] = split
        else:
            two = jnp.concatenate([r.held[...], split], 1).astype(BF)
            rows = slice((h // 2 % 2) * 16, (h // 2 % 2) * 16 + 16)
            if h < 4:
                r.gb[0, :, rows, :] = two
            else:
                for s in range(NS):
                    r.gb[1, s % 4 * 8 + s // 8 * 2 + s // 4 % 2, rows, :] = two[s]
    for half, axis in enumerate("zx"):
        for i in range(1, 4):
            dev, q = peer_on(at, axis, i)
            rcopy(
                r.gb.at[half, pl.ds(q * 8, 8)],
                r.gb1.at[half, i - 1],
                r.b1s.at[half],
                r.b1r.at[half],
                dev,
            ).start()
    attended = r.acc[0]
    gated = (r.gsig[...] * attended).astype(BF)
    r.gheads[:, 1152:] = (r.ggat[...] * attended * r.gsig[...] * (1.0 - r.gsig[...])).astype(BF)
    grad_q = (r.acc[1] * SCALE).astype(BF)
    r.gheads[:, :384] = grad_q
    r.gheads[:, 384:768] = (r.acc[2] * SCALE).astype(BF)
    r.gheads[:, 768:1152] = r.acc[3].astype(BF)
    for j in range(3):
        r.small_w[9 + j : 10 + j] = jnp.sum(
            grad_q[:, j * 128 : (j + 1) * 128].astype(F32), 0, keepdims=True
        )
    for b in blocks:
        branch_out(0, b, dot(gated, r.wout[:, b]))
    r.mixs[...] = r.mixf[...].astype(BF)
    mix_copy = rcopy(r.mixs, r.mixr, r.hs.at[1], r.hr.at[1], head_dev(at))
    mix_copy.start()
    r.flipped[:384] = flip(gated)
    for i, b in enumerate(blocks):
        put(r.tiles[2], T_OUT + i * 48, dot(r.flipped[:384], r.gao[:, b]))
    r.flipped[...] = flip(r.ain[...])
    for i in range(6):
        put(r.tiles[2], T_QKVG + i * 96, dot(r.flipped[...], r.gheads[:, i * 256 : (i + 1) * 256]))
    r.tiles[2][T_WPAD:] = jnp.zeros((TILES[2] - T_WPAD, 16, 128), BF)
    sums.core_start(2)
    for b in blocks:
        total = dot_t(r.gheads[:, :384], r.wq[0, b, :])
        for k in range(1, 4):
            total = total + dot_t(r.gheads[:, k * 384 : (k + 1) * 384], r.wq[k, b, :])
        branch_in(0, b, total)
    r.acts[...] = r.actf[...].astype(BF)
    act_copy = rcopy(r.acts, r.actr, r.hs.at[2], r.hr.at[2], head_dev(at))
    act_copy.start()
    conditioned(0, r.tiles[3])
    conditioning_back(0)
    r.tiles[3][T_SMALL:T_APAD] = r.small_a[...].astype(BF).reshape(2, 16, 128)
    r.tiles[3][T_APAD:] = jnp.zeros((TILES[3] - T_APAD, 16, 128), BF)
    sums.core_start(3)
    for g in FIRST:
        sums.rs_end(g, 0)
        sums.rs_start(g, 1)
    sums.core_end(2)
    sums.rs_start(4, 0)
    sums.rs_start(5, 0)
    for half in range(2):
        arrived(r.gb1.at[half], r.b1s.at[half], r.b1r.at[half], at)
        own = pl.ds(at["zx"[half]] * 8, 8)
        total = r.gb[half, own].astype(F32)
        for i in range(3):
            total = total + r.gb1[half, i].astype(F32)
        r.gb[half, own] = total.astype(BF)
        for i in range(1, 8):
            dev, q = peer_on(at, ("lx", "zl")[half], i)
            rcopy(
                r.gb.at[half, at["zx"[half]] * 8 + q],
                r.gb2.at[half, i - 1],
                r.b2s.at[half],
                r.b2r.at[half],
                dev,
            ).start()
    sums.core_end(3)
    for g in (6, 7, 8):
        sums.rs_start(g, 0)
    grad_single = norm_back(r.gsh[...], r.shat[...], r.sinv[:, :1]) + r.zterm[...]
    put(r.tiles[4], 0, grad_single)
    r.tiles[4][48:] = jnp.zeros((TILES[4] - 48, 16, 128), BF)
    sums.rs_start(9, 0)
    for g in FIRST:
        sums.rs_end(g, 1)
        sums.ag_start(g, 1)
    places = (at["z"] * 8 + at["l"] * 4 + at["x"], at["x"] * 8 + at["z"] * 2 + at["l"])
    for half in range(2):
        arrived(r.gb2.at[half], r.b2s.at[half], r.b2r.at[half], at)
        total = r.gb[half, places[half]].astype(F32)
        for i in range(7):
            total = total + r.gb2[half, i].astype(F32)
        r.gball[hd, half * 32 : half * 32 + 32] = total.astype(BF)
    rows_copy = rcopy(r.gball.at[hd], r.gball.at[hd], r.hs.at[3], r.hr.at[3], head_dev(at))
    rows_copy.start()
    mix_copy.wait()

    def last_mix(i):
        rows = pl.ds(i * 16, 16)
        value = r.mixs[rows].astype(F32) + r.mixr[rows].astype(F32)
        r.hidden[rows] = (r.act[rows].astype(F32) + value).astype(BF)

    loop(16, last_mix)
    leave(r.hidden, "mixed_o")
    for g in FIRST:
        sums.ag_end(g, 1)
        sums.ag_start(g, 0)

    rows_copy.wait()
    r.rows[...] = r.gball[hd].astype(F32).reshape(8, 8, N)
    r.held[:16] = r.gball[...].astype(F32).reshape(16, 8, N)
    wt_all = (
        jnp.concatenate([r.wall[0].astype(F32)[:8], r.wall[1].astype(F32)[:8]], 0).astype(BF)
    )
    weight = jnp.zeros((8, 128), F32)
    total = jnp.zeros((1, 128), F32)
    for i in range(8):
        normed, inv = normalize(r.pair[i].astype(F32))
        weight = weight + dot(r.rows[:, i, :].astype(BF), (normed * pgain).astype(BF))
        grad_low = dot_l(r.held[:16, i, :].astype(BF), wt_all)
        total = total + jnp.sum(grad_low * normed, 0, keepdims=True)
        r.gpair[i] = norm_back(grad_low * pgain, normed, inv)
    leave(r.gpair, "pair_o")
    r.small_w[:8] = weight
    r.small_w[8:9] = total

    def small_start(k):
        axis = "czxl"[k]
        mine = at[axis]
        r.slot[k, mine] = r.small_w[...]
        for i in range(1, SIZE.get(axis, 2)):
            dev = core_dev(at) if axis == "c" else peer_on(at, axis, i)[0]
            rcopy(r.slot.at[k, mine], r.slot.at[k, mine], r.ss.at[k], r.sr.at[k], dev).start()

    def small_end(k):
        arrived(r.slot.at[k, pl.ds(0, SIZE.get("czxl"[k], 2) - 1)], r.ss.at[k], r.sr.at[k], at)
        total = r.slot[k, 0]
        for i in range(1, SIZE.get("czxl"[k], 2)):
            total = total + r.slot[k, i]
        r.small_w[...] = total

    small_start(0)
    for g in SECOND:
        sums.rs_end(g, 0)
        sums.rs_start(g, 1)
    small_end(0)
    small_start(1)
    act_copy.wait()

    def last_act(i):
        rows = pl.ds(i * 16, 16)
        grad = r.acts[rows].astype(F32) + r.actr[rows].astype(F32)
        normed, inv = normalize(r.act[rows].astype(F32))
        r.mixf[rows] = r.cot[rows].astype(F32) + norm_back(grad, normed, inv)

    loop(16, last_act)
    leave(r.mixf, "act_o")
    small_end(1)
    small_start(2)
    for g in SECOND:
        sums.rs_end(g, 1)
        sums.ag_start(g, 1)
    small_end(2)
    small_start(3)
    for g in FIRST:
        sums.ag_end(g, 0)
        sums.share_start(g)
    for g in SECOND:
        sums.ag_end(g, 1)
        sums.ag_start(g, 0)
    small_end(3)
    leave(r.small_w, "small_o")
    for b in (0, 1):
        sums.share_end(b)
        leave(r.sums[b], "sum%d" % b)
    for g in SECOND:
        sums.ag_end(g, 0)
        sums.share_start(g)
    leave(r.sums[4], "sum4")
    for b in (2, 3):
        sums.share_end(b)
        leave(r.sums[b], "sum%d" % b)
    for cp in copies:
        cp.wait()


def whole(shape, dtype):
    return jax.ShapeDtypeStruct(shape, dtype)


def mega(counts, *args):
    return pl.pallas_call(
        mega_kernel,
        out_shape=tuple(whole(shape, dtype) for _, shape, dtype in OUTPUTS),
        in_specs=[pl.BlockSpec(memory_space=pltpu.SMEM)]
        + [pl.BlockSpec(memory_space=pl.ANY)] * len(INPUTS),
        out_specs=[pl.BlockSpec(memory_space=pl.ANY)] * len(OUTPUTS),
        scratch_shapes=[pltpu.VMEM(shape, BF) for _, shape in INPUTS]
        + [pltpu.VMEM(shape, dtype) for _, shape, dtype in SCRATCH]
        + [pltpu.VMEM((t, 16, 128), BF) for t in TILES]
        + [pltpu.VMEM((t, 16, 128), BF) for t in TILES]
        + [pltpu.VMEM(shape, BF) for _, shape in recv_shapes()]
        + [pltpu.SemaphoreType.DMA(shape) for _, shape in SEMS],
        compiler_params=pltpu.CompilerParams(
            collective_id=0, has_side_effects=True, vmem_limit_bytes=63 * 2**20
        ),
        name="block",
    )(counts, *args)


FINAL = (
    ("qkvg", (D, 4, 384)),
    ("win", (D, 2, D)),
    ("hid", (D, D)),
    ("ada", (2, 384, 2 * D)),
    ("zero", (2, 384, D)),
    ("wout", (384, D)),
    ("single", (N, 384)),
    ("adab", (2, D)),
    ("zerob", (2, D)),
    ("gain", (2, 384)),
    ("wt", (8, 128)),
    ("qb", (384,)),
    ("pgain", (128,)),
)


def finish_kernel(*refs):
    refs = list(refs)

    def take(count):
        got = refs[:count]
        del refs[:count]
        return got

    ins = take(9)
    outs = take(3 + len(FINAL))
    held = take(9)
    f = Refs()
    for (name, _), ref in zip(FINAL, take(len(FINAL))):
        setattr(f, name, ref)
    in_sem, out_sem = take(2)
    loads = []
    for i in range(9):
        cp = pltpu.make_async_copy(ins[i], held[i], in_sem.at[i])
        cp.start()
        loads.append(cp)
    copies = []

    def leave(name):
        i = [k for k, _ in FINAL].index(name)
        cp = pltpu.make_async_copy(getattr(f, name), outs[3 + i], out_sem.at[3 + i])
        cp.start()
        copies.append(cp)

    def get(b, start, rows):
        return held[b][pl.ds(start, rows // 16)].astype(F32).reshape(rows, 128)

    cols = [slice(j * 128, (j + 1) * 128) for j in range(12)]
    loads[0].wait()
    for k in range(2):
        for j in range(6):
            f.win[:, k, cols[j]] = get(0, T_IN + (k * 6 + j) * 48, 768)
    leave("win")
    for i in range(3):
        loads[6 + i].wait()
        cp = pltpu.make_async_copy(held[6 + i], outs[i], out_sem.at[i])
        cp.start()
        copies.append(cp)
    loads[2].wait()
    for j in range(5):
        f.hid[:, cols[j]] = get(0, T_HID + j * 48, 768)
    f.hid[:256, cols[5]] = get(0, T_HID + 240, 256)
    f.hid[256:, cols[5]] = get(2, T_HID2, 512)
    leave("hid")
    for k in range(4):
        for j in range(3):
            f.qkvg[:, k, cols[j]] = get(2, T_QKVG + (k * 3 + j) * 48, 768)
    leave("qkvg")
    for j in range(6):
        f.wout[:, cols[j]] = get(2, T_OUT + j * 24, 384)
    leave("wout")
    loads[1].wait()
    loads[3].wait()
    for w in range(2):
        for j in range(12):
            f.ada[w, :, cols[j]] = get(3 - 2 * w, T_ADA[w] + j * 24, 384)
    leave("ada")
    for w in range(2):
        for j in range(6):
            if w == 1 and j >= 4:
                f.zero[w, :, cols[j]] = get(3, T_ZERO2 + (j - 4) * 24, 384)
            else:
                f.zero[w, :, cols[j]] = get(3 - 2 * w, T_ZERO[w] + j * 24, 384)
    leave("zero")
    loads[4].wait()
    for j in range(3):
        f.single[:, cols[j]] = get(4, j * 16, 256)
    leave("single")
    small = held[3][T_SMALL:T_APAD].astype(F32).reshape(32, 128)
    for w in range(2):
        for j in range(6):
            f.adab[w : w + 1, cols[j]] = small[6 * w + j : 6 * w + j + 1]
            f.zerob[w : w + 1, cols[j]] = small[12 + 6 * w + j : 13 + 6 * w + j]
        for j in range(3):
            f.gain[w : w + 1, cols[j]] = small[24 + 3 * w + j : 25 + 3 * w + j]
    loads[5].wait()
    f.wt[...] = held[5][:8]
    f.pgain[...] = held[5][8]
    for j in range(3):
        f.qb[cols[j]] = held[5][9 + j]
    for name in ("adab", "zerob", "gain", "wt", "pgain", "qb"):
        leave(name)
    for cp in copies:
        cp.wait()


def finish(*args):
    shapes = [whole((N, D), BF), whole((N, D), F32), whole((8, N, 128), F32)]
    shapes += [whole(shape, F32) for _, shape in FINAL]
    return pl.pallas_call(
        finish_kernel,
        out_shape=tuple(shapes),
        in_specs=[pl.BlockSpec(memory_space=pl.ANY)] * len(args),
        out_specs=[pl.BlockSpec(memory_space=pl.ANY)] * len(shapes),
        scratch_shapes=[pltpu.VMEM(a.shape, a.dtype) for a in args]
        + [pltpu.VMEM(shape, F32) for _, shape in FINAL]
        + [pltpu.SemaphoreType.DMA((9,)), pltpu.SemaphoreType.DMA((len(shapes),))],
        compiler_params=pltpu.CompilerParams(vmem_limit_bytes=48 * 2**20),
        name="finish",
    )(*args)


def local(
    activations,
    conditioning,
    pair,
    counts,
    ada_weight,
    ada_bias,
    cond_gain,
    zero_weight,
    zero_bias,
    qkvg_weight,
    q_bias,
    out_weight,
    in_weight,
    hid_weight,
    pair_gain,
    bias_weight,
    cotangent,
):
    results = mega(
        counts,
        pair[0],
        pair_gain,
        bias_weight.T,
        conditioning[0],
        cond_gain,
        ada_weight,
        ada_bias,
        zero_weight,
        zero_bias,
        activations[0, 0],
        cotangent[0, 0],
        in_weight.transpose(1, 0, 2),
        hid_weight,
        qkvg_weight.transpose(1, 0, 2),
        q_bias,
        out_weight,
    )
    outs = finish(*results)
    mixed, act, grad_pair = outs[:3]
    o = dict(zip([name for name, _ in FINAL], outs[3:]))
    return (
        mixed[None, None],
        act[None, None],
        o["single"][None],
        grad_pair[None],
        o["ada"],
        o["adab"],
        o["gain"],
        o["zero"],
        o["zerob"],
        o["qkvg"],
        o["qb"],
        o["wout"],
        o["win"],
        o["hid"],
        o["pgain"],
        o["wt"].T,
    )


def solution(mesh):
    placed = (
        P("cplx", "samp", None, None),
        P("cplx", None, None),
        P("cplx", "samp", None, None),
        P("cplx"),
        P(),
        P(),
        P(),
        P(),
        P(),
        P(None, None, "head"),
        P("head"),
        P("head", None),
        P(None, None, "head"),
        P("head", None),
        P(),
        P(None, "head"),
        P("cplx", "samp", None, None),
    )
    return jax.shard_map(
        local,
        mesh=mesh,
        in_specs=placed,
        out_specs=(
            P("cplx", "samp", None, None),
            P("cplx", "samp", None, None),
            P("cplx", None, None),
            P("cplx", "samp", None, None),
            P(),
            P(),
            P(),
            P(),
            P(),
            P(None, None, "head"),
            P("head"),
            P("head", None),
            P(None, None, "head"),
            P("head", None),
            P(),
            P(None, "head"),
        ),
        check_vma=False,
    )
```

```python
import functools
import math

import jax
import jax.numpy as jnp
from jax import lax
from jax.experimental import pallas as pl
from jax.experimental.pallas import tpu as pltpu
from jax.sharding import PartitionSpec as P

D = 768
HD = 48
EPS = 1e-05
HIGH = lax.Precision.HIGHEST
MESH = pl.DeviceIdType.MESH
BF = jnp.bfloat16
F32 = jnp.float32
NS = 32
VMEM = pltpu.VMEM


def place():
    samp = lax.axis_index("samp")
    return {
        "c": lax.axis_index("cplx"),
        "h": lax.axis_index("head"),
        "s": samp,
        "z": samp // 8,
        "l": (samp // 4) % 2,
        "x": samp % 4,
        "y": lax.axis_index("head") * 2 + (samp // 4) % 2,
    }


SIZE = {"z": 4, "x": 4, "y": 4, "l": 2}


def extent(axes):
    size = 1
    for a in axes:
        size *= SIZE[a]
    return size


def index_on(at, axes):
    index = 0
    for a in axes:
        index = index * SIZE[a] + at[a]
    return index


def peer_on(at, axes, step):
    now = dict(at)
    for a in reversed(axes):
        now[a] = (at[a] + step % SIZE[a]) % SIZE[a]
        step //= SIZE[a]
    if "y" in axes:
        now["h"], now["l"] = now["y"] // 2, now["y"] % 2
    dev = {"cplx": at["c"], "samp": now["z"] * 8 + now["l"] * 4 + now["x"], "head": now["h"]}
    return dev, index_on(now, axes)


def signal(bar, dev):
    pl.semaphore_signal(bar, inc=1, device_id=dev, device_id_type=MESH)


def samp_dev(at, other):
    return {"cplx": at["c"], "samp": other, "head": at["h"]}


def head_dev(at):
    return {"cplx": at["c"], "samp": at["s"], "head": 1 - at["h"]}


def core_dev(at):
    return {"cplx": 1 - at["c"], "samp": at["s"], "head": at["h"]}


def rcopy(src, dst, send, recv, dev):
    return pltpu.make_async_remote_copy(
        src_ref=src, dst_ref=dst, send_sem=send, recv_sem=recv, device_id=dev, device_id_type=MESH
    )


def greet_samp(at, bar):
    def one(i, _):
        signal(bar, samp_dev(at, (at["s"] + i) % NS))
        return 0

    lax.fori_loop(1, NS, one, 0)


SCALE = 1.0 / math.sqrt(HD)


def dot(a, b):
    return lax.dot_general(a, b, (((1,), (0,)), ((), ())), preferred_element_type=F32)


def dot_t(a, b):
    return lax.dot_general(a, b, (((1,), (1,)), ((), ())), preferred_element_type=F32)


def dot_l(a, b):
    return lax.dot_general(a, b, (((0,), (0,)), ((), ())), preferred_element_type=F32)


def mean(v):
    return jnp.mean(v, -1, keepdims=True)


def normalize(tensor):
    centered = tensor - mean(tensor)
    inv_std = lax.rsqrt(mean(centered * centered) + EPS)
    return (centered * inv_std, inv_std)


def norm_back(grad_hat, normed, inv_std):
    return inv_std * (grad_hat - mean(grad_hat) - normed * mean(grad_hat * normed))


def sigmoid(v):
    return 1.0 / (1.0 + jnp.exp(-v))


def flip(v):
    return v.astype(F32).T.astype(BF)


def loop(count, body):
    def step(i, _):
        body(i)
        return 0

    lax.fori_loop(0, count, step, 0)


def put(ref, start, value):
    rows, cols = value.shape
    n = rows // 16
    for j in range(cols // 128):
        ref[pl.ds(start + j * n, n)] = (
            value[:, j * 128 : (j + 1) * 128].astype(BF).reshape(n, 16, 128)
        )


TILES = (384, 448, 384, 768, 512, 64)
HALF = (192, 224, 192, 384, 256, 64)
GROUPS = (
    (0, 0, 192, "z", "xl"),
    (1, 0, 224, "x", "zl"),
    (2, 0, 64, "y", "zx"),
    (2, 64, 64, "z", "yx"),
    (2, 128, 64, "x", "yz"),
    (3, 0, 192, "z", "xl"),
    (3, 192, 192, "x", "zl"),
    (4, 0, 128, "y", "xz"),
    (4, 128, 64, "z", "yx"),
    (4, 192, 64, "x", "yz"),
    (5, 0, 64, "y", "zx"),
)
FIRST = (0, 1, 2, 3, 4)
SECOND = (5, 6, 7, 8, 9, 10)
T_HID, T_IN0, T_IN = 0, 288, 0
T_ADA, T_ZERO = (0, 0), (288, 288)
T_QKVG, T_OUT, T_IN2, T_WPAD = 0, 576, 720, 752
T_ZERO2, T_SMALL, T_APAD = 432, 480, 482

INPUTS = (
    ("pair", (8, 256, 128)),
    ("pgain", (128,)),
    ("wt", (8, 128)),
    ("single", (256, 384)),
    ("gain", (2, 384)),
    ("ada", (2, 384, 1536)),
    ("adab", (2, 768)),
    ("zero", (2, 384, 768)),
    ("zerob", (2, 768)),
    ("act", (256, 768)),
    ("cot", (256, 768)),
    ("win", (2, 768, 768)),
    ("hid", (768, 768)),
    ("wq", (4, 768, 384)),
    ("qb", (384,)),
    ("wout", (384, 768)),
)
LOADS = (
    ("pair", "pgain", "wt", "single", "gain", "adab", "zerob", "ada1", "zero1", "act", "cot")
    + ("win", "hid", "ada0", "zero0", "wq", "qb", "wout")
)
N = 256
SCRATCH = (
    ("rows", (8, 8, N), F32),
    ("part", (64, N), BF),
    ("bias", (NS, 64, N), BF),
    ("wall", (2, 16, 128), BF),
    ("shat", (N, 384), F32),
    ("sinv", (N, 128), F32),
    ("s_hi", (2, N, 384), BF),
    ("s_lo", (2, N, 384), BF),
    ("s_t", (2, 384, N), BF),
    ("one_t", (384, N), BF),
    ("mg", (2, N, D), F32),
    ("ms", (N, D), F32),
    ("zg", (2, N, D), F32),
    ("hat", (N, D), F32),
    ("ain", (N, D), BF),
    ("tin", (N, D), BF),
    ("gao", (N, D), BF),
    ("gto", (N, D), BF),
    ("hidden", (N, D), BF),
    ("ffn", (N, 2 * D), BF),
    ("pre", (N, 2 * D), BF),
    ("zp", (N, D), BF),
    ("mixf", (N, D), F32),
    ("actf", (N, D), F32),
    ("mixs", (N, D), BF),
    ("mixr", (N, D), BF),
    ("acts", (N, D), BF),
    ("actr", (N, D), BF),
    ("gsh", (N, 384), F32),
    ("zterm", (N, 384), F32),
    ("qkv", (3, N, 384), BF),
    ("gsig", (N, 384), F32),
    ("ggat", (N, 384), F32),
    ("gatt", (N, 384), BF),
    ("acc", (4, N, 384), F32),
    ("gheads", (N, 1536), BF),
    ("flipped", (D, N), BF),
    ("held", (NS, 8, N), F32),
    ("small_a", (32, 128), F32),
    ("small_w", (16, 128), F32),
    ("gb", (2, NS, 32, N), BF),
    ("gb1", (2, 3, 8, 32, N), BF),
    ("gb2", (2, 7, 32, N), BF),
    ("gball", (2, 64, N), BF),
    ("gpair", (8, N, 128), F32),
    ("slot", (4, 4, 16, 128), F32),
)
SEMS = (
    ("ld", (len(LOADS),)),
    ("bs", (1,)),
    ("br", (1,)),
    ("hs", (4,)),
    ("hr", (4,)),
    ("cs", (5,)),
    ("cr", (5,)),
    ("rs", (len(GROUPS), 6)),
    ("rr", (len(GROUPS), 6)),
    ("fs", (5,)),
    ("fr", (5,)),
    ("b1s", (2,)),
    ("b1r", (2,)),
    ("b2s", (2,)),
    ("b2r", (2,)),
    ("out", (12,)),
    ("ss", (4,)),
    ("sr", (4,)),
)
OUTPUTS = tuple(("sum%d" % i, (t, 16, 128), BF) for i, t in enumerate(TILES)) + (
    ("small_o", (16, 128), F32),
    ("mixed_o", (N, D), BF),
    ("act_o", (N, D), F32),
    ("pair_o", (8, N, 128), F32),
)


class Refs:
    pass


def recv_shapes():
    shapes = []
    for g, (_, _, tiles, _, plane) in enumerate(GROUPS):
        part = tiles // 4
        small = part // extent(plane)
        shapes.append(((g, "opp"), (2, part // 2, 16, 128)))
        shapes.append(((g, "near"), (2, part, 16, 128)))
        shapes.append(((g, "plane"), (extent(plane) - 1, small, 16, 128)))
    return shapes


def arrived(like, send, recv, at):
    cp = rcopy(like, like, send, recv, core_dev(at))
    cp.wait_send()
    cp.wait_recv()


class Sums:
    def __init__(self, r, at):
        self.r, self.at = r, at
        self.shift = [at["c"] * HALF[b] if b < 5 else 0 for b in range(6)]
        self.pairs = {}

    def core_start(self, buf):
        r, at, half = self.r, self.at, HALF[buf]
        other = pl.ds((1 - at["c"]) * half, half)
        cp = rcopy(
            r.tiles[buf].at[other], r.sums[buf].at[other], r.cs.at[buf], r.cr.at[buf], core_dev(at)
        )
        cp.start()
        self.pairs[buf] = cp

    def core_end(self, buf):
        self.pairs[buf].wait()
        self.add(self.r.tiles[buf], self.shift[buf], HALF[buf], [self.r.sums[buf].at[pl.ds(self.shift[buf], HALF[buf])]])

    def add(self, to, start, count, others, src=None):
        src = to if src is None else src
        block = max(b for b in range(1, 17) if count % b == 0)

        def some(i):
            mine = pl.ds(start + i * block, block)
            rows = pl.ds(i * block, block)
            total = src[mine].astype(F32)
            for o in others:
                total = total + o[rows].astype(F32)
            to[mine] = total.astype(BF)

        loop(count // block, some)

    def send(self, g, sem, src, dst, dev):
        rcopy(src, dst, self.r.rs.at[g, sem], self.r.rr.at[g, sem], dev).start()

    def wait(self, g, sem, like):
        arrived(like, self.r.rs.at[g, sem], self.r.rr.at[g, sem], self.at)

    def ring(self, g):
        buf, start, tiles, axis, _ = GROUPS[g]
        part = tiles // 4
        first = self.shift[buf] + start
        quarters = [first + (self.at[axis] + i) % 4 * part for i in range(4)]
        right, left = peer_on(self.at, axis, 1)[0], peer_on(self.at, axis, 3)[0]
        return buf, part, quarters, right, left

    def ring_start(self, g):
        buf, part, (_, to_right, far, to_left), right, left = self.ring(g)
        half = part // 2
        tiles, opp, near = self.r.tiles[buf], self.r.recv[g, "opp"], self.r.recv[g, "near"]
        self.send(g, 0, tiles.at[pl.ds(far, half)], opp.at[0], right)
        self.send(g, 0, tiles.at[pl.ds(far + half, half)], opp.at[1], left)
        low, high = pl.ds(0, half), pl.ds(half, half)
        self.send(g, 1, tiles.at[pl.ds(to_right + half, half)], near.at[0, high], right)
        self.send(g, 1, tiles.at[pl.ds(to_left, half)], near.at[1, low], left)

    def ring_relay(self, g):
        buf, part, (_, to_right, _, to_left), right, left = self.ring(g)
        half = part // 2
        tiles, opp, near = self.r.tiles[buf], self.r.recv[g, "opp"], self.r.recv[g, "near"]
        self.wait(g, 0, opp)
        low, high = pl.ds(0, half), pl.ds(half, half)
        self.add(tiles, to_right, half, [opp.at[0]])
        self.send(g, 1, tiles.at[pl.ds(to_right, half)], near.at[0, low], right)
        self.add(tiles, to_left + half, half, [opp.at[1]])
        self.send(g, 1, tiles.at[pl.ds(to_left + half, half)], near.at[1, high], left)

    def plane_start(self, g):
        buf, part, quarters, _, _ = self.ring(g)
        near = self.r.recv[g, "near"]
        self.wait(g, 1, near)
        self.add(self.r.tiles[buf], quarters[0], part, [near.at[0], near.at[1]])
        plane = GROUPS[g][4]
        small = part // extent(plane)
        for i in range(1, extent(plane)):
            dev, q = peer_on(self.at, plane, i)
            src = self.r.tiles[buf].at[pl.ds(quarters[0] + q * small, small)]
            self.send(g, 2, src, self.r.recv[g, "plane"].at[i - 1], dev)

    def gather_start(self, g):
        buf, part, quarters, _, _ = self.ring(g)
        plane = GROUPS[g][4]
        count = extent(plane)
        small = part // count
        got = self.r.recv[g, "plane"]
        self.wait(g, 2, got)
        here = quarters[0] + index_on(self.at, plane) * small
        self.add(
            self.r.sums[buf], here, small, [got.at[i] for i in range(count - 1)], self.r.tiles[buf]
        )
        mine = self.r.sums[buf].at[pl.ds(here, small)]
        for i in range(1, count):
            self.send(g, 3, mine, mine, peer_on(self.at, plane, i)[0])

    def gather_ring(self, g):
        buf, part, quarters, right, left = self.ring(g)
        sums = self.r.sums[buf]
        count = extent(GROUPS[g][4])
        self.wait(g, 3, sums.at[pl.ds(0, (count - 1) * (part // count))])
        mine = sums.at[pl.ds(quarters[0], part)]
        self.send(g, 4, mine, mine, right)
        self.send(g, 4, mine, mine, left)
        self.share(g, 0)

    def gather_relay(self, g):
        buf, part, (_, of_right, _, of_left), right, left = self.ring(g)
        half = part // 2
        sums = self.r.sums[buf]
        self.wait(g, 4, sums.at[pl.ds(0, 2 * part)])
        low = sums.at[pl.ds(of_left, half)]
        self.send(g, 5, low, low, right)
        high = sums.at[pl.ds(of_right + half, half)]
        self.send(g, 5, high, high, left)
        self.share(g, 1)
        self.share(g, 3)

    def gather_end(self, g):
        buf, part, _, _, _ = self.ring(g)
        self.wait(g, 5, self.r.sums[buf].at[pl.ds(0, part)])
        self.share(g, 2)

    def share(self, g, i):
        buf, part, quarters, _, _ = self.ring(g)
        r = self.r
        if buf < 5:
            rows = r.sums[buf].at[pl.ds(quarters[i], part)]
            rcopy(rows, rows, r.fs.at[buf], r.fr.at[buf], core_dev(self.at)).start()

    def share_end(self, buf):
        r = self.r
        arrived(r.sums[buf].at[pl.ds(0, HALF[buf])], r.fs.at[buf], r.fr.at[buf], self.at)


def mega_kernel(*refs):
    r = Refs()
    refs = list(refs)

    def take(count):
        got = refs[:count]
        del refs[:count]
        return got

    counts_ref = take(1)[0]
    hbm = take(len(INPUTS))
    outs = dict(zip([o[0] for o in OUTPUTS], take(len(OUTPUTS))))
    for (name, _), ref in zip(INPUTS, take(len(INPUTS))):
        setattr(r, name, ref)
    for (name, _, _), ref in zip(SCRATCH, take(len(SCRATCH))):
        setattr(r, name, ref)
    r.tiles = take(6)
    r.sums = take(6)
    r.recv = {}
    for (key, _), ref in zip(recv_shapes(), take(len(recv_shapes()))):
        r.recv[key] = ref
    for (name, _), ref in zip(SEMS, take(len(SEMS))):
        setattr(r, name, ref)

    at = place()
    me, hd = at["s"], at["h"]
    blocks = [slice(i * 256, (i + 1) * 256) for i in range(3)]
    loads = {}
    places = {name: i for i, (name, _) in enumerate(INPUTS)}
    for k, name in enumerate(LOADS):
        src, dst = hbm[places[name.rstrip("01")]], getattr(r, name.rstrip("01"))
        if name[-1] in "01":
            src, dst = src.at[int(name[-1])], dst.at[int(name[-1])]
        cp = pltpu.make_async_copy(src, dst, r.ld.at[k])
        cp.start()
        loads[name] = cp

    def need(*names):
        for name in names:
            loads[name].wait()

    copies = []

    def leave(src, name, rows=None):
        dst = outs[name] if rows is None else outs[name].at[rows]
        cp = pltpu.make_async_copy(src, dst, r.out.at[len(copies)])
        cp.start()
        copies.append(cp)

    need("pair", "pgain", "wt")
    pgain = r.pgain[...].astype(F32).reshape(1, 128)
    wt = r.wt[...]
    r.wall[hd] = jnp.concatenate([wt.astype(F32), jnp.zeros((8, 128), F32)], 0).astype(BF)
    for i in range(8):
        normed, _ = normalize(r.pair[i].astype(F32))
        r.rows[:, i, :] = dot_t(wt, (normed * pgain).astype(BF))
    r.part[...] = r.rows[...].reshape(64, N).astype(BF)
    r.bias[me] = r.part[...]
    bar = pltpu.get_barrier_semaphore()
    greet_samp(at, bar)
    cross = {"cplx": at["c"], "samp": at["z"] * 8 + (1 - at["l"]) * 4 + at["x"], "head": 1 - hd}
    for dev in (head_dev(at), core_dev(at), cross):
        signal(bar, dev)
    pl.semaphore_wait(bar, NS + 2)

    def bias_copy(i):
        return rcopy(
            r.part, r.bias.at[me], r.bs.at[0], r.br.at[0], samp_dev(at, (me + i) % NS)
        )

    loop(NS - 1, lambda i: bias_copy(i + 1).start())
    wt_copy = rcopy(r.wall.at[hd], r.wall.at[hd], r.hs.at[0], r.hr.at[0], head_dev(at))
    wt_copy.start()

    r.small_a[...] = jnp.zeros(r.small_a.shape, F32)
    r.small_w[...] = jnp.zeros(r.small_w.shape, F32)
    need("single", "gain")
    gains = r.gain[...].astype(F32)

    def cond(i):
        rows = pl.ds(i * 32, 32)
        normed, inv = normalize(r.single[rows].astype(F32))
        r.shat[rows] = normed
        r.sinv[rows] = jnp.broadcast_to(inv, (32, 128))
        for w in range(2):
            scaled = normed * gains[w : w + 1]
            high = scaled.astype(BF)
            r.s_hi[w, rows] = high
            r.s_lo[w, rows] = (scaled - high.astype(F32)).astype(BF)

    loop(N // 32, cond)

    def modulation(w):
        adab = r.adab[...].astype(F32)
        zerob = r.zerob[...].astype(F32)
        for b in blocks:
            later = slice(D + b.start, D + b.stop)
            pre_gate = dot(r.s_hi[w], r.ada[w, :, b]) + dot(r.s_lo[w], r.ada[w, :, b])
            r.mg[w, :, b] = sigmoid(pre_gate + adab[w : w + 1, b])
            r.ms[:, b] = dot(r.s_hi[w], r.ada[w, :, later]) + dot(r.s_lo[w], r.ada[w, :, later])
            r.zg[w, :, b] = sigmoid(dot(r.single[...], r.zero[w, :, b]) + zerob[w : w + 1, b])

    def branch_start(w, x_ref, g_ref):
        def some(i):
            rows = pl.ds(i * 16, 16)
            if w == 1:
                normed, _ = normalize(r.act[rows].astype(F32))
                r.hat[rows] = normed
            else:
                normed = r.hat[rows]
            x_ref[rows] = (r.mg[w, rows] * normed + r.ms[rows]).astype(BF)
            g_ref[rows] = (r.zg[w, rows] * r.cot[rows].astype(F32)).astype(BF)

        loop(N // 16, some)

    need("adab", "zerob", "ada1", "zero1")
    modulation(1)
    need("act", "cot")
    branch_start(1, r.tin, r.gto)

    def branch_out(w, b, part):
        gate = r.zg[w, :, b]
        share = gate * part
        r.mixf[:, b] = share if w == 1 else r.mixf[:, b] + share
        grad = r.cot[:, b].astype(F32) * share * (1.0 - gate)
        r.zp[:, b] = grad.astype(BF)
        for j in range(2):
            row = 12 + 6 * w + b.start // 128 + j
            r.small_a[row : row + 1] = jnp.sum(grad[:, j * 128 : (j + 1) * 128], 0, keepdims=True)

    def branch_in(w, b, grad_in):
        gate = r.mg[w, :, b]
        share = gate * grad_in
        r.actf[:, b] = share if w == 1 else r.actf[:, b] + share
        grad = share * r.hat[:, b] * (1.0 - gate)
        r.pre[:, b] = grad.astype(BF)
        r.pre[:, D + b.start : D + b.stop] = grad_in.astype(BF)
        for j in range(2):
            row = 6 * w + b.start // 128 + j
            r.small_a[row : row + 1] = jnp.sum(grad[:, j * 128 : (j + 1) * 128], 0, keepdims=True)

    def conditioned(w, to):
        for i in range(6):
            put(to, T_ADA[w] + i * 48, dot(r.s_t[w], r.pre[:, i * 256 : (i + 1) * 256]))
        for i, b in enumerate(blocks):
            value = dot(r.one_t[...], r.zp[:, b])
            if w == 1 and i == 2:
                put(r.tiles[4], T_ZERO2, value)
            else:
                put(to, T_ZERO[w] + i * 48, value)

    def conditioning_back(w):
        for j in range(3):
            b = slice(j * 128, (j + 1) * 128)
            scaled = dot_t(r.pre[...], r.ada[w, b, :])
            row = 24 + 3 * w + j
            r.small_a[row : row + 1] = jnp.sum(scaled * r.shat[:, b], 0, keepdims=True)
            share = scaled * gains[w : w + 1, b]
            through = dot_t(r.zp[...], r.zero[w, b, :])
            r.gsh[:, b] = share if w == 1 else r.gsh[:, b] + share
            r.zterm[:, b] = through if w == 1 else r.zterm[:, b] + through

    for w in range(2):
        r.s_t[w] = flip(r.s_hi[w])
    r.one_t[...] = flip(r.single[...])
    need("win", "hid")
    for b in blocks:
        gate_in = dot(r.tin[...], r.win[0, :, b])
        up_in = dot(r.tin[...], r.win[1, :, b])
        grad_hidden = dot_t(r.gto[...], r.hid[b, :])
        sig = sigmoid(gate_in)
        silu = gate_in * sig
        r.hidden[:, b] = (silu * up_in).astype(BF)
        r.ffn[:, b] = (grad_hidden * up_in * sig * (1.0 + gate_in * (1.0 - sig))).astype(BF)
        r.ffn[:, D + b.start : D + b.stop] = (grad_hidden * silu).astype(BF)
    sums = Sums(r, at)
    r.flipped[...] = flip(r.hidden[...])
    for i, b in enumerate(blocks):
        put(r.tiles[0], T_HID + i * 96, dot(r.flipped[...], r.gto[:, b]))
    r.flipped[...] = flip(r.tin[...])
    put(r.tiles[0], T_IN0, dot(r.flipped[...], r.ffn[:, :256]))
    sums.core_start(0)
    for i in range(1, 6):
        value = dot(r.flipped[...], r.ffn[:, i * 256 : (i + 1) * 256])
        if i < 5:
            put(r.tiles[1], T_IN + (i - 1) * 96, value)
        else:
            put(r.tiles[1], T_IN + 384, value[:, :128])
            put(r.tiles[1], T_IN + 432, value[:256, 128:])
            put(r.tiles[3], T_IN2, value[256:, 128:])
    sums.core_start(1)
    sums.core_end(0)
    sums.ring_start(0)
    for b in blocks:
        branch_out(1, b, dot(r.hidden[...], r.hid[:, b]))
    for b in blocks:
        branch_in(
            1, b, dot_t(r.ffn[:, :D], r.win[0, b, :]) + dot_t(r.ffn[:, D:], r.win[1, b, :])
        )
    sums.core_end(1)
    sums.ring_start(1)
    conditioned(1, r.tiles[2])
    sums.core_start(2)
    need("ada0", "zero0")
    modulation(0)
    branch_start(0, r.ain, r.gao)
    sums.core_end(2)
    for g in (2, 3, 4):
        sums.ring_start(g)
    sums.ring_relay(0)

    need("wq", "qb", "wout")
    r.qkv[0] = (dot(r.ain[...], r.wq[0]) + r.qb[...].astype(F32).reshape(1, 384)).astype(BF)
    r.qkv[1] = dot(r.ain[...], r.wq[1]).astype(BF)
    r.qkv[2] = dot(r.ain[...], r.wq[2]).astype(BF)
    r.gsig[...] = sigmoid(dot(r.ain[...], r.wq[3]))
    r.ggat[...] = dot_t(r.gao[...], r.wout[...])
    r.gatt[...] = (r.ggat[...] * r.gsig[...]).astype(BF)
    conditioning_back(1)
    sums.ring_relay(1)
    arrived(r.bias.at[pl.ds(0, NS - 1)], r.bs.at[0], r.br.at[0], at)
    wt_copy.wait()
    r.acc[...] = jnp.zeros(r.acc.shape, F32)
    lane = lax.broadcasted_iota(jnp.int32, (1, 256), 1)
    mask = jnp.where(lane < counts_ref[0], 0.0, -1e9)
    for h in range(8):
        lo = 0 if h < 5 else 128
        win = slice(lo, lo + 256)
        first = h * HD - lo
        mine = (lane >= first) & (lane < first + HD)
        pick = jnp.where(mine, 1.0, 0.0).astype(BF)
        q_m = r.qkv[0, :, win] * pick
        k_m = r.qkv[1, :, win] * pick
        v_m = r.qkv[2, :, win] * pick
        g_m = r.gatt[:, win] * pick
        pair_rows = r.bias[:, (h // 2) * 16 : (h // 2) * 16 + 16, :].astype(F32)
        bias = pair_rows[:, (h % 2) * 8 : (h % 2) * 8 + 8, :].reshape(N, N)
        scores = dot_t(q_m, r.qkv[1, :, win]) * SCALE + bias + mask
        top = jnp.max(scores, -1, keepdims=True)
        weights = jnp.exp(scores - top)
        probs = weights * (1.0 / jnp.sum(weights, -1, keepdims=True))
        low = probs.astype(BF)
        r.acc[0, :, win] += dot(low, v_m)
        grad_probs = dot_t(g_m, r.qkv[2, :, win])
        delta = jnp.sum(probs * grad_probs, -1, keepdims=True)
        grad_s = probs * (grad_probs - delta)
        grad_low = grad_s.astype(BF)
        r.acc[1, :, win] += dot(grad_low, k_m)
        r.acc[2, :, win] += dot_l(grad_low, q_m)
        r.acc[3, :, win] += dot_l(low, g_m)
        split = grad_s.reshape(NS, 8, N)
        if h % 2 == 0:
            r.held[...] = split
        else:
            two = jnp.concatenate([r.held[...], split], 1).astype(BF)
            rows = slice((h // 2 % 2) * 16, (h // 2 % 2) * 16 + 16)
            if h < 4:
                r.gb[0, :, rows, :] = two
            else:
                for s in range(NS):
                    r.gb[1, s % 4 * 8 + s // 8 * 2 + s // 4 % 2, rows, :] = two[s]
        if h == 1:
            for g in (2, 3, 4):
                sums.ring_relay(g)
        if h == 4:
            sums.plane_start(0)
        if h == 6:
            sums.plane_start(1)
    for half, axis in enumerate("zx"):
        for i in range(1, 4):
            dev, q = peer_on(at, axis, i)
            rcopy(
                r.gb.at[half, pl.ds(q * 8, 8)],
                r.gb1.at[half, i - 1],
                r.b1s.at[half],
                r.b1r.at[half],
                dev,
            ).start()
    attended = r.acc[0]
    gated = (r.gsig[...] * attended).astype(BF)
    r.gheads[:, 1152:] = (r.ggat[...] * attended * r.gsig[...] * (1.0 - r.gsig[...])).astype(BF)
    grad_q = (r.acc[1] * SCALE).astype(BF)
    r.gheads[:, :384] = grad_q
    r.gheads[:, 384:768] = (r.acc[2] * SCALE).astype(BF)
    r.gheads[:, 768:1152] = r.acc[3].astype(BF)
    for j in range(3):
        r.small_w[9 + j : 10 + j] = jnp.sum(
            grad_q[:, j * 128 : (j + 1) * 128].astype(F32), 0, keepdims=True
        )
    for b in blocks:
        branch_out(0, b, dot(gated, r.wout[:, b]))
    r.mixs[...] = r.mixf[...].astype(BF)
    mix_copy = rcopy(r.mixs, r.mixr, r.hs.at[1], r.hr.at[1], head_dev(at))
    mix_copy.start()
    for g in (2, 3, 4):
        sums.plane_start(g)
    r.flipped[:384] = flip(gated)
    for i, b in enumerate(blocks):
        put(r.tiles[3], T_OUT + i * 48, dot(r.flipped[:384], r.gao[:, b]))
    r.flipped[...] = flip(r.ain[...])
    for i in range(6):
        put(r.tiles[3], T_QKVG + i * 96, dot(r.flipped[...], r.gheads[:, i * 256 : (i + 1) * 256]))
    r.tiles[3][T_WPAD:] = jnp.zeros((TILES[3] - T_WPAD, 16, 128), BF)
    sums.core_start(3)
    for g in (0, 1):
        sums.gather_start(g)
    for b in blocks:
        total = dot_t(r.gheads[:, :384], r.wq[0, b, :])
        for k in range(1, 4):
            total = total + dot_t(r.gheads[:, k * 384 : (k + 1) * 384], r.wq[k, b, :])
        branch_in(0, b, total)
    r.acts[...] = r.actf[...].astype(BF)
    act_copy = rcopy(r.acts, r.actr, r.hs.at[2], r.hr.at[2], head_dev(at))
    act_copy.start()
    conditioned(0, r.tiles[4])
    conditioning_back(0)
    r.tiles[4][T_SMALL:T_APAD] = r.small_a[...].astype(BF).reshape(2, 16, 128)
    r.tiles[4][T_APAD:] = jnp.zeros((TILES[4] - T_APAD, 16, 128), BF)
    sums.core_start(4)
    sums.core_end(3)
    for g in (5, 6):
        sums.ring_start(g)
    grad_single = norm_back(r.gsh[...], r.shat[...], r.sinv[:, :1]) + r.zterm[...]
    put(r.tiles[5], 0, grad_single)
    r.tiles[5][48:] = jnp.zeros((TILES[5] - 48, 16, 128), BF)
    sums.ring_start(10)
    for g in (2, 3, 4):
        sums.gather_start(g)
    for g in (0, 1):
        sums.gather_ring(g)
    sums.core_end(4)
    for g in (7, 8, 9):
        sums.ring_start(g)
    for half in range(2):
        arrived(r.gb1.at[half], r.b1s.at[half], r.b1r.at[half], at)
        own = pl.ds(at["zx"[half]] * 8, 8)
        total = r.gb[half, own].astype(F32)
        for i in range(3):
            total = total + r.gb1[half, i].astype(F32)
        r.gb[half, own] = total.astype(BF)
        for i in range(1, 8):
            dev, q = peer_on(at, ("lx", "zl")[half], i)
            rcopy(
                r.gb.at[half, at["zx"[half]] * 8 + q],
                r.gb2.at[half, i - 1],
                r.b2s.at[half],
                r.b2r.at[half],
                dev,
            ).start()
    for g in (5, 6, 10):
        sums.ring_relay(g)
    for g in (2, 3, 4):
        sums.gather_ring(g)
    for g in (7, 8, 9):
        sums.ring_relay(g)
    for g in (0, 1):
        sums.gather_relay(g)
    places = (at["z"] * 8 + at["l"] * 4 + at["x"], at["x"] * 8 + at["z"] * 2 + at["l"])
    for half in range(2):
        arrived(r.gb2.at[half], r.b2s.at[half], r.b2r.at[half], at)
        total = r.gb[half, places[half]].astype(F32)
        for i in range(7):
            total = total + r.gb2[half, i].astype(F32)
        r.gball[hd, half * 32 : half * 32 + 32] = total.astype(BF)
    rows_copy = rcopy(r.gball.at[hd], r.gball.at[hd], r.hs.at[3], r.hr.at[3], head_dev(at))
    rows_copy.start()
    mix_copy.wait()

    def last_mix(i):
        rows = pl.ds(i * 16, 16)
        value = r.mixs[rows].astype(F32) + r.mixr[rows].astype(F32)
        r.hidden[rows] = (r.act[rows].astype(F32) + value).astype(BF)

    loop(16, last_mix)
    leave(r.hidden, "mixed_o")
    for g in (5, 6):
        sums.plane_start(g)
    for g in (2, 3, 4):
        sums.gather_relay(g)
    for g in (7, 8, 9, 10):
        sums.plane_start(g)

    rows_copy.wait()
    r.rows[...] = r.gball[hd].astype(F32).reshape(8, 8, N)
    r.held[:16] = r.gball[...].astype(F32).reshape(16, 8, N)
    wt_all = (
        jnp.concatenate([r.wall[0].astype(F32)[:8], r.wall[1].astype(F32)[:8]], 0).astype(BF)
    )
    weight = jnp.zeros((8, 128), F32)
    total = jnp.zeros((1, 128), F32)
    for i in range(8):
        normed, inv = normalize(r.pair[i].astype(F32))
        weight = weight + dot(r.rows[:, i, :].astype(BF), (normed * pgain).astype(BF))
        grad_low = dot_l(r.held[:16, i, :].astype(BF), wt_all)
        total = total + jnp.sum(grad_low * normed, 0, keepdims=True)
        r.gpair[i] = norm_back(grad_low * pgain, normed, inv)
    leave(r.gpair, "pair_o")
    r.small_w[:8] = weight
    r.small_w[8:9] = total

    def small_start(k):
        axis = "czxl"[k]
        mine = at[axis]
        r.slot[k, mine] = r.small_w[...]
        for i in range(1, SIZE.get(axis, 2)):
            dev = core_dev(at) if axis == "c" else peer_on(at, axis, i)[0]
            rcopy(r.slot.at[k, mine], r.slot.at[k, mine], r.ss.at[k], r.sr.at[k], dev).start()

    def small_end(k):
        arrived(r.slot.at[k, pl.ds(0, SIZE.get("czxl"[k], 2) - 1)], r.ss.at[k], r.sr.at[k], at)
        total = r.slot[k, 0]
        for i in range(1, SIZE.get("czxl"[k], 2)):
            total = total + r.slot[k, i]
        r.small_w[...] = total

    small_start(0)
    for g in FIRST:
        sums.gather_end(g)
    small_end(0)
    small_start(1)
    for g in SECOND:
        sums.gather_start(g)
    act_copy.wait()

    def last_act(i):
        rows = pl.ds(i * 16, 16)
        grad = r.acts[rows].astype(F32) + r.actr[rows].astype(F32)
        normed, inv = normalize(r.act[rows].astype(F32))
        r.mixf[rows] = r.cot[rows].astype(F32) + norm_back(grad, normed, inv)

    loop(16, last_act)
    leave(r.mixf, "act_o")
    small_end(1)
    small_start(2)
    for g in SECOND:
        sums.gather_ring(g)
    for b in (0, 1, 2):
        sums.share_end(b)
        leave(r.sums[b], "sum%d" % b)
    small_end(2)
    small_start(3)
    for g in SECOND:
        sums.gather_relay(g)
    small_end(3)
    leave(r.small_w, "small_o")
    for g in SECOND:
        sums.gather_end(g)
    leave(r.sums[5], "sum5")
    own = [pl.ds(sums.shift[b], HALF[b]) for b in range(5)]
    other = [pl.ds((1 - at["c"]) * HALF[b], HALF[b]) for b in range(5)]
    for b in (3, 4):
        leave(r.sums[b].at[own[b]], "sum%d" % b, own[b])
    for b in (3, 4):
        sums.share_end(b)
        leave(r.sums[b].at[other[b]], "sum%d" % b, other[b])
    for cp in copies:
        cp.wait()


def whole(shape, dtype):
    return jax.ShapeDtypeStruct(shape, dtype)


def mega(counts, *args):
    return pl.pallas_call(
        mega_kernel,
        out_shape=tuple(whole(shape, dtype) for _, shape, dtype in OUTPUTS),
        in_specs=[pl.BlockSpec(memory_space=pltpu.SMEM)]
        + [pl.BlockSpec(memory_space=pl.ANY)] * len(INPUTS),
        out_specs=[pl.BlockSpec(memory_space=pl.ANY)] * len(OUTPUTS),
        scratch_shapes=[pltpu.VMEM(shape, BF) for _, shape in INPUTS]
        + [pltpu.VMEM(shape, dtype) for _, shape, dtype in SCRATCH]
        + [pltpu.VMEM((t, 16, 128), BF) for t in TILES]
        + [pltpu.VMEM((t, 16, 128), BF) for t in TILES]
        + [pltpu.VMEM(shape, BF) for _, shape in recv_shapes()]
        + [pltpu.SemaphoreType.DMA(shape) for _, shape in SEMS],
        compiler_params=pltpu.CompilerParams(
            collective_id=0, has_side_effects=True, vmem_limit_bytes=63 * 2**20
        ),
        name="block",
    )(counts, *args)


FINAL = (
    ("qkvg", (D, 4, 384)),
    ("win", (D, 2, D)),
    ("hid", (D, D)),
    ("ada", (2, 384, 2 * D)),
    ("zero", (2, 384, D)),
    ("wout", (384, D)),
    ("single", (N, 384)),
    ("adab", (2, D)),
    ("zerob", (2, D)),
    ("gain", (2, 384)),
    ("wt", (8, 128)),
    ("qb", (384,)),
    ("pgain", (128,)),
)


def finish_kernel(*refs):
    refs = list(refs)

    def take(count):
        got = refs[:count]
        del refs[:count]
        return got

    ins = take(10)
    outs = take(3 + len(FINAL))
    held = take(10)
    f = Refs()
    for (name, _), ref in zip(FINAL, take(len(FINAL))):
        setattr(f, name, ref)
    in_sem, out_sem = take(2)
    loads = []
    for i in range(10):
        cp = pltpu.make_async_copy(ins[i], held[i], in_sem.at[i])
        cp.start()
        loads.append(cp)
    copies = []

    def leave(name):
        i = [k for k, _ in FINAL].index(name)
        cp = pltpu.make_async_copy(getattr(f, name), outs[3 + i], out_sem.at[3 + i])
        cp.start()
        copies.append(cp)

    def get(b, start, rows):
        return held[b][pl.ds(start, rows // 16)].astype(F32).reshape(rows, 128)

    cols = [slice(j * 128, (j + 1) * 128) for j in range(12)]
    for i in range(3):
        loads[7 + i].wait()
        cp = pltpu.make_async_copy(held[7 + i], outs[i], out_sem.at[i])
        cp.start()
        copies.append(cp)
    loads[0].wait()
    for j in range(6):
        f.hid[:, cols[j]] = get(0, T_HID + j * 48, 768)
    leave("hid")
    loads[3].wait()
    for k in range(4):
        for j in range(3):
            f.qkvg[:, k, cols[j]] = get(3, T_QKVG + (k * 3 + j) * 48, 768)
    leave("qkvg")
    for j in range(6):
        f.wout[:, cols[j]] = get(3, T_OUT + j * 24, 384)
    leave("wout")
    loads[1].wait()
    for i in range(12):
        k, j = i // 6, i % 6
        if i < 2:
            f.win[:, k, cols[j]] = get(0, T_IN0 + i * 48, 768)
        elif i < 11:
            f.win[:, k, cols[j]] = get(1, T_IN + (i - 2) * 48, 768)
        else:
            f.win[:256, k, cols[j]] = get(1, T_IN + 432, 256)
            f.win[256:, k, cols[j]] = get(3, T_IN2, 512)
    leave("win")
    loads[2].wait()
    loads[4].wait()
    for w in range(2):
        for j in range(12):
            f.ada[w, :, cols[j]] = get(4 - 2 * w, T_ADA[w] + j * 24, 384)
    leave("ada")
    for w in range(2):
        for j in range(6):
            if w == 1 and j >= 4:
                f.zero[w, :, cols[j]] = get(4, T_ZERO2 + (j - 4) * 24, 384)
            else:
                f.zero[w, :, cols[j]] = get(4 - 2 * w, T_ZERO[w] + j * 24, 384)
    leave("zero")
    loads[5].wait()
    for j in range(3):
        f.single[:, cols[j]] = get(5, j * 16, 256)
    leave("single")
    small = held[4][T_SMALL:T_APAD].astype(F32).reshape(32, 128)
    for w in range(2):
        for j in range(6):
            f.adab[w : w + 1, cols[j]] = small[6 * w + j : 6 * w + j + 1]
            f.zerob[w : w + 1, cols[j]] = small[12 + 6 * w + j : 13 + 6 * w + j]
        for j in range(3):
            f.gain[w : w + 1, cols[j]] = small[24 + 3 * w + j : 25 + 3 * w + j]
    loads[6].wait()
    f.wt[...] = held[6][:8]
    f.pgain[...] = held[6][8]
    for j in range(3):
        f.qb[cols[j]] = held[6][9 + j]
    for name in ("adab", "zerob", "gain", "wt", "pgain", "qb"):
        leave(name)
    for cp in copies:
        cp.wait()


def finish(*args):
    shapes = [whole((N, D), BF), whole((N, D), F32), whole((8, N, 128), F32)]
    shapes += [whole(shape, F32) for _, shape in FINAL]
    return pl.pallas_call(
        finish_kernel,
        out_shape=tuple(shapes),
        in_specs=[pl.BlockSpec(memory_space=pl.ANY)] * len(args),
        out_specs=[pl.BlockSpec(memory_space=pl.ANY)] * len(shapes),
        scratch_shapes=[pltpu.VMEM(a.shape, a.dtype) for a in args]
        + [pltpu.VMEM(shape, F32) for _, shape in FINAL]
        + [pltpu.SemaphoreType.DMA((10,)), pltpu.SemaphoreType.DMA((len(shapes),))],
        compiler_params=pltpu.CompilerParams(vmem_limit_bytes=63 * 2**20),
        name="finish",
    )(*args)


def local(
    activations,
    conditioning,
    pair,
    counts,
    ada_weight,
    ada_bias,
    cond_gain,
    zero_weight,
    zero_bias,
    qkvg_weight,
    q_bias,
    out_weight,
    in_weight,
    hid_weight,
    pair_gain,
    bias_weight,
    cotangent,
):
    results = mega(
        counts,
        pair[0],
        pair_gain,
        bias_weight.T,
        conditioning[0],
        cond_gain,
        ada_weight,
        ada_bias,
        zero_weight,
        zero_bias,
        activations[0, 0],
        cotangent[0, 0],
        in_weight.transpose(1, 0, 2),
        hid_weight,
        qkvg_weight.transpose(1, 0, 2),
        q_bias,
        out_weight,
    )
    outs = finish(*results)
    mixed, act, grad_pair = outs[:3]
    o = dict(zip([name for name, _ in FINAL], outs[3:]))
    return (
        mixed[None, None],
        act[None, None],
        o["single"][None],
        grad_pair[None],
        o["ada"],
        o["adab"],
        o["gain"],
        o["zero"],
        o["zerob"],
        o["qkvg"],
        o["qb"],
        o["wout"],
        o["win"],
        o["hid"],
        o["pgain"],
        o["wt"].T,
    )


def solution(mesh):
    placed = (
        P("cplx", "samp", None, None),
        P("cplx", None, None),
        P("cplx", "samp", None, None),
        P("cplx"),
        P(),
        P(),
        P(),
        P(),
        P(),
        P(None, None, "head"),
        P("head"),
        P("head", None),
        P(None, None, "head"),
        P("head", None),
        P(),
        P(None, "head"),
        P("cplx", "samp", None, None),
    )
    return jax.shard_map(
        local,
        mesh=mesh,
        in_specs=placed,
        out_specs=(
            P("cplx", "samp", None, None),
            P("cplx", "samp", None, None),
            P("cplx", None, None),
            P("cplx", "samp", None, None),
            P(),
            P(),
            P(),
            P(),
            P(),
            P(None, None, "head"),
            P("head"),
            P("head", None),
            P(None, None, "head"),
            P("head", None),
            P(),
            P(None, "head"),
        ),
        check_vma=False,
    )
```

```python
import functools
import math

import jax
import jax.numpy as jnp
from jax import lax
from jax.experimental import pallas as pl
from jax.experimental.pallas import tpu as pltpu
from jax.sharding import PartitionSpec as P

D = 768
HD = 48
EPS = 1e-05
HIGH = lax.Precision.HIGHEST
MESH = pl.DeviceIdType.MESH
BF = jnp.bfloat16
F32 = jnp.float32
NS = 32
VMEM = pltpu.VMEM


def place():
    samp = lax.axis_index("samp")
    return {
        "c": lax.axis_index("cplx"),
        "h": lax.axis_index("head"),
        "s": samp,
        "z": samp // 8,
        "l": (samp // 4) % 2,
        "x": samp % 4,
        "y": lax.axis_index("head") * 2 + (samp // 4) % 2,
    }


SIZE = {"z": 4, "x": 4, "y": 4, "l": 2}


def extent(axes):
    size = 1
    for a in axes:
        size *= SIZE[a]
    return size


def index_on(at, axes):
    index = 0
    for a in axes:
        index = index * SIZE[a] + at[a]
    return index


def peer_on(at, axes, step):
    now = dict(at)
    for a in reversed(axes):
        now[a] = (at[a] + step % SIZE[a]) % SIZE[a]
        step //= SIZE[a]
    if "y" in axes:
        now["h"], now["l"] = now["y"] // 2, now["y"] % 2
    dev = {"cplx": at["c"], "samp": now["z"] * 8 + now["l"] * 4 + now["x"], "head": now["h"]}
    return dev, index_on(now, axes)


def signal(bar, dev):
    pl.semaphore_signal(bar, inc=1, device_id=dev, device_id_type=MESH)


def samp_dev(at, other):
    return {"cplx": at["c"], "samp": other, "head": at["h"]}


def head_dev(at):
    return {"cplx": at["c"], "samp": at["s"], "head": 1 - at["h"]}


def core_dev(at):
    return {"cplx": 1 - at["c"], "samp": at["s"], "head": at["h"]}


def rcopy(src, dst, send, recv, dev):
    return pltpu.make_async_remote_copy(
        src_ref=src, dst_ref=dst, send_sem=send, recv_sem=recv, device_id=dev, device_id_type=MESH
    )


def greet_samp(at, bar):
    def one(i, _):
        signal(bar, samp_dev(at, (at["s"] + i) % NS))
        return 0

    lax.fori_loop(1, NS, one, 0)


SCALE = 1.0 / math.sqrt(HD)


def dot(a, b):
    return lax.dot_general(a, b, (((1,), (0,)), ((), ())), preferred_element_type=F32)


def dot_t(a, b):
    return lax.dot_general(a, b, (((1,), (1,)), ((), ())), preferred_element_type=F32)


def dot_l(a, b):
    return lax.dot_general(a, b, (((0,), (0,)), ((), ())), preferred_element_type=F32)


def mean(v):
    return jnp.mean(v, -1, keepdims=True)


def normalize(tensor):
    centered = tensor - mean(tensor)
    inv_std = lax.rsqrt(mean(centered * centered) + EPS)
    return (centered * inv_std, inv_std)


def norm_back(grad_hat, normed, inv_std):
    return inv_std * (grad_hat - mean(grad_hat) - normed * mean(grad_hat * normed))


def sigmoid(v):
    return 1.0 / (1.0 + jnp.exp(-v))


def flip(v):
    return v.astype(F32).T.astype(BF)


def loop(count, body):
    def step(i, _):
        body(i)
        return 0

    lax.fori_loop(0, count, step, 0)


def put(ref, start, value):
    rows, cols = value.shape
    n = rows // 16
    for j in range(cols // 128):
        ref[pl.ds(start + j * n, n)] = (
            value[:, j * 128 : (j + 1) * 128].astype(BF).reshape(n, 16, 128)
        )


TILES = (384, 448, 384, 768, 512, 64)
HALF = (192, 224, 192, 384, 256, 64)
GROUPS = (
    (0, 0, 192, "z", "xl"),
    (1, 0, 224, "x", "zl"),
    (2, 0, 64, "y", "zx"),
    (2, 64, 64, "z", "yx"),
    (2, 128, 64, "x", "yz"),
    (3, 0, 192, "z", "xl"),
    (3, 192, 192, "x", "zl"),
    (4, 0, 128, "y", "xz"),
    (4, 128, 64, "z", "yx"),
    (4, 192, 64, "x", "yz"),
    (5, 0, 64, "y", "zx"),
)
FIRST = (0, 1, 2, 3, 4)
SECOND = (5, 6, 7, 8, 9, 10)
T_HID, T_IN0, T_IN = 0, 288, 0
T_ADA, T_ZERO = (0, 0), (288, 288)
T_QKVG, T_OUT, T_IN2, T_WPAD = 0, 576, 720, 752
T_ZERO2, T_APAD = 432, 480

INPUTS = (
    ("pair", (8, 256, 128)),
    ("pgain", (128,)),
    ("wt", (8, 128)),
    ("single", (256, 384)),
    ("gain", (2, 384)),
    ("ada", (2, 384, 1536)),
    ("adab", (2, 768)),
    ("zero", (2, 384, 768)),
    ("zerob", (2, 768)),
    ("act", (256, 768)),
    ("cot", (256, 768)),
    ("win", (2, 768, 768)),
    ("hid", (768, 768)),
    ("wq", (4, 768, 384)),
    ("qb", (384,)),
    ("wout", (384, 768)),
)
LOADS = (
    ("pair", "pgain", "wt", "single", "gain", "adab", "zerob", "ada1", "zero1", "act", "cot")
    + ("win", "hid", "ada0", "zero0", "wq", "qb", "wout")
)
N = 256
SCRATCH = (
    ("rows", (8, 8, N), F32),
    ("part", (64, N), BF),
    ("bias", (NS, 64, N), BF),
    ("wall", (2, 16, 128), BF),
    ("shat", (N, 384), F32),
    ("sinv", (N, 128), F32),
    ("s_hi", (2, N, 384), BF),
    ("s_t", (2, 384, N), BF),
    ("one_t", (384, N), BF),
    ("mg", (2, N, D), F32),
    ("ms", (N, D), F32),
    ("zg", (2, N, D), F32),
    ("hat", (N, D), F32),
    ("ain", (N, D), BF),
    ("tin", (N, D), BF),
    ("gao", (N, D), BF),
    ("gto", (N, D), BF),
    ("hidden", (N, D), BF),
    ("ffn", (N, 2 * D), BF),
    ("pre", (2, N, 2 * D), BF),
    ("zp", (2, N, D), BF),
    ("mixf", (N, D), F32),
    ("actf", (N, D), F32),
    ("mixs", (N, D), BF),
    ("mixr", (N, D), BF),
    ("acts", (N, D), BF),
    ("actr", (N, D), BF),
    ("gsh", (N, 384), F32),
    ("zterm", (N, 384), F32),
    ("qkv", (3, N, 384), BF),
    ("gsig", (N, 384), F32),
    ("ggat", (N, 384), F32),
    ("gatt", (N, 384), BF),
    ("acc", (2, N, 384), F32),
    ("qt", (384, N), BF),
    ("gt", (384, N), BF),
    ("dkt", (384, N), F32),
    ("dvt", (384, N), F32),
    ("gheads", (N, 1536), BF),
    ("flipped", (D, N), BF),
    ("held", (NS, 8, N), F32),
    ("small", (48, 128), F32),
    ("gb", (2, NS, 32, N), BF),
    ("gb1", (2, 3, 8, 32, N), BF),
    ("gb2", (2, 7, 32, N), BF),
    ("gball", (2, 64, N), BF),
    ("gpair", (8, N, 128), F32),
    ("slot", (5, 4, 48, 128), F32),
)
SEMS = (
    ("ld", (len(LOADS),)),
    ("bs", (1,)),
    ("br", (1,)),
    ("hs", (4,)),
    ("hr", (4,)),
    ("cs", (5,)),
    ("cr", (5,)),
    ("rs", (len(GROUPS), 6)),
    ("rr", (len(GROUPS), 6)),
    ("fs", (5,)),
    ("fr", (5,)),
    ("b1s", (2,)),
    ("b1r", (2,)),
    ("b2s", (2,)),
    ("b2r", (2,)),
    ("out", (12,)),
    ("ss", (5,)),
    ("sr", (5,)),
)
OUTPUTS = tuple(("sum%d" % i, (t, 16, 128), BF) for i, t in enumerate(TILES)) + (
    ("small_o", (48, 128), F32),
    ("mixed_o", (N, D), BF),
    ("act_o", (N, D), F32),
    ("pair_o", (8, N, 128), F32),
)


class Refs:
    pass


def recv_shapes():
    shapes = []
    for g, (_, _, tiles, _, plane) in enumerate(GROUPS):
        part = tiles // 4
        small = part // extent(plane)
        shapes.append(((g, "opp"), (2, part // 2, 16, 128)))
        shapes.append(((g, "near"), (2, part, 16, 128)))
        shapes.append(((g, "plane"), (extent(plane) - 1, small, 16, 128)))
    return shapes


def arrived(like, send, recv, at):
    cp = rcopy(like, like, send, recv, core_dev(at))
    cp.wait_send()
    cp.wait_recv()


class Sums:
    def __init__(self, r, at):
        self.r, self.at = r, at
        self.shift = [at["c"] * HALF[b] if b < 5 else 0 for b in range(6)]
        self.pairs = {}

    def core_start(self, buf):
        r, at, half = self.r, self.at, HALF[buf]
        other = pl.ds((1 - at["c"]) * half, half)
        cp = rcopy(
            r.tiles[buf].at[other], r.sums[buf].at[other], r.cs.at[buf], r.cr.at[buf], core_dev(at)
        )
        cp.start()
        self.pairs[buf] = cp

    def core_end(self, buf):
        self.pairs[buf].wait()
        self.add(self.r.tiles[buf], self.shift[buf], HALF[buf], [self.r.sums[buf].at[pl.ds(self.shift[buf], HALF[buf])]])

    def add(self, to, start, count, others, src=None):
        src = to if src is None else src
        block = max(b for b in range(1, 17) if count % b == 0)

        def some(i):
            mine = pl.ds(start + i * block, block)
            rows = pl.ds(i * block, block)
            total = src[mine].astype(F32)
            for o in others:
                total = total + o[rows].astype(F32)
            to[mine] = total.astype(BF)

        loop(count // block, some)

    def send(self, g, sem, src, dst, dev):
        rcopy(src, dst, self.r.rs.at[g, sem], self.r.rr.at[g, sem], dev).start()

    def wait(self, g, sem, like):
        arrived(like, self.r.rs.at[g, sem], self.r.rr.at[g, sem], self.at)

    def ring(self, g):
        buf, start, tiles, axis, _ = GROUPS[g]
        part = tiles // 4
        first = self.shift[buf] + start
        quarters = [first + (self.at[axis] + i) % 4 * part for i in range(4)]
        right, left = peer_on(self.at, axis, 1)[0], peer_on(self.at, axis, 3)[0]
        return buf, part, quarters, right, left

    def ring_start(self, g):
        buf, part, (_, to_right, far, to_left), right, left = self.ring(g)
        half = part // 2
        tiles, opp, near = self.r.tiles[buf], self.r.recv[g, "opp"], self.r.recv[g, "near"]
        self.send(g, 0, tiles.at[pl.ds(far, half)], opp.at[0], right)
        self.send(g, 0, tiles.at[pl.ds(far + half, half)], opp.at[1], left)
        low, high = pl.ds(0, half), pl.ds(half, half)
        self.send(g, 1, tiles.at[pl.ds(to_right + half, half)], near.at[0, high], right)
        self.send(g, 1, tiles.at[pl.ds(to_left, half)], near.at[1, low], left)

    def ring_relay(self, g):
        buf, part, (_, to_right, _, to_left), right, left = self.ring(g)
        half = part // 2
        tiles, opp, near = self.r.tiles[buf], self.r.recv[g, "opp"], self.r.recv[g, "near"]
        self.wait(g, 0, opp)
        low, high = pl.ds(0, half), pl.ds(half, half)
        self.add(tiles, to_right, half, [opp.at[0]])
        self.send(g, 1, tiles.at[pl.ds(to_right, half)], near.at[0, low], right)
        self.add(tiles, to_left + half, half, [opp.at[1]])
        self.send(g, 1, tiles.at[pl.ds(to_left + half, half)], near.at[1, high], left)

    def plane_start(self, g):
        buf, part, quarters, _, _ = self.ring(g)
        near = self.r.recv[g, "near"]
        self.wait(g, 1, near)
        self.add(self.r.tiles[buf], quarters[0], part, [near.at[0], near.at[1]])
        plane = GROUPS[g][4]
        small = part // extent(plane)
        for i in range(1, extent(plane)):
            dev, q = peer_on(self.at, plane, i)
            src = self.r.tiles[buf].at[pl.ds(quarters[0] + q * small, small)]
            self.send(g, 2, src, self.r.recv[g, "plane"].at[i - 1], dev)

    def gather_start(self, g):
        buf, part, quarters, _, _ = self.ring(g)
        plane = GROUPS[g][4]
        count = extent(plane)
        small = part // count
        got = self.r.recv[g, "plane"]
        self.wait(g, 2, got)
        here = quarters[0] + index_on(self.at, plane) * small
        self.add(
            self.r.sums[buf], here, small, [got.at[i] for i in range(count - 1)], self.r.tiles[buf]
        )
        mine = self.r.sums[buf].at[pl.ds(here, small)]
        for i in range(1, count):
            self.send(g, 3, mine, mine, peer_on(self.at, plane, i)[0])

    def gather_ring(self, g):
        buf, part, quarters, right, left = self.ring(g)
        sums = self.r.sums[buf]
        count = extent(GROUPS[g][4])
        self.wait(g, 3, sums.at[pl.ds(0, (count - 1) * (part // count))])
        mine = sums.at[pl.ds(quarters[0], part)]
        self.send(g, 4, mine, mine, right)
        self.send(g, 4, mine, mine, left)
        self.share(g, 0)

    def gather_relay(self, g):
        buf, part, (_, of_right, _, of_left), right, left = self.ring(g)
        half = part // 2
        sums = self.r.sums[buf]
        self.wait(g, 4, sums.at[pl.ds(0, 2 * part)])
        low = sums.at[pl.ds(of_left, half)]
        self.send(g, 5, low, low, right)
        high = sums.at[pl.ds(of_right + half, half)]
        self.send(g, 5, high, high, left)
        self.share(g, 1)
        self.share(g, 3)

    def gather_end(self, g):
        buf, part, _, _, _ = self.ring(g)
        self.wait(g, 5, self.r.sums[buf].at[pl.ds(0, part)])
        self.share(g, 2)

    def share(self, g, i):
        buf, part, quarters, _, _ = self.ring(g)
        r = self.r
        if buf < 5:
            rows = r.sums[buf].at[pl.ds(quarters[i], part)]
            rcopy(rows, rows, r.fs.at[buf], r.fr.at[buf], core_dev(self.at)).start()

    def share_end(self, buf):
        r = self.r
        arrived(r.sums[buf].at[pl.ds(0, HALF[buf])], r.fs.at[buf], r.fr.at[buf], self.at)


def mega_kernel(*refs):
    r = Refs()
    refs = list(refs)

    def take(count):
        got = refs[:count]
        del refs[:count]
        return got

    counts_ref = take(1)[0]
    hbm = take(len(INPUTS))
    outs = dict(zip([o[0] for o in OUTPUTS], take(len(OUTPUTS))))
    for (name, _), ref in zip(INPUTS, take(len(INPUTS))):
        setattr(r, name, ref)
    for (name, _, _), ref in zip(SCRATCH, take(len(SCRATCH))):
        setattr(r, name, ref)
    r.tiles = take(6)
    r.sums = take(6)
    r.recv = {}
    for (key, _), ref in zip(recv_shapes(), take(len(recv_shapes()))):
        r.recv[key] = ref
    for (name, _), ref in zip(SEMS, take(len(SEMS))):
        setattr(r, name, ref)

    at = place()
    me, hd = at["s"], at["h"]
    bar = pltpu.get_barrier_semaphore()
    greet_samp(at, bar)
    cross = {"cplx": at["c"], "samp": at["z"] * 8 + (1 - at["l"]) * 4 + at["x"], "head": 1 - hd}
    for dev in (head_dev(at), core_dev(at), cross):
        signal(bar, dev)
    blocks = [slice(i * 256, (i + 1) * 256) for i in range(3)]
    loads = {}
    places = {name: i for i, (name, _) in enumerate(INPUTS)}
    for k, name in enumerate(LOADS):
        src, dst = hbm[places[name.rstrip("01")]], getattr(r, name.rstrip("01"))
        if name[-1] in "01":
            src, dst = src.at[int(name[-1])], dst.at[int(name[-1])]
        cp = pltpu.make_async_copy(src, dst, r.ld.at[k])
        cp.start()
        loads[name] = cp

    def need(*names):
        for name in names:
            loads[name].wait()

    copies = []

    def leave(src, name, rows=None):
        dst = outs[name] if rows is None else outs[name].at[rows]
        cp = pltpu.make_async_copy(src, dst, r.out.at[len(copies)])
        cp.start()
        copies.append(cp)

    need("pair", "pgain", "wt")
    pgain = r.pgain[...].astype(F32).reshape(1, 128)
    wt = r.wt[...]
    r.wall[hd] = jnp.concatenate([wt.astype(F32), jnp.zeros((8, 128), F32)], 0).astype(BF)
    for i in range(8):
        normed, _ = normalize(r.pair[i].astype(F32))
        r.rows[:, i, :] = dot_t(wt, (normed * pgain).astype(BF))
    r.part[...] = r.rows[...].reshape(64, N).astype(BF)
    r.bias[me] = r.part[...]
    pl.semaphore_wait(bar, NS + 2)

    def bias_copy(i):
        return rcopy(
            r.part, r.bias.at[me], r.bs.at[0], r.br.at[0], samp_dev(at, (me + i) % NS)
        )

    loop(NS - 1, lambda i: bias_copy(i + 1).start())
    wt_copy = rcopy(r.wall.at[hd], r.wall.at[hd], r.hs.at[0], r.hr.at[0], head_dev(at))
    wt_copy.start()

    r.small[...] = jnp.zeros(r.small.shape, F32)
    need("single", "gain")
    gains = r.gain[...].astype(F32)

    def cond(i):
        rows = pl.ds(i * 32, 32)
        normed, inv = normalize(r.single[rows].astype(F32))
        r.shat[rows] = normed
        r.sinv[rows] = jnp.broadcast_to(inv, (32, 128))
        for w in range(2):
            r.s_hi[w, rows] = (normed * gains[w : w + 1]).astype(BF)

    loop(N // 32, cond)

    def modulation(w):
        adab = r.adab[...].astype(F32)
        zerob = r.zerob[...].astype(F32)
        for b in blocks:
            later = slice(D + b.start, D + b.stop)
            r.mg[w, :, b] = sigmoid(dot(r.s_hi[w], r.ada[w, :, b]) + adab[w : w + 1, b])
            r.ms[:, b] = dot(r.s_hi[w], r.ada[w, :, later])
            r.zg[w, :, b] = sigmoid(dot(r.single[...], r.zero[w, :, b]) + zerob[w : w + 1, b])

    def branch_start(w, x_ref, g_ref):
        def some(i):
            rows = pl.ds(i * 16, 16)
            if w == 1:
                normed, _ = normalize(r.act[rows].astype(F32))
                r.hat[rows] = normed
            else:
                normed = r.hat[rows]
            x_ref[rows] = (r.mg[w, rows] * normed + r.ms[rows]).astype(BF)
            g_ref[rows] = (r.zg[w, rows] * r.cot[rows].astype(F32)).astype(BF)

        loop(N // 16, some)

    need("adab", "zerob", "ada1", "zero1")
    modulation(1)
    need("act", "cot")
    branch_start(1, r.tin, r.gto)

    def branch_out(w, b, part):
        gate = r.zg[w, :, b]
        share = gate * part
        r.mixf[:, b] = share if w == 1 else r.mixf[:, b] + share
        grad = r.cot[:, b].astype(F32) * share * (1.0 - gate)
        r.zp[w, :, b] = grad.astype(BF)
        for j in range(2):
            row = 28 + 6 * w + b.start // 128 + j
            r.small[row : row + 1] = jnp.sum(grad[:, j * 128 : (j + 1) * 128], 0, keepdims=True)

    def branch_in(w, b, grad_in):
        gate = r.mg[w, :, b]
        share = gate * grad_in
        r.actf[:, b] = share if w == 1 else r.actf[:, b] + share
        grad = share * r.hat[:, b] * (1.0 - gate)
        r.pre[w, :, b] = grad.astype(BF)
        r.pre[w, :, D + b.start : D + b.stop] = grad_in.astype(BF)
        for j in range(2):
            row = 16 + 6 * w + b.start // 128 + j
            r.small[row : row + 1] = jnp.sum(grad[:, j * 128 : (j + 1) * 128], 0, keepdims=True)

    def conditioned(w, to):
        for i in range(6):
            put(to, T_ADA[w] + i * 48, dot(r.s_t[w], r.pre[w, :, i * 256 : (i + 1) * 256]))
        for i, b in enumerate(blocks):
            value = dot(r.one_t[...], r.zp[w, :, b])
            if w == 1 and i == 2:
                put(r.tiles[4], T_ZERO2, value)
            else:
                put(to, T_ZERO[w] + i * 48, value)

    def conditioning_back(w):
        for j in range(3):
            b = slice(j * 128, (j + 1) * 128)
            scaled = dot_t(r.pre[w], r.ada[w, b, :])
            row = 40 + 3 * w + j
            r.small[row : row + 1] = jnp.sum(scaled * r.shat[:, b], 0, keepdims=True)
            share = scaled * gains[w : w + 1, b]
            through = dot_t(r.zp[w], r.zero[w, b, :])
            r.gsh[:, b] = share if w == 1 else r.gsh[:, b] + share
            r.zterm[:, b] = through if w == 1 else r.zterm[:, b] + through

    for w in range(2):
        r.s_t[w] = flip(r.s_hi[w])
    r.one_t[...] = flip(r.single[...])
    need("win", "hid")
    for b in blocks:
        gate_in = dot(r.tin[...], r.win[0, :, b])
        up_in = dot(r.tin[...], r.win[1, :, b])
        grad_hidden = dot_t(r.gto[...], r.hid[b, :])
        sig = sigmoid(gate_in)
        silu = gate_in * sig
        r.hidden[:, b] = (silu * up_in).astype(BF)
        r.ffn[:, b] = (grad_hidden * up_in * sig * (1.0 + gate_in * (1.0 - sig))).astype(BF)
        r.ffn[:, D + b.start : D + b.stop] = (grad_hidden * silu).astype(BF)
    sums = Sums(r, at)
    r.flipped[...] = flip(r.hidden[...])
    for i, b in enumerate(blocks):
        put(r.tiles[0], T_HID + i * 96, dot(r.flipped[...], r.gto[:, b]))
    r.flipped[...] = flip(r.tin[...])
    put(r.tiles[0], T_IN0, dot(r.flipped[...], r.ffn[:, :256]))
    sums.core_start(0)
    for i in range(1, 6):
        value = dot(r.flipped[...], r.ffn[:, i * 256 : (i + 1) * 256])
        if i < 5:
            put(r.tiles[1], T_IN + (i - 1) * 96, value)
        else:
            put(r.tiles[1], T_IN + 384, value[:, :128])
            put(r.tiles[1], T_IN + 432, value[:256, 128:])
            put(r.tiles[3], T_IN2, value[256:, 128:])
    sums.core_start(1)
    sums.core_end(0)
    sums.ring_start(0)
    for b in blocks:
        branch_out(1, b, dot(r.hidden[...], r.hid[:, b]))
    for b in blocks:
        branch_in(
            1, b, dot_t(r.ffn[:, :D], r.win[0, b, :]) + dot_t(r.ffn[:, D:], r.win[1, b, :])
        )
    sums.core_end(1)
    sums.ring_start(1)
    conditioned(1, r.tiles[2])
    sums.core_start(2)
    need("ada0", "zero0")
    modulation(0)
    branch_start(0, r.ain, r.gao)
    sums.core_end(2)
    for g in (2, 3, 4):
        sums.ring_start(g)
    sums.ring_relay(0)

    need("wq", "qb", "wout")
    r.qkv[0] = (dot(r.ain[...], r.wq[0]) + r.qb[...].astype(F32).reshape(1, 384)).astype(BF)
    r.qkv[1] = dot(r.ain[...], r.wq[1]).astype(BF)
    r.qkv[2] = dot(r.ain[...], r.wq[2]).astype(BF)
    r.gsig[...] = sigmoid(dot(r.ain[...], r.wq[3]))
    r.ggat[...] = dot_t(r.gao[...], r.wout[...])
    grad_att = r.ggat[...] * r.gsig[...]
    r.gatt[...] = grad_att.astype(BF)
    r.gt[...] = grad_att.T.astype(BF)
    r.qt[...] = flip(r.qkv[0])
    sums.ring_relay(1)
    arrived(r.bias.at[pl.ds(0, NS - 1)], r.bs.at[0], r.br.at[0], at)
    wt_copy.wait()
    r.acc[...] = jnp.zeros(r.acc.shape, F32)
    lane = lax.broadcasted_iota(jnp.int32, (1, 256), 1)
    mask = jnp.where(lane < counts_ref[0], 0.0, -1e9)
    for h in range(8):
        lo = 0 if h < 5 else 128
        win = slice(lo, lo + 256)
        first = h * HD - lo
        mine = (lane >= first) & (lane < first + HD)
        pick = jnp.where(mine, 1.0, 0.0).astype(BF)
        q_m = r.qkv[0, :, win] * pick
        k_m = r.qkv[1, :, win] * pick
        v_m = r.qkv[2, :, win] * pick
        g_m = r.gatt[:, win] * pick
        pair_rows = r.bias[:, (h // 2) * 16 : (h // 2) * 16 + 16, :].astype(F32)
        bias = pair_rows[:, (h % 2) * 8 : (h % 2) * 8 + 8, :].reshape(N, N)
        scores = dot_t(q_m, r.qkv[1, :, win]) * SCALE + bias + mask
        top = jnp.max(scores, -1, keepdims=True)
        weights = jnp.exp(scores - top)
        probs = weights * (1.0 / jnp.sum(weights, -1, keepdims=True))
        low = probs.astype(BF)
        r.acc[0, :, win] += dot(low, v_m)
        grad_probs = dot_t(g_m, r.qkv[2, :, win])
        delta = jnp.sum(probs * grad_probs, -1, keepdims=True)
        grad_s = probs * (grad_probs - delta)
        grad_low = grad_s.astype(BF)
        r.acc[1, :, win] += dot(grad_low, k_m)
        own = slice(h * HD, (h + 1) * HD)
        r.dkt[own] = dot(r.qt[own], grad_low)
        r.dvt[own] = dot(r.gt[own], low)
        split = grad_s.reshape(NS, 8, N)
        if h % 2 == 0:
            r.held[...] = split
        else:
            two = jnp.concatenate([r.held[...], split], 1).astype(BF)
            rows = slice((h // 2 % 2) * 16, (h // 2 % 2) * 16 + 16)
            if h < 4:
                r.gb[0, :, rows, :] = two
            else:
                for s in range(NS):
                    r.gb[1, s % 4 * 8 + s // 8 * 2 + s // 4 % 2, rows, :] = two[s]
        if h == 1:
            for g in (2, 3, 4):
                sums.ring_relay(g)
        if h == 4:
            sums.plane_start(0)
        if h == 6:
            sums.plane_start(1)
    for half, axis in enumerate("zx"):
        for i in range(1, 4):
            dev, q = peer_on(at, axis, i)
            rcopy(
                r.gb.at[half, pl.ds(q * 8, 8)],
                r.gb1.at[half, i - 1],
                r.b1s.at[half],
                r.b1r.at[half],
                dev,
            ).start()
    attended = r.acc[0]
    gated = (r.gsig[...] * attended).astype(BF)
    r.gheads[:, 1152:] = (r.ggat[...] * attended * r.gsig[...] * (1.0 - r.gsig[...])).astype(BF)
    grad_q = (r.acc[1] * SCALE).astype(BF)
    r.gheads[:, :384] = grad_q
    r.gheads[:, 384:768] = (r.dkt[...].T * SCALE).astype(BF)
    r.gheads[:, 768:1152] = r.dvt[...].T.astype(BF)
    for j in range(3):
        r.small[9 + j : 10 + j] = jnp.sum(
            grad_q[:, j * 128 : (j + 1) * 128].astype(F32), 0, keepdims=True
        )
    for b in blocks:
        branch_out(0, b, dot(gated, r.wout[:, b]))
    r.mixs[...] = r.mixf[...].astype(BF)
    mix_copy = rcopy(r.mixs, r.mixr, r.hs.at[1], r.hr.at[1], head_dev(at))
    mix_copy.start()
    for g in (2, 3, 4):
        sums.plane_start(g)
    r.flipped[:384] = flip(gated)
    for i, b in enumerate(blocks):
        put(r.tiles[3], T_OUT + i * 48, dot(r.flipped[:384], r.gao[:, b]))
    r.flipped[...] = flip(r.ain[...])
    for i in range(6):
        put(r.tiles[3], T_QKVG + i * 96, dot(r.flipped[...], r.gheads[:, i * 256 : (i + 1) * 256]))
    r.tiles[3][T_WPAD:] = jnp.zeros((TILES[3] - T_WPAD, 16, 128), BF)
    sums.core_start(3)
    for g in (0, 1):
        sums.gather_start(g)
    for b in blocks:
        total = dot_t(r.gheads[:, :384], r.wq[0, b, :])
        for k in range(1, 4):
            total = total + dot_t(r.gheads[:, k * 384 : (k + 1) * 384], r.wq[k, b, :])
        branch_in(0, b, total)
    r.acts[...] = r.actf[...].astype(BF)
    act_copy = rcopy(r.acts, r.actr, r.hs.at[2], r.hr.at[2], head_dev(at))
    act_copy.start()
    conditioned(0, r.tiles[4])
    r.tiles[4][T_APAD:] = jnp.zeros((TILES[4] - T_APAD, 16, 128), BF)
    sums.core_start(4)
    sums.core_end(3)
    for g in (5, 6):
        sums.ring_start(g)
    for g in (2, 3, 4):
        sums.gather_start(g)
    for g in (0, 1):
        sums.gather_ring(g)
    sums.core_end(4)
    for g in (7, 8, 9):
        sums.ring_start(g)
    conditioning_back(1)
    conditioning_back(0)
    grad_single = norm_back(r.gsh[...], r.shat[...], r.sinv[:, :1]) + r.zterm[...]
    put(r.tiles[5], 0, grad_single)
    r.tiles[5][48:] = jnp.zeros((TILES[5] - 48, 16, 128), BF)
    sums.ring_start(10)
    for half in range(2):
        arrived(r.gb1.at[half], r.b1s.at[half], r.b1r.at[half], at)
        own = pl.ds(at["zx"[half]] * 8, 8)
        total = r.gb[half, own].astype(F32)
        for i in range(3):
            total = total + r.gb1[half, i].astype(F32)
        r.gb[half, own] = total.astype(BF)
        for i in range(1, 8):
            dev, q = peer_on(at, ("lx", "zl")[half], i)
            rcopy(
                r.gb.at[half, at["zx"[half]] * 8 + q],
                r.gb2.at[half, i - 1],
                r.b2s.at[half],
                r.b2r.at[half],
                dev,
            ).start()
    for g in (5, 6):
        sums.ring_relay(g)
    for g in (2, 3, 4):
        sums.gather_ring(g)
    for g in (7, 8, 9):
        sums.ring_relay(g)
    for g in (0, 1):
        sums.gather_relay(g)
    sums.ring_relay(10)
    places = (at["z"] * 8 + at["l"] * 4 + at["x"], at["x"] * 8 + at["z"] * 2 + at["l"])
    for half in range(2):
        arrived(r.gb2.at[half], r.b2s.at[half], r.b2r.at[half], at)
        total = r.gb[half, places[half]].astype(F32)
        for i in range(7):
            total = total + r.gb2[half, i].astype(F32)
        r.gball[hd, half * 32 : half * 32 + 32] = total.astype(BF)
    rows_copy = rcopy(r.gball.at[hd], r.gball.at[hd], r.hs.at[3], r.hr.at[3], head_dev(at))
    rows_copy.start()
    mix_copy.wait()

    def last_mix(i):
        rows = pl.ds(i * 16, 16)
        value = r.mixs[rows].astype(F32) + r.mixr[rows].astype(F32)
        r.hidden[rows] = (r.act[rows].astype(F32) + value).astype(BF)

    loop(16, last_mix)
    leave(r.hidden, "mixed_o")
    for g in (5, 6):
        sums.plane_start(g)
    for g in (2, 3, 4):
        sums.gather_relay(g)
    for g in (7, 8, 9, 10):
        sums.plane_start(g)

    rows_copy.wait()
    r.rows[...] = r.gball[hd].astype(F32).reshape(8, 8, N)
    r.held[:16] = r.gball[...].astype(F32).reshape(16, 8, N)
    wt_all = (
        jnp.concatenate([r.wall[0].astype(F32)[:8], r.wall[1].astype(F32)[:8]], 0).astype(BF)
    )
    weight = jnp.zeros((8, 128), F32)
    total = jnp.zeros((1, 128), F32)
    for i in range(8):
        normed, inv = normalize(r.pair[i].astype(F32))
        weight = weight + dot(r.rows[:, i, :].astype(BF), (normed * pgain).astype(BF))
        grad_low = dot_l(r.held[:16, i, :].astype(BF), wt_all)
        total = total + jnp.sum(grad_low * normed, 0, keepdims=True)
        r.gpair[i] = norm_back(grad_low * pgain, normed, inv)
    leave(r.gpair, "pair_o")
    r.small[:8] = weight
    r.small[8:9] = total

    def small_start(k):
        axis = "czxlh"[k]
        mine = at[axis]
        first = 16 if axis == "h" else 0
        r.slot[k, mine] = r.small[...]
        rows = r.slot.at[k, mine, pl.ds(first, 48 - first)]
        for i in range(1, SIZE.get(axis, 2)):
            dev = {"c": core_dev, "h": head_dev}.get(axis, lambda a: peer_on(a, axis, i)[0])(at)
            rcopy(rows, rows, r.ss.at[k], r.sr.at[k], dev).start()

    def small_end(k):
        axis = "czxlh"[k]
        first = 16 if axis == "h" else 0
        count = SIZE.get(axis, 2)
        like = r.slot.at[k, pl.ds(0, count - 1), pl.ds(first, 48 - first)]
        arrived(like, r.ss.at[k], r.sr.at[k], at)
        total = r.slot[k, 0, first:]
        for i in range(1, count):
            total = total + r.slot[k, i, first:]
        r.small[first:] = total

    small_start(0)
    for g in FIRST:
        sums.gather_end(g)
    small_end(0)
    small_start(1)
    for g in SECOND:
        sums.gather_start(g)
    act_copy.wait()

    def last_act(i):
        rows = pl.ds(i * 16, 16)
        grad = r.acts[rows].astype(F32) + r.actr[rows].astype(F32)
        normed, inv = normalize(r.act[rows].astype(F32))
        r.mixf[rows] = r.cot[rows].astype(F32) + norm_back(grad, normed, inv)

    loop(16, last_act)
    leave(r.mixf, "act_o")
    small_end(1)
    small_start(2)
    for g in SECOND:
        sums.gather_ring(g)
    for b in (0, 1, 2):
        sums.share_end(b)
        leave(r.sums[b], "sum%d" % b)
    small_end(2)
    small_start(3)
    for g in SECOND:
        sums.gather_relay(g)
    small_end(3)
    small_start(4)
    for g in SECOND:
        sums.gather_end(g)
    small_end(4)
    leave(r.small, "small_o")
    leave(r.sums[5], "sum5")
    own = [pl.ds(sums.shift[b], HALF[b]) for b in range(5)]
    other = [pl.ds((1 - at["c"]) * HALF[b], HALF[b]) for b in range(5)]
    for b in (3, 4):
        leave(r.sums[b].at[own[b]], "sum%d" % b, own[b])
    for b in (3, 4):
        sums.share_end(b)
        leave(r.sums[b].at[other[b]], "sum%d" % b, other[b])
    for cp in copies:
        cp.wait()


def whole(shape, dtype):
    return jax.ShapeDtypeStruct(shape, dtype)


def mega(counts, *args):
    return pl.pallas_call(
        mega_kernel,
        out_shape=tuple(whole(shape, dtype) for _, shape, dtype in OUTPUTS),
        in_specs=[pl.BlockSpec(memory_space=pltpu.SMEM)]
        + [pl.BlockSpec(memory_space=pl.ANY)] * len(INPUTS),
        out_specs=[pl.BlockSpec(memory_space=pl.ANY)] * len(OUTPUTS),
        scratch_shapes=[pltpu.VMEM(shape, BF) for _, shape in INPUTS]
        + [pltpu.VMEM(shape, dtype) for _, shape, dtype in SCRATCH]
        + [pltpu.VMEM((t, 16, 128), BF) for t in TILES]
        + [pltpu.VMEM((t, 16, 128), BF) for t in TILES]
        + [pltpu.VMEM(shape, BF) for _, shape in recv_shapes()]
        + [pltpu.SemaphoreType.DMA(shape) for _, shape in SEMS],
        compiler_params=pltpu.CompilerParams(
            collective_id=0, has_side_effects=True, vmem_limit_bytes=63 * 2**20
        ),
        name="block",
    )(counts, *args)


FINAL = (
    ("qkvg", (D, 4, 384)),
    ("win", (D, 2, D)),
    ("hid", (D, D)),
    ("ada", (2, 384, 2 * D)),
    ("zero", (2, 384, D)),
    ("wout", (384, D)),
    ("single", (N, 384)),
    ("adab", (2, D)),
    ("zerob", (2, D)),
    ("gain", (2, 384)),
    ("wt", (8, 128)),
    ("qb", (384,)),
    ("pgain", (128,)),
)


def finish_kernel(*refs):
    refs = list(refs)

    def take(count):
        got = refs[:count]
        del refs[:count]
        return got

    ins = take(10)
    outs = take(3 + len(FINAL))
    held = take(10)
    f = Refs()
    for (name, _), ref in zip(FINAL, take(len(FINAL))):
        setattr(f, name, ref)
    in_sem, out_sem = take(2)
    loads = []
    for i in range(10):
        loads.append(pltpu.make_async_copy(ins[i], held[i], in_sem.at[i]))
    for i in (2, 4, 0, 3, 1, 5, 6, 7, 8, 9):
        loads[i].start()
    copies = []

    def leave(name, half=None):
        i = [k for k, _ in FINAL].index(name)
        src, dst = getattr(f, name), outs[3 + i]
        if half is not None:
            rows = pl.ds(half * 384, 384)
            src, dst = src.at[rows], dst.at[rows]
        cp = pltpu.make_async_copy(src, dst, out_sem.at[len(copies)])
        cp.start()
        copies.append(cp)

    def get(b, start, rows):
        return held[b][pl.ds(start, rows // 16)].astype(F32).reshape(rows, 128)

    cols = [slice(j * 128, (j + 1) * 128) for j in range(12)]
    loads[2].wait()
    loads[4].wait()
    for w in range(2):
        for j in range(12):
            f.ada[w, :, cols[j]] = get(4 - 2 * w, T_ADA[w] + j * 24, 384)
    leave("ada")
    for w in range(2):
        for j in range(6):
            if w == 1 and j >= 4:
                f.zero[w, :, cols[j]] = get(4, T_ZERO2 + (j - 4) * 24, 384)
            else:
                f.zero[w, :, cols[j]] = get(4 - 2 * w, T_ZERO[w] + j * 24, 384)
    leave("zero")
    loads[0].wait()
    for j in range(6):
        f.hid[:, cols[j]] = get(0, T_HID + j * 48, 768)
    leave("hid")
    loads[3].wait()
    for c in range(2):
        for k in range(4):
            for j in range(3):
                f.qkvg[c * 384 : c * 384 + 384, k, cols[j]] = get(
                    3, T_QKVG + (k * 3 + j) * 48 + c * 24, 384
                )
        leave("qkvg", c)
    for j in range(6):
        f.wout[:, cols[j]] = get(3, T_OUT + j * 24, 384)
    leave("wout")
    loads[1].wait()
    for c in range(2):
        for i in range(12):
            k, j = i // 6, i % 6
            if i < 2:
                value = get(0, T_IN0 + i * 48 + c * 24, 384)
            elif i < 11:
                value = get(1, T_IN + (i - 2) * 48 + c * 24, 384)
            elif c == 0:
                value = jnp.concatenate([get(1, T_IN + 432, 256), get(3, T_IN2, 128)], 0)
            else:
                value = get(3, T_IN2 + 8, 384)
            f.win[c * 384 : c * 384 + 384, k, cols[j]] = value
        leave("win", c)
    for i in range(3):
        loads[7 + i].wait()
        cp = pltpu.make_async_copy(held[7 + i], outs[i], out_sem.at[len(copies)])
        cp.start()
        copies.append(cp)
    loads[5].wait()
    for j in range(3):
        f.single[:, cols[j]] = get(5, j * 16, 256)
    leave("single")
    loads[6].wait()
    small = held[6][16:]
    for w in range(2):
        for j in range(6):
            f.adab[w : w + 1, cols[j]] = small[6 * w + j : 6 * w + j + 1]
            f.zerob[w : w + 1, cols[j]] = small[12 + 6 * w + j : 13 + 6 * w + j]
        for j in range(3):
            f.gain[w : w + 1, cols[j]] = small[24 + 3 * w + j : 25 + 3 * w + j]
    f.wt[...] = held[6][:8]
    f.pgain[...] = held[6][8]
    for j in range(3):
        f.qb[cols[j]] = held[6][9 + j]
    for name in ("adab", "zerob", "gain", "wt", "pgain", "qb"):
        leave(name)
    for cp in copies:
        cp.wait()


def finish(*args):
    shapes = [whole((N, D), BF), whole((N, D), F32), whole((8, N, 128), F32)]
    shapes += [whole(shape, F32) for _, shape in FINAL]
    return pl.pallas_call(
        finish_kernel,
        out_shape=tuple(shapes),
        in_specs=[pl.BlockSpec(memory_space=pl.ANY)] * len(args),
        out_specs=[pl.BlockSpec(memory_space=pl.ANY)] * len(shapes),
        scratch_shapes=[pltpu.VMEM(a.shape, a.dtype) for a in args]
        + [pltpu.VMEM(shape, F32) for _, shape in FINAL]
        + [pltpu.SemaphoreType.DMA((10,)), pltpu.SemaphoreType.DMA((len(shapes) + 2,))],
        compiler_params=pltpu.CompilerParams(vmem_limit_bytes=63 * 2**20),
        name="finish",
    )(*args)


def local(
    activations,
    conditioning,
    pair,
    counts,
    ada_weight,
    ada_bias,
    cond_gain,
    zero_weight,
    zero_bias,
    qkvg_weight,
    q_bias,
    out_weight,
    in_weight,
    hid_weight,
    pair_gain,
    bias_weight,
    cotangent,
):
    results = mega(
        counts,
        pair[0],
        pair_gain,
        bias_weight.T,
        conditioning[0],
        cond_gain,
        ada_weight,
        ada_bias,
        zero_weight,
        zero_bias,
        activations[0, 0],
        cotangent[0, 0],
        in_weight.transpose(1, 0, 2),
        hid_weight,
        qkvg_weight.transpose(1, 0, 2),
        q_bias,
        out_weight,
    )
    outs = finish(*results)
    mixed, act, grad_pair = outs[:3]
    o = dict(zip([name for name, _ in FINAL], outs[3:]))
    return (
        mixed[None, None],
        act[None, None],
        o["single"][None],
        grad_pair[None],
        o["ada"],
        o["adab"],
        o["gain"],
        o["zero"],
        o["zerob"],
        o["qkvg"],
        o["qb"],
        o["wout"],
        o["win"],
        o["hid"],
        o["pgain"],
        o["wt"].T,
    )


def solution(mesh):
    placed = (
        P("cplx", "samp", None, None),
        P("cplx", None, None),
        P("cplx", "samp", None, None),
        P("cplx"),
        P(),
        P(),
        P(),
        P(),
        P(),
        P(None, None, "head"),
        P("head"),
        P("head", None),
        P(None, None, "head"),
        P("head", None),
        P(),
        P(None, "head"),
        P("cplx", "samp", None, None),
    )
    return jax.shard_map(
        local,
        mesh=mesh,
        in_specs=placed,
        out_specs=(
            P("cplx", "samp", None, None),
            P("cplx", "samp", None, None),
            P("cplx", None, None),
            P("cplx", "samp", None, None),
            P(),
            P(),
            P(),
            P(),
            P(),
            P(None, None, "head"),
            P("head"),
            P("head", None),
            P(None, None, "head"),
            P("head", None),
            P(),
            P(None, "head"),
        ),
        check_vma=False,
    )
```

```python
import functools
import math

import jax
import jax.numpy as jnp
from jax import lax
from jax.experimental import pallas as pl
from jax.experimental.pallas import tpu as pltpu
from jax.sharding import PartitionSpec as P

D = 768
HD = 48
EPS = 1e-05
HIGH = lax.Precision.HIGHEST
MESH = pl.DeviceIdType.MESH
BF = jnp.bfloat16
F32 = jnp.float32
NS = 32
VMEM = pltpu.VMEM


def place():
    samp = lax.axis_index("samp")
    return {
        "c": lax.axis_index("cplx"),
        "h": lax.axis_index("head"),
        "s": samp,
        "z": samp // 8,
        "l": (samp // 4) % 2,
        "x": samp % 4,
        "y": lax.axis_index("head") * 2 + (samp // 4) % 2,
    }


SIZE = {"z": 4, "x": 4, "y": 4, "l": 2}


def extent(axes):
    size = 1
    for a in axes:
        size *= SIZE[a]
    return size


def index_on(at, axes):
    index = 0
    for a in axes:
        index = index * SIZE[a] + at[a]
    return index


def peer_on(at, axes, step):
    now = dict(at)
    for a in reversed(axes):
        now[a] = (at[a] + step % SIZE[a]) % SIZE[a]
        step //= SIZE[a]
    if "y" in axes:
        now["h"], now["l"] = now["y"] // 2, now["y"] % 2
    dev = {"cplx": at["c"], "samp": now["z"] * 8 + now["l"] * 4 + now["x"], "head": now["h"]}
    return dev, index_on(now, axes)


def signal(bar, dev):
    pl.semaphore_signal(bar, inc=1, device_id=dev, device_id_type=MESH)


def samp_dev(at, other):
    return {"cplx": at["c"], "samp": other, "head": at["h"]}


def head_dev(at):
    return {"cplx": at["c"], "samp": at["s"], "head": 1 - at["h"]}


def core_dev(at):
    return {"cplx": 1 - at["c"], "samp": at["s"], "head": at["h"]}


def rcopy(src, dst, send, recv, dev):
    return pltpu.make_async_remote_copy(
        src_ref=src, dst_ref=dst, send_sem=send, recv_sem=recv, device_id=dev, device_id_type=MESH
    )


def greet_samp(at, bar):
    def one(i, _):
        signal(bar, samp_dev(at, (at["s"] + i) % NS))
        return 0

    lax.fori_loop(1, NS, one, 0)


SCALE = 1.0 / math.sqrt(HD)


def dot(a, b):
    return lax.dot_general(a, b, (((1,), (0,)), ((), ())), preferred_element_type=F32)


def dot_t(a, b):
    return lax.dot_general(a, b, (((1,), (1,)), ((), ())), preferred_element_type=F32)


def dot_l(a, b):
    return lax.dot_general(a, b, (((0,), (0,)), ((), ())), preferred_element_type=F32)


def mean(v):
    return jnp.mean(v, -1, keepdims=True)


def normalize(tensor):
    centered = tensor - mean(tensor)
    inv_std = lax.rsqrt(mean(centered * centered) + EPS)
    return (centered * inv_std, inv_std)


def norm_back(grad_hat, normed, inv_std):
    return inv_std * (grad_hat - mean(grad_hat) - normed * mean(grad_hat * normed))


def sigmoid(v):
    return 1.0 / (1.0 + jnp.exp(-v))


def flip(v):
    return v.astype(F32).T.astype(BF)


def loop(count, body):
    def step(i, _):
        body(i)
        return 0

    lax.fori_loop(0, count, step, 0)


def put(ref, start, value):
    rows, cols = value.shape
    n = rows // 16
    for j in range(cols // 128):
        ref[pl.ds(start + j * n, n)] = (
            value[:, j * 128 : (j + 1) * 128].astype(BF).reshape(n, 16, 128)
        )


TILES = (384, 448, 384, 768, 512, 64)
HALF = (192, 224, 192, 384, 256, 64)
GROUPS = (
    (0, 0, 192, "z", "xl"),
    (1, 0, 224, "x", "zl"),
    (2, 0, 64, "y", "zx"),
    (2, 64, 64, "z", "yx"),
    (2, 128, 64, "x", "yz"),
    (3, 0, 192, "z", "xl"),
    (3, 192, 192, "x", "zl"),
    (4, 0, 128, "y", "xz"),
    (4, 128, 64, "z", "yx"),
    (4, 192, 64, "x", "yz"),
    (5, 0, 64, "y", "zx"),
)
FIRST = (0, 1, 2, 3, 4)
SECOND = (5, 6, 7, 8, 9, 10)
T_HID, T_IN0, T_IN = 0, 288, 0
T_ADA, T_ZERO = (0, 0), (288, 288)
T_QKVG, T_OUT, T_IN2, T_WPAD = 0, 576, 720, 752
T_ZERO2, T_APAD = 432, 480

INPUTS = (
    ("pair", (8, 256, 128)),
    ("pgain", (128,)),
    ("wt", (8, 128)),
    ("single", (256, 384)),
    ("gain", (2, 384)),
    ("ada", (2, 384, 1536)),
    ("adab", (2, 768)),
    ("zero", (2, 384, 768)),
    ("zerob", (2, 768)),
    ("act", (256, 768)),
    ("cot", (256, 768)),
    ("win", (2, 768, 768)),
    ("hid", (768, 768)),
    ("wq", (4, 768, 384)),
    ("qb", (384,)),
    ("wout", (384, 768)),
)
LOADS = (
    ("pair", "pgain", "wt", "single", "gain", "adab", "zerob", "ada1", "zero1", "act", "cot")
    + ("win", "hid", "ada0", "zero0", "wq", "qb", "wout")
)
N = 256
SCRATCH = (
    ("rows", (8, 8, N), F32),
    ("bias", (2, NS, 32, N), BF),
    ("wall", (2, 16, 128), BF),
    ("shat", (N, 384), F32),
    ("sinv", (N, 128), F32),
    ("s_hi", (2, N, 384), BF),
    ("s_t", (2, 384, N), BF),
    ("one_t", (384, N), BF),
    ("mg", (2, N, D), F32),
    ("ms", (N, D), F32),
    ("zg", (2, N, D), F32),
    ("hat", (N, D), F32),
    ("ain", (N, D), BF),
    ("tin", (N, D), BF),
    ("gao", (N, D), BF),
    ("gto", (N, D), BF),
    ("hidden", (N, D), BF),
    ("ffn", (N, 2 * D), BF),
    ("pre", (2, N, 2 * D), BF),
    ("zp", (2, N, D), BF),
    ("mixf", (N, D), F32),
    ("actf", (N, D), F32),
    ("mixs", (N, D), BF),
    ("mixr", (N, D), BF),
    ("acts", (N, D), BF),
    ("actr", (N, D), BF),
    ("gsh", (N, 384), F32),
    ("zterm", (N, 384), F32),
    ("qkv", (3, N, 384), BF),
    ("gsig", (N, 384), F32),
    ("ggat", (N, 384), F32),
    ("gatt", (N, 384), BF),
    ("acc", (2, N, 384), F32),
    ("qt", (384, N), BF),
    ("gt", (384, N), BF),
    ("dkt", (384, N), F32),
    ("dvt", (384, N), F32),
    ("gheads", (N, 1536), BF),
    ("flipped", (D, N), BF),
    ("held", (NS, 8, N), F32),
    ("small", (48, 128), F32),
    ("gb", (2, NS, 32, N), BF),
    ("gb1", (2, 3, 8, 32, N), BF),
    ("gb2", (2, 7, 32, N), BF),
    ("gball", (2, 64, N), BF),
    ("gpair", (8, N, 128), F32),
    ("slot", (5, 4, 48, 128), F32),
)
SEMS = (
    ("ld", (len(LOADS),)),
    ("bs", (4,)),
    ("br", (4,)),
    ("hs", (4,)),
    ("hr", (4,)),
    ("cs", (5,)),
    ("cr", (5,)),
    ("rs", (len(GROUPS), 6)),
    ("rr", (len(GROUPS), 6)),
    ("fs", (5,)),
    ("fr", (5,)),
    ("b1s", (2,)),
    ("b1r", (2,)),
    ("b2s", (2,)),
    ("b2r", (2,)),
    ("out", (12,)),
    ("ss", (5,)),
    ("sr", (5,)),
)
OUTPUTS = tuple(("sum%d" % i, (t, 16, 128), BF) for i, t in enumerate(TILES)) + (
    ("small_o", (48, 128), F32),
    ("mixed_o", (N, D), BF),
    ("act_o", (N, D), F32),
    ("pair_o", (8, N, 128), F32),
)


class Refs:
    pass


def recv_shapes():
    shapes = []
    for g, (_, _, tiles, _, plane) in enumerate(GROUPS):
        part = tiles // 4
        small = part // extent(plane)
        shapes.append(((g, "opp"), (2, part // 2, 16, 128)))
        shapes.append(((g, "near"), (2, part, 16, 128)))
        shapes.append(((g, "plane"), (extent(plane) - 1, small, 16, 128)))
    return shapes


def arrived(like, send, recv, at):
    cp = rcopy(like, like, send, recv, core_dev(at))
    cp.wait_send()
    cp.wait_recv()


class Sums:
    def __init__(self, r, at):
        self.r, self.at = r, at
        self.shift = [at["c"] * HALF[b] if b < 5 else 0 for b in range(6)]
        self.pairs = {}

    def core_start(self, buf):
        r, at, half = self.r, self.at, HALF[buf]
        other = pl.ds((1 - at["c"]) * half, half)
        cp = rcopy(
            r.tiles[buf].at[other], r.sums[buf].at[other], r.cs.at[buf], r.cr.at[buf], core_dev(at)
        )
        cp.start()
        self.pairs[buf] = cp

    def core_end(self, buf):
        self.pairs[buf].wait()
        self.add(self.r.tiles[buf], self.shift[buf], HALF[buf], [self.r.sums[buf].at[pl.ds(self.shift[buf], HALF[buf])]])

    def add(self, to, start, count, others, src=None):
        src = to if src is None else src
        block = max(b for b in range(1, 17) if count % b == 0)

        def some(i):
            mine = pl.ds(start + i * block, block)
            rows = pl.ds(i * block, block)
            total = src[mine].astype(F32)
            for o in others:
                total = total + o[rows].astype(F32)
            to[mine] = total.astype(BF)

        loop(count // block, some)

    def send(self, g, sem, src, dst, dev):
        rcopy(src, dst, self.r.rs.at[g, sem], self.r.rr.at[g, sem], dev).start()

    def wait(self, g, sem, like):
        arrived(like, self.r.rs.at[g, sem], self.r.rr.at[g, sem], self.at)

    def ring(self, g):
        buf, start, tiles, axis, _ = GROUPS[g]
        part = tiles // 4
        first = self.shift[buf] + start
        quarters = [first + (self.at[axis] + i) % 4 * part for i in range(4)]
        right, left = peer_on(self.at, axis, 1)[0], peer_on(self.at, axis, 3)[0]
        return buf, part, quarters, right, left

    def ring_start(self, g):
        buf, part, (_, to_right, far, to_left), right, left = self.ring(g)
        half = part // 2
        tiles, opp, near = self.r.tiles[buf], self.r.recv[g, "opp"], self.r.recv[g, "near"]
        self.send(g, 0, tiles.at[pl.ds(far, half)], opp.at[0], right)
        self.send(g, 0, tiles.at[pl.ds(far + half, half)], opp.at[1], left)
        low, high = pl.ds(0, half), pl.ds(half, half)
        self.send(g, 1, tiles.at[pl.ds(to_right + half, half)], near.at[0, high], right)
        self.send(g, 1, tiles.at[pl.ds(to_left, half)], near.at[1, low], left)

    def ring_relay(self, g):
        buf, part, (_, to_right, _, to_left), right, left = self.ring(g)
        half = part // 2
        tiles, opp, near = self.r.tiles[buf], self.r.recv[g, "opp"], self.r.recv[g, "near"]
        self.wait(g, 0, opp)
        low, high = pl.ds(0, half), pl.ds(half, half)
        self.add(tiles, to_right, half, [opp.at[0]])
        self.send(g, 1, tiles.at[pl.ds(to_right, half)], near.at[0, low], right)
        self.add(tiles, to_left + half, half, [opp.at[1]])
        self.send(g, 1, tiles.at[pl.ds(to_left + half, half)], near.at[1, high], left)

    def plane_start(self, g):
        buf, part, quarters, _, _ = self.ring(g)
        near = self.r.recv[g, "near"]
        self.wait(g, 1, near)
        self.add(self.r.tiles[buf], quarters[0], part, [near.at[0], near.at[1]])
        plane = GROUPS[g][4]
        small = part // extent(plane)
        for i in range(1, extent(plane)):
            dev, q = peer_on(self.at, plane, i)
            src = self.r.tiles[buf].at[pl.ds(quarters[0] + q * small, small)]
            self.send(g, 2, src, self.r.recv[g, "plane"].at[i - 1], dev)

    def gather_start(self, g):
        buf, part, quarters, _, _ = self.ring(g)
        plane = GROUPS[g][4]
        count = extent(plane)
        small = part // count
        got = self.r.recv[g, "plane"]
        self.wait(g, 2, got)
        here = quarters[0] + index_on(self.at, plane) * small
        self.add(
            self.r.sums[buf], here, small, [got.at[i] for i in range(count - 1)], self.r.tiles[buf]
        )
        mine = self.r.sums[buf].at[pl.ds(here, small)]
        for i in range(1, count):
            self.send(g, 3, mine, mine, peer_on(self.at, plane, i)[0])

    def gather_ring(self, g):
        buf, part, quarters, right, left = self.ring(g)
        sums = self.r.sums[buf]
        count = extent(GROUPS[g][4])
        self.wait(g, 3, sums.at[pl.ds(0, (count - 1) * (part // count))])
        mine = sums.at[pl.ds(quarters[0], part)]
        self.send(g, 4, mine, mine, right)
        self.send(g, 4, mine, mine, left)
        self.share(g, 0)

    def gather_relay(self, g):
        buf, part, (_, of_right, _, of_left), right, left = self.ring(g)
        half = part // 2
        sums = self.r.sums[buf]
        self.wait(g, 4, sums.at[pl.ds(0, 2 * part)])
        low = sums.at[pl.ds(of_left, half)]
        self.send(g, 5, low, low, right)
        high = sums.at[pl.ds(of_right + half, half)]
        self.send(g, 5, high, high, left)
        self.share(g, 1)
        self.share(g, 3)

    def gather_end(self, g):
        buf, part, _, _, _ = self.ring(g)
        self.wait(g, 5, self.r.sums[buf].at[pl.ds(0, part)])
        self.share(g, 2)

    def share(self, g, i):
        buf, part, quarters, _, _ = self.ring(g)
        r = self.r
        if buf < 5:
            rows = r.sums[buf].at[pl.ds(quarters[i], part)]
            rcopy(rows, rows, r.fs.at[buf], r.fr.at[buf], core_dev(self.at)).start()

    def share_end(self, buf):
        r = self.r
        arrived(r.sums[buf].at[pl.ds(0, HALF[buf])], r.fs.at[buf], r.fr.at[buf], self.at)


def mega_kernel(*refs):
    r = Refs()
    refs = list(refs)

    def take(count):
        got = refs[:count]
        del refs[:count]
        return got

    counts_ref = take(1)[0]
    hbm = take(len(INPUTS))
    outs = dict(zip([o[0] for o in OUTPUTS], take(len(OUTPUTS))))
    for (name, _), ref in zip(INPUTS, take(len(INPUTS))):
        setattr(r, name, ref)
    for (name, _, _), ref in zip(SCRATCH, take(len(SCRATCH))):
        setattr(r, name, ref)
    r.tiles = take(6)
    r.sums = take(6)
    r.recv = {}
    for (key, _), ref in zip(recv_shapes(), take(len(recv_shapes()))):
        r.recv[key] = ref
    for (name, _), ref in zip(SEMS, take(len(SEMS))):
        setattr(r, name, ref)

    at = place()
    me, hd = at["s"], at["h"]
    bar = pltpu.get_barrier_semaphore()
    greet_samp(at, bar)
    cross = {"cplx": at["c"], "samp": at["z"] * 8 + (1 - at["l"]) * 4 + at["x"], "head": 1 - hd}
    for dev in (head_dev(at), core_dev(at), cross):
        signal(bar, dev)
    blocks = [slice(i * 256, (i + 1) * 256) for i in range(3)]
    loads = {}
    index = {name: i for i, (name, _) in enumerate(INPUTS)}
    for k, name in enumerate(LOADS):
        src, dst = hbm[index[name.rstrip("01")]], getattr(r, name.rstrip("01"))
        if name[-1] in "01":
            src, dst = src.at[int(name[-1])], dst.at[int(name[-1])]
        cp = pltpu.make_async_copy(src, dst, r.ld.at[k])
        cp.start()
        loads[name] = cp

    def need(*names):
        for name in names:
            loads[name].wait()

    copies = []

    def leave(src, name, rows=None):
        dst = outs[name] if rows is None else outs[name].at[rows]
        cp = pltpu.make_async_copy(src, dst, r.out.at[len(copies)])
        cp.start()
        copies.append(cp)

    need("pair", "pgain", "wt")
    pgain = r.pgain[...].astype(F32).reshape(1, 128)
    wt = r.wt[...]
    r.wall[hd] = jnp.concatenate([wt.astype(F32), jnp.zeros((8, 128), F32)], 0).astype(BF)
    for i in range(8):
        normed, _ = normalize(r.pair[i].astype(F32))
        r.rows[:, i, :] = dot_t(wt, (normed * pgain).astype(BF))
    places = (at["z"] * 8 + at["l"] * 4 + at["x"], at["x"] * 8 + at["z"] * 2 + at["l"])
    part = r.rows[...].reshape(64, N).astype(BF)
    for half in range(2):
        r.bias[half, places[half]] = part[half * 32 : half * 32 + 32]
    pl.semaphore_wait(bar, NS + 2)

    def bias_send(half, hop):
        if hop == 0:
            rows, axes = pl.ds(places[half], 1), ("lx", "zl")[half]
        else:
            rows, axes = pl.ds(at["zx"[half]] * 8, 8), "zx"[half]
        mine = r.bias.at[half, rows]
        k = half + 2 * hop
        for i in range(1, extent(axes)):
            rcopy(mine, mine, r.bs.at[k], r.br.at[k], peer_on(at, axes, i)[0]).start()

    def bias_wait(half, hop):
        k = half + 2 * hop
        arrived(r.bias.at[half, pl.ds(0, (7, 24)[hop])], r.bs.at[k], r.br.at[k], at)

    for half in range(2):
        bias_send(half, 0)
    wt_copy = rcopy(r.wall.at[hd], r.wall.at[hd], r.hs.at[0], r.hr.at[0], head_dev(at))
    wt_copy.start()

    r.small[...] = jnp.zeros(r.small.shape, F32)
    need("single", "gain")
    gains = r.gain[...].astype(F32)

    def cond(i):
        rows = pl.ds(i * 32, 32)
        normed, inv = normalize(r.single[rows].astype(F32))
        r.shat[rows] = normed
        r.sinv[rows] = jnp.broadcast_to(inv, (32, 128))
        for w in range(2):
            r.s_hi[w, rows] = (normed * gains[w : w + 1]).astype(BF)

    loop(N // 32, cond)

    def modulation(w):
        adab = r.adab[...].astype(F32)
        zerob = r.zerob[...].astype(F32)
        for b in blocks:
            later = slice(D + b.start, D + b.stop)
            r.mg[w, :, b] = sigmoid(dot(r.s_hi[w], r.ada[w, :, b]) + adab[w : w + 1, b])
            r.ms[:, b] = dot(r.s_hi[w], r.ada[w, :, later])
            r.zg[w, :, b] = sigmoid(dot(r.single[...], r.zero[w, :, b]) + zerob[w : w + 1, b])

    def branch_start(w, x_ref, g_ref):
        def some(i):
            rows = pl.ds(i * 16, 16)
            if w == 1:
                normed, _ = normalize(r.act[rows].astype(F32))
                r.hat[rows] = normed
            else:
                normed = r.hat[rows]
            x_ref[rows] = (r.mg[w, rows] * normed + r.ms[rows]).astype(BF)
            g_ref[rows] = (r.zg[w, rows] * r.cot[rows].astype(F32)).astype(BF)

        loop(N // 16, some)

    need("adab", "zerob", "ada1", "zero1")
    modulation(1)
    need("act", "cot")
    branch_start(1, r.tin, r.gto)
    for half in range(2):
        bias_wait(half, 0)
        bias_send(half, 1)

    def branch_out(w, b, part):
        gate = r.zg[w, :, b]
        share = gate * part
        r.mixf[:, b] = share if w == 1 else r.mixf[:, b] + share
        grad = r.cot[:, b].astype(F32) * share * (1.0 - gate)
        r.zp[w, :, b] = grad.astype(BF)
        for j in range(2):
            row = 28 + 6 * w + b.start // 128 + j
            r.small[row : row + 1] = jnp.sum(grad[:, j * 128 : (j + 1) * 128], 0, keepdims=True)

    def branch_in(w, b, grad_in):
        gate = r.mg[w, :, b]
        share = gate * grad_in
        r.actf[:, b] = share if w == 1 else r.actf[:, b] + share
        grad = share * r.hat[:, b] * (1.0 - gate)
        r.pre[w, :, b] = grad.astype(BF)
        r.pre[w, :, D + b.start : D + b.stop] = grad_in.astype(BF)
        for j in range(2):
            row = 16 + 6 * w + b.start // 128 + j
            r.small[row : row + 1] = jnp.sum(grad[:, j * 128 : (j + 1) * 128], 0, keepdims=True)

    def conditioned(w, to):
        for i in range(6):
            put(to, T_ADA[w] + i * 48, dot(r.s_t[w], r.pre[w, :, i * 256 : (i + 1) * 256]))
        for i, b in enumerate(blocks):
            value = dot(r.one_t[...], r.zp[w, :, b])
            if w == 1 and i == 2:
                put(r.tiles[4], T_ZERO2, value)
            else:
                put(to, T_ZERO[w] + i * 48, value)

    def conditioning_back(w):
        for j in range(3):
            b = slice(j * 128, (j + 1) * 128)
            scaled = dot_t(r.pre[w], r.ada[w, b, :])
            row = 40 + 3 * w + j
            r.small[row : row + 1] = jnp.sum(scaled * r.shat[:, b], 0, keepdims=True)
            share = scaled * gains[w : w + 1, b]
            through = dot_t(r.zp[w], r.zero[w, b, :])
            r.gsh[:, b] = share if w == 1 else r.gsh[:, b] + share
            r.zterm[:, b] = through if w == 1 else r.zterm[:, b] + through

    for w in range(2):
        r.s_t[w] = flip(r.s_hi[w])
    r.one_t[...] = flip(r.single[...])
    need("win", "hid")
    for b in blocks:
        gate_in = dot(r.tin[...], r.win[0, :, b])
        up_in = dot(r.tin[...], r.win[1, :, b])
        grad_hidden = dot_t(r.gto[...], r.hid[b, :])
        sig = sigmoid(gate_in)
        silu = gate_in * sig
        r.hidden[:, b] = (silu * up_in).astype(BF)
        r.ffn[:, b] = (grad_hidden * up_in * sig * (1.0 + gate_in * (1.0 - sig))).astype(BF)
        r.ffn[:, D + b.start : D + b.stop] = (grad_hidden * silu).astype(BF)
    sums = Sums(r, at)
    r.flipped[...] = flip(r.hidden[...])
    for i, b in enumerate(blocks):
        put(r.tiles[0], T_HID + i * 96, dot(r.flipped[...], r.gto[:, b]))
    r.flipped[...] = flip(r.tin[...])
    put(r.tiles[0], T_IN0, dot(r.flipped[...], r.ffn[:, :256]))
    sums.core_start(0)
    for i in range(1, 6):
        value = dot(r.flipped[...], r.ffn[:, i * 256 : (i + 1) * 256])
        if i < 5:
            put(r.tiles[1], T_IN + (i - 1) * 96, value)
        else:
            put(r.tiles[1], T_IN + 384, value[:, :128])
            put(r.tiles[1], T_IN + 432, value[:256, 128:])
            put(r.tiles[3], T_IN2, value[256:, 128:])
    sums.core_start(1)
    sums.core_end(0)
    sums.ring_start(0)
    for b in blocks:
        branch_out(1, b, dot(r.hidden[...], r.hid[:, b]))
    for b in blocks:
        branch_in(
            1, b, dot_t(r.ffn[:, :D], r.win[0, b, :]) + dot_t(r.ffn[:, D:], r.win[1, b, :])
        )
    sums.core_end(1)
    sums.ring_start(1)
    conditioned(1, r.tiles[2])
    sums.core_start(2)
    need("ada0", "zero0")
    modulation(0)
    branch_start(0, r.ain, r.gao)
    sums.core_end(2)
    for g in (2, 3, 4):
        sums.ring_start(g)
    sums.ring_relay(0)

    need("wq", "qb", "wout")
    r.qkv[0] = (dot(r.ain[...], r.wq[0]) + r.qb[...].astype(F32).reshape(1, 384)).astype(BF)
    r.qkv[1] = dot(r.ain[...], r.wq[1]).astype(BF)
    r.qkv[2] = dot(r.ain[...], r.wq[2]).astype(BF)
    r.gsig[...] = sigmoid(dot(r.ain[...], r.wq[3]))
    r.ggat[...] = dot_t(r.gao[...], r.wout[...])
    grad_att = r.ggat[...] * r.gsig[...]
    r.gatt[...] = grad_att.astype(BF)
    r.gt[...] = grad_att.T.astype(BF)
    r.qt[...] = flip(r.qkv[0])
    sums.ring_relay(1)
    bias_wait(0, 1)
    bias_wait(1, 1)
    wt_copy.wait()
    r.acc[...] = jnp.zeros(r.acc.shape, F32)
    lane = lax.broadcasted_iota(jnp.int32, (1, 256), 1)
    mask = jnp.where(lane < counts_ref[0], 0.0, -1e9)
    for h in range(8):
        lo = 0 if h < 5 else 128
        win = slice(lo, lo + 256)
        first = h * HD - lo
        mine = (lane >= first) & (lane < first + HD)
        pick = jnp.where(mine, 1.0, 0.0).astype(BF)
        q_m = r.qkv[0, :, win] * pick
        k_m = r.qkv[1, :, win] * pick
        v_m = r.qkv[2, :, win] * pick
        g_m = r.gatt[:, win] * pick
        rows = slice((h // 2 % 2) * 16, (h // 2 % 2) * 16 + 16)
        pair_rows = r.bias[h // 4, :, rows, :].astype(F32)
        if h >= 4:
            order = [s % 4 * 8 + s // 8 * 2 + s // 4 % 2 for s in range(NS)]
            pair_rows = jnp.stack([pair_rows[s] for s in order])
        bias = pair_rows[:, (h % 2) * 8 : (h % 2) * 8 + 8, :].reshape(N, N)
        scores = dot_t(q_m, r.qkv[1, :, win]) * SCALE + bias + mask
        top = jnp.max(scores, -1, keepdims=True)
        weights = jnp.exp(scores - top)
        probs = weights * (1.0 / jnp.sum(weights, -1, keepdims=True))
        low = probs.astype(BF)
        r.acc[0, :, win] += dot(low, v_m)
        grad_probs = dot_t(g_m, r.qkv[2, :, win])
        delta = jnp.sum(probs * grad_probs, -1, keepdims=True)
        grad_s = probs * (grad_probs - delta)
        grad_low = grad_s.astype(BF)
        r.acc[1, :, win] += dot(grad_low, k_m)
        own = slice(h * HD, (h + 1) * HD)
        r.dkt[own] = dot(r.qt[own], grad_low)
        r.dvt[own] = dot(r.gt[own], low)
        split = grad_s.reshape(NS, 8, N)
        if h % 2 == 0:
            r.held[...] = split
        else:
            two = jnp.concatenate([r.held[...], split], 1).astype(BF)
            rows = slice((h // 2 % 2) * 16, (h // 2 % 2) * 16 + 16)
            if h < 4:
                r.gb[0, :, rows, :] = two
            else:
                for s in range(NS):
                    r.gb[1, s % 4 * 8 + s // 8 * 2 + s // 4 % 2, rows, :] = two[s]
        if h == 1:
            for g in (2, 3, 4):
                sums.ring_relay(g)
        if h == 4:
            sums.plane_start(0)
        if h == 6:
            sums.plane_start(1)
    for half, axis in enumerate("zx"):
        for i in range(1, 4):
            dev, q = peer_on(at, axis, i)
            rcopy(
                r.gb.at[half, pl.ds(q * 8, 8)],
                r.gb1.at[half, i - 1],
                r.b1s.at[half],
                r.b1r.at[half],
                dev,
            ).start()
    attended = r.acc[0]
    gated = (r.gsig[...] * attended).astype(BF)
    r.gheads[:, 1152:] = (r.ggat[...] * attended * r.gsig[...] * (1.0 - r.gsig[...])).astype(BF)
    grad_q = (r.acc[1] * SCALE).astype(BF)
    r.gheads[:, :384] = grad_q
    r.gheads[:, 384:768] = (r.dkt[...].T * SCALE).astype(BF)
    r.gheads[:, 768:1152] = r.dvt[...].T.astype(BF)
    for j in range(3):
        r.small[9 + j : 10 + j] = jnp.sum(
            grad_q[:, j * 128 : (j + 1) * 128].astype(F32), 0, keepdims=True
        )
    for b in blocks:
        branch_out(0, b, dot(gated, r.wout[:, b]))
    r.mixs[...] = r.mixf[...].astype(BF)
    mix_copy = rcopy(r.mixs, r.mixr, r.hs.at[1], r.hr.at[1], head_dev(at))
    mix_copy.start()
    for g in (2, 3, 4):
        sums.plane_start(g)
    r.flipped[:384] = flip(gated)
    for i, b in enumerate(blocks):
        put(r.tiles[3], T_OUT + i * 48, dot(r.flipped[:384], r.gao[:, b]))
    r.flipped[...] = flip(r.ain[...])
    for i in range(6):
        put(r.tiles[3], T_QKVG + i * 96, dot(r.flipped[...], r.gheads[:, i * 256 : (i + 1) * 256]))
    r.tiles[3][T_WPAD:] = jnp.zeros((TILES[3] - T_WPAD, 16, 128), BF)
    sums.core_start(3)
    for g in (0, 1):
        sums.gather_start(g)
    for b in blocks:
        total = dot_t(r.gheads[:, :384], r.wq[0, b, :])
        for k in range(1, 4):
            total = total + dot_t(r.gheads[:, k * 384 : (k + 1) * 384], r.wq[k, b, :])
        branch_in(0, b, total)
    r.acts[...] = r.actf[...].astype(BF)
    act_copy = rcopy(r.acts, r.actr, r.hs.at[2], r.hr.at[2], head_dev(at))
    act_copy.start()
    conditioned(0, r.tiles[4])
    r.tiles[4][T_APAD:] = jnp.zeros((TILES[4] - T_APAD, 16, 128), BF)
    sums.core_start(4)
    sums.core_end(3)
    for g in (5, 6):
        sums.ring_start(g)
    for g in (2, 3, 4):
        sums.gather_start(g)
    for g in (0, 1):
        sums.gather_ring(g)
    sums.core_end(4)
    for g in (7, 8, 9):
        sums.ring_start(g)
    conditioning_back(1)
    conditioning_back(0)
    grad_single = norm_back(r.gsh[...], r.shat[...], r.sinv[:, :1]) + r.zterm[...]
    put(r.tiles[5], 0, grad_single)
    r.tiles[5][48:] = jnp.zeros((TILES[5] - 48, 16, 128), BF)
    sums.ring_start(10)
    for half in range(2):
        arrived(r.gb1.at[half], r.b1s.at[half], r.b1r.at[half], at)
        own = pl.ds(at["zx"[half]] * 8, 8)
        total = r.gb[half, own].astype(F32)
        for i in range(3):
            total = total + r.gb1[half, i].astype(F32)
        r.gb[half, own] = total.astype(BF)
        for i in range(1, 8):
            dev, q = peer_on(at, ("lx", "zl")[half], i)
            rcopy(
                r.gb.at[half, at["zx"[half]] * 8 + q],
                r.gb2.at[half, i - 1],
                r.b2s.at[half],
                r.b2r.at[half],
                dev,
            ).start()
    for g in (5, 6):
        sums.ring_relay(g)
    for g in (2, 3, 4):
        sums.gather_ring(g)
    for g in (7, 8, 9):
        sums.ring_relay(g)
    for g in (0, 1):
        sums.gather_relay(g)
    sums.ring_relay(10)
    for half in range(2):
        arrived(r.gb2.at[half], r.b2s.at[half], r.b2r.at[half], at)
        total = r.gb[half, places[half]].astype(F32)
        for i in range(7):
            total = total + r.gb2[half, i].astype(F32)
        r.gball[hd, half * 32 : half * 32 + 32] = total.astype(BF)
    rows_copy = rcopy(r.gball.at[hd], r.gball.at[hd], r.hs.at[3], r.hr.at[3], head_dev(at))
    rows_copy.start()
    mix_copy.wait()

    def last_mix(i):
        rows = pl.ds(i * 16, 16)
        value = r.mixs[rows].astype(F32) + r.mixr[rows].astype(F32)
        r.hidden[rows] = (r.act[rows].astype(F32) + value).astype(BF)

    loop(16, last_mix)
    leave(r.hidden, "mixed_o")
    for g in (5, 6):
        sums.plane_start(g)
    for g in (2, 3, 4):
        sums.gather_relay(g)
    for g in (7, 8, 9, 10):
        sums.plane_start(g)

    rows_copy.wait()
    r.rows[...] = r.gball[hd].astype(F32).reshape(8, 8, N)
    r.held[:16] = r.gball[...].astype(F32).reshape(16, 8, N)
    wt_all = (
        jnp.concatenate([r.wall[0].astype(F32)[:8], r.wall[1].astype(F32)[:8]], 0).astype(BF)
    )
    weight = jnp.zeros((8, 128), F32)
    total = jnp.zeros((1, 128), F32)
    for i in range(8):
        normed, inv = normalize(r.pair[i].astype(F32))
        weight = weight + dot(r.rows[:, i, :].astype(BF), (normed * pgain).astype(BF))
        grad_low = dot_l(r.held[:16, i, :].astype(BF), wt_all)
        total = total + jnp.sum(grad_low * normed, 0, keepdims=True)
        r.gpair[i] = norm_back(grad_low * pgain, normed, inv)
    leave(r.gpair, "pair_o")
    r.small[:8] = weight
    r.small[8:9] = total

    def small_start(k):
        axis = "czxlh"[k]
        mine = at[axis]
        first = 16 if axis == "h" else 0
        r.slot[k, mine] = r.small[...]
        rows = r.slot.at[k, mine, pl.ds(first, 48 - first)]
        for i in range(1, SIZE.get(axis, 2)):
            dev = {"c": core_dev, "h": head_dev}.get(axis, lambda a: peer_on(a, axis, i)[0])(at)
            rcopy(rows, rows, r.ss.at[k], r.sr.at[k], dev).start()

    def small_end(k):
        axis = "czxlh"[k]
        first = 16 if axis == "h" else 0
        count = SIZE.get(axis, 2)
        like = r.slot.at[k, pl.ds(0, count - 1), pl.ds(first, 48 - first)]
        arrived(like, r.ss.at[k], r.sr.at[k], at)
        total = r.slot[k, 0, first:]
        for i in range(1, count):
            total = total + r.slot[k, i, first:]
        r.small[first:] = total

    small_start(0)
    for g in FIRST:
        sums.gather_end(g)
    small_end(0)
    small_start(1)
    for g in SECOND:
        sums.gather_start(g)
    act_copy.wait()

    def last_act(i):
        rows = pl.ds(i * 16, 16)
        grad = r.acts[rows].astype(F32) + r.actr[rows].astype(F32)
        normed, inv = normalize(r.act[rows].astype(F32))
        r.mixf[rows] = r.cot[rows].astype(F32) + norm_back(grad, normed, inv)

    loop(16, last_act)
    leave(r.mixf, "act_o")
    small_end(1)
    small_start(2)
    for g in SECOND:
        sums.gather_ring(g)
    for b in (0, 1, 2):
        sums.share_end(b)
        leave(r.sums[b], "sum%d" % b)
    small_end(2)
    small_start(3)
    for g in SECOND:
        sums.gather_relay(g)
    small_end(3)
    small_start(4)
    for g in SECOND:
        sums.gather_end(g)
    small_end(4)
    leave(r.small, "small_o")
    leave(r.sums[5], "sum5")
    own = [pl.ds(sums.shift[b], HALF[b]) for b in range(5)]
    other = [pl.ds((1 - at["c"]) * HALF[b], HALF[b]) for b in range(5)]
    for b in (3, 4):
        leave(r.sums[b].at[own[b]], "sum%d" % b, own[b])
    for b in (3, 4):
        sums.share_end(b)
        leave(r.sums[b].at[other[b]], "sum%d" % b, other[b])
    for cp in copies:
        cp.wait()


def whole(shape, dtype):
    return jax.ShapeDtypeStruct(shape, dtype)


def mega(counts, *args):
    return pl.pallas_call(
        mega_kernel,
        out_shape=tuple(whole(shape, dtype) for _, shape, dtype in OUTPUTS),
        in_specs=[pl.BlockSpec(memory_space=pltpu.SMEM)]
        + [pl.BlockSpec(memory_space=pl.ANY)] * len(INPUTS),
        out_specs=[pl.BlockSpec(memory_space=pl.ANY)] * len(OUTPUTS),
        scratch_shapes=[pltpu.VMEM(shape, BF) for _, shape in INPUTS]
        + [pltpu.VMEM(shape, dtype) for _, shape, dtype in SCRATCH]
        + [pltpu.VMEM((t, 16, 128), BF) for t in TILES]
        + [pltpu.VMEM((t, 16, 128), BF) for t in TILES]
        + [pltpu.VMEM(shape, BF) for _, shape in recv_shapes()]
        + [pltpu.SemaphoreType.DMA(shape) for _, shape in SEMS],
        compiler_params=pltpu.CompilerParams(
            collective_id=0, has_side_effects=True, vmem_limit_bytes=63 * 2**20
        ),
        name="block",
    )(counts, *args)


FINAL = (
    ("qkvg", (D, 4, 384)),
    ("win", (D, 2, D)),
    ("hid", (D, D)),
    ("ada", (2, 384, 2 * D)),
    ("zero", (2, 384, D)),
    ("wout", (384, D)),
    ("single", (N, 384)),
    ("adab", (2, D)),
    ("zerob", (2, D)),
    ("gain", (2, 384)),
    ("wt", (8, 128)),
    ("qb", (384,)),
    ("pgain", (128,)),
)


def finish_kernel(*refs):
    refs = list(refs)

    def take(count):
        got = refs[:count]
        del refs[:count]
        return got

    ins = take(10)
    outs = take(3 + len(FINAL))
    held = take(10)
    f = Refs()
    for (name, _), ref in zip(FINAL, take(len(FINAL))):
        setattr(f, name, ref)
    in_sem, out_sem = take(2)
    loads = []
    for i in range(10):
        loads.append(pltpu.make_async_copy(ins[i], held[i], in_sem.at[i]))
    for i in (2, 4, 0, 3, 1, 5, 6, 7, 8, 9):
        loads[i].start()
    copies = []

    def leave(name, half=None):
        i = [k for k, _ in FINAL].index(name)
        src, dst = getattr(f, name), outs[3 + i]
        if half is not None:
            rows = pl.ds(half * 384, 384)
            src, dst = src.at[rows], dst.at[rows]
        cp = pltpu.make_async_copy(src, dst, out_sem.at[len(copies)])
        cp.start()
        copies.append(cp)

    def get(b, start, rows):
        return held[b][pl.ds(start, rows // 16)].astype(F32).reshape(rows, 128)

    cols = [slice(j * 128, (j + 1) * 128) for j in range(12)]
    loads[2].wait()
    loads[4].wait()
    for w in range(2):
        for j in range(12):
            f.ada[w, :, cols[j]] = get(4 - 2 * w, T_ADA[w] + j * 24, 384)
    leave("ada")
    for w in range(2):
        for j in range(6):
            if w == 1 and j >= 4:
                f.zero[w, :, cols[j]] = get(4, T_ZERO2 + (j - 4) * 24, 384)
            else:
                f.zero[w, :, cols[j]] = get(4 - 2 * w, T_ZERO[w] + j * 24, 384)
    leave("zero")
    loads[0].wait()
    for j in range(6):
        f.hid[:, cols[j]] = get(0, T_HID + j * 48, 768)
    leave("hid")
    loads[3].wait()
    for c in range(2):
        for k in range(4):
            for j in range(3):
                f.qkvg[c * 384 : c * 384 + 384, k, cols[j]] = get(
                    3, T_QKVG + (k * 3 + j) * 48 + c * 24, 384
                )
        leave("qkvg", c)
    for j in range(6):
        f.wout[:, cols[j]] = get(3, T_OUT + j * 24, 384)
    leave("wout")
    loads[1].wait()
    for c in range(2):
        for i in range(12):
            k, j = i // 6, i % 6
            if i < 2:
                value = get(0, T_IN0 + i * 48 + c * 24, 384)
            elif i < 11:
                value = get(1, T_IN + (i - 2) * 48 + c * 24, 384)
            elif c == 0:
                value = jnp.concatenate([get(1, T_IN + 432, 256), get(3, T_IN2, 128)], 0)
            else:
                value = get(3, T_IN2 + 8, 384)
            f.win[c * 384 : c * 384 + 384, k, cols[j]] = value
        leave("win", c)
    for i in range(3):
        loads[7 + i].wait()
        cp = pltpu.make_async_copy(held[7 + i], outs[i], out_sem.at[len(copies)])
        cp.start()
        copies.append(cp)
    loads[5].wait()
    for j in range(3):
        f.single[:, cols[j]] = get(5, j * 16, 256)
    leave("single")
    loads[6].wait()
    small = held[6][16:]
    for w in range(2):
        for j in range(6):
            f.adab[w : w + 1, cols[j]] = small[6 * w + j : 6 * w + j + 1]
            f.zerob[w : w + 1, cols[j]] = small[12 + 6 * w + j : 13 + 6 * w + j]
        for j in range(3):
            f.gain[w : w + 1, cols[j]] = small[24 + 3 * w + j : 25 + 3 * w + j]
    f.wt[...] = held[6][:8]
    f.pgain[...] = held[6][8]
    for j in range(3):
        f.qb[cols[j]] = held[6][9 + j]
    for name in ("adab", "zerob", "gain", "wt", "pgain", "qb"):
        leave(name)
    for cp in copies:
        cp.wait()


def finish(*args):
    shapes = [whole((N, D), BF), whole((N, D), F32), whole((8, N, 128), F32)]
    shapes += [whole(shape, F32) for _, shape in FINAL]
    return pl.pallas_call(
        finish_kernel,
        out_shape=tuple(shapes),
        in_specs=[pl.BlockSpec(memory_space=pl.ANY)] * len(args),
        out_specs=[pl.BlockSpec(memory_space=pl.ANY)] * len(shapes),
        scratch_shapes=[pltpu.VMEM(a.shape, a.dtype) for a in args]
        + [pltpu.VMEM(shape, F32) for _, shape in FINAL]
        + [pltpu.SemaphoreType.DMA((10,)), pltpu.SemaphoreType.DMA((len(shapes) + 2,))],
        compiler_params=pltpu.CompilerParams(vmem_limit_bytes=63 * 2**20),
        name="finish",
    )(*args)


def local(
    activations,
    conditioning,
    pair,
    counts,
    ada_weight,
    ada_bias,
    cond_gain,
    zero_weight,
    zero_bias,
    qkvg_weight,
    q_bias,
    out_weight,
    in_weight,
    hid_weight,
    pair_gain,
    bias_weight,
    cotangent,
):
    results = mega(
        counts,
        pair[0],
        pair_gain,
        bias_weight.T,
        conditioning[0],
        cond_gain,
        ada_weight,
        ada_bias,
        zero_weight,
        zero_bias,
        activations[0, 0],
        cotangent[0, 0],
        in_weight.transpose(1, 0, 2),
        hid_weight,
        qkvg_weight.transpose(1, 0, 2),
        q_bias,
        out_weight,
    )
    outs = finish(*results)
    mixed, act, grad_pair = outs[:3]
    o = dict(zip([name for name, _ in FINAL], outs[3:]))
    return (
        mixed[None, None],
        act[None, None],
        o["single"][None],
        grad_pair[None],
        o["ada"],
        o["adab"],
        o["gain"],
        o["zero"],
        o["zerob"],
        o["qkvg"],
        o["qb"],
        o["wout"],
        o["win"],
        o["hid"],
        o["pgain"],
        o["wt"].T,
    )


def solution(mesh):
    placed = (
        P("cplx", "samp", None, None),
        P("cplx", None, None),
        P("cplx", "samp", None, None),
        P("cplx"),
        P(),
        P(),
        P(),
        P(),
        P(),
        P(None, None, "head"),
        P("head"),
        P("head", None),
        P(None, None, "head"),
        P("head", None),
        P(),
        P(None, "head"),
        P("cplx", "samp", None, None),
    )
    return jax.shard_map(
        local,
        mesh=mesh,
        in_specs=placed,
        out_specs=(
            P("cplx", "samp", None, None),
            P("cplx", "samp", None, None),
            P("cplx", None, None),
            P("cplx", "samp", None, None),
            P(),
            P(),
            P(),
            P(),
            P(),
            P(None, None, "head"),
            P("head"),
            P("head", None),
            P(None, None, "head"),
            P("head", None),
            P(),
            P(None, "head"),
        ),
        check_vma=False,
    )
```
